32 devices in a mesh: pix: 16 (over z, x, core), ch: 2 (over y).
Axes of the slice: x: 2, y: 2, z: 4, core: 2. Of those that a mesh axis runs over, the one named last changes fastest.
Arguments:
- features: float32 [1536, 64, 256], P('pix', None, 'ch'), may hold values from -250 to 250, as said below
- sea_mask: int32 [1536, 64], P('pix'), may hold values from 0 to 1, as said below
- edge_flip: int32 [4, 2], replicated, may hold values from 0 to 1
- w_first: float32 [3, 3, 256, 256], P(None, None, None, 'ch'), may hold values from -0.125 to 0.125
- b_first: float32 [256], P('ch'), may hold values from -1.5 to 1.5
- w_second: float32 [3, 3, 256, 256], P(None, None, None, 'ch'), may hold values from -0.125 to 0.125
- b_second: float32 [256], P('ch'), may hold values from -1.5 to 1.5
- w_skip: float32 [256, 256], P(None, 'ch'), may hold values from -0.375 to 0.375
- b_skip: float32 [256], P('ch'), may hold values from -1.5 to 1.5
- run_mean: float32 [256], P('ch'), may hold values from -4 to 4
- run_var: float32 [256], P('ch'), may hold values from 0.5 to 20
- cotangent: float32 [1536, 64, 256], P('pix', None, 'ch'), may hold values from -6 to 6
Outputs:
- output: float32 [1536, 64, 256], P('pix', None, 'ch')
- grad_features: float32 [1536, 64, 256], P('pix', None, 'ch')
- grad_w_first: float32 [3, 3, 256, 256], P(None, None, None, 'ch')
- grad_b_first: float32 [256], P('ch')
- grad_w_second: float32 [3, 3, 256, 256], P(None, None, None, 'ch')
- grad_b_second: float32 [256], P('ch')
- grad_w_skip: float32 [256, 256], P(None, 'ch')
- grad_b_skip: float32 [256], P('ch')
- new_mean: float32 [256], P('ch')
- new_var: float32 [256], P('ch')
The draws below stay inside these ranges and needn't reach their ends.
Inputs may be any that keep to these rules, and one draw needn't show every extreme that they name: `features`: channels of one field, scaled. `sea_mask`: 1 marks a valid sea pixel; the share of sea pixels is drawn for each face. `edge_flip`: entry [r, 0] reverses ribbon r's top rim, entry [r, 1] its bottom rim.
All inputs are finite; a program needn't handle non-finite values.
Results may differ from the reference program's by a relative error of at most 0.0003.
Values sent between devices are 32-bit elements; how exact they have to be, the bound alone decides.
No kernel may reach another device: no remote copies, remote signals or barrier semaphores. Data moves between devices by JAX's collectives and lax.ppermute only.
A program may use at most 256 MiB of HBM per device.

```python
import math
import jax
import jax.numpy as jnp
from jax import lax

C = 256
FACE = 64
SAMPLES = 2
ROWS = 1536


def draw_features(key, part):
    key = jax.random.fold_in(key, 7)
    subkeys = jax.random.split(key, 4)
    position = jnp.arange(ROWS, dtype=jnp.float32) / ROWS
    growth = jnp.exp(math.log(3.0) * position)[:, None, None]
    roughness = jax.random.uniform(subkeys[0], (ROWS, FACE, 1), jnp.float32, 0.7, 1.4)
    channel_scale = jnp.exp(jax.random.uniform(subkeys[1], (1, 1, C), jnp.float32, 0.0, math.log(10.0)))
    channel_centre = jax.random.uniform(subkeys[2], (1, 1, C), jnp.float32, -2.0, 2.0)
    fluctuation = jnp.clip(jax.random.normal(subkeys[3], (ROWS, FACE, C), jnp.float32), -4.0, 4.0)
    return (channel_centre + fluctuation * growth * roughness) * channel_scale


def draw_sea_mask(key, part):
    key = jax.random.fold_in(key, 13)
    subkeys = jax.random.split(key, 2)
    face_count = ROWS // FACE
    threshold = jax.random.randint(subkeys[0], (face_count, 1, 1), 30, 96)
    scores = jax.random.randint(subkeys[1], (face_count, FACE, FACE), 0, 100)
    return (scores < threshold).astype(jnp.int32).reshape(ROWS, FACE)


def place_ends(array, rng, low, largest):
    longest = array.shape.index(max(array.shape))
    spots = []
    for shift in (0, 1):
        where = [jax.random.randint(jax.random.fold_in(rng, axis), (), 0, length) for axis, length in enumerate(array.shape)]
        where[longest] = (where[longest] + shift) % array.shape[longest]
        spots.append(tuple(where))
    return array.at[spots[0]].set(low).at[spots[1]].set(largest)


def shard_levels(rng, shape, shards, low, high):
    def one(axis_at, parts):
        draws = jax.random.uniform(jax.random.fold_in(jax.random.fold_in(rng, 6), axis_at), (parts,), jnp.float32, low / len(shards), high / len(shards))
        return jnp.repeat(jnp.exp(draws), shape[axis_at] // parts).reshape((-1,) + (1,) * (len(shape) - axis_at - 1))

    gain = one(*shards[0])
    for cut in shards[1:]:
        gain = gain * one(*cut)
    return gain


def gaussian(key, extent, width, bound, cuts=(), kind=jnp.bfloat16):
    values = width * jax.random.normal(key, extent, jnp.float32)
    if cuts:
        values = values * shard_levels(key, extent, cuts, -0.22, 0.18)
    return jnp.clip(values, -bound, bound).astype(kind)


def setup_inputs(seed: int = 0) -> dict:
    key_of = jax.random.split(jax.random.key(seed), 13)
    return {
        "features": draw_features(jax.random.fold_in(key_of[12], 71), 0),
        "sea_mask": draw_sea_mask(jax.random.fold_in(key_of[12], 71), 0),
        "edge_flip": place_ends(jax.random.randint(key_of[2], (4, 2), 0, 2), jax.random.fold_in(key_of[2], 1), 0, 1).astype(jnp.int32),
        "w_first": gaussian(key_of[3], (3, 3, C, C), (9 * C) ** -0.5, 0.125, ((3, 2),), jnp.float32),
        "b_first": gaussian(key_of[4], (C,), 0.3, 1.5, ((0, 2),), jnp.float32),
        "w_second": gaussian(key_of[5], (3, 3, C, C), (9 * C) ** -0.5, 0.125, ((3, 2),), jnp.float32),
        "b_second": gaussian(key_of[6], (C,), 0.3, 1.5, ((0, 2),), jnp.float32),
        "w_skip": gaussian(key_of[7], (C, C), C ** -0.5, 0.375, ((1, 2),), jnp.float32),
        "b_skip": gaussian(key_of[8], (C,), 0.3, 1.5, ((0, 2),), jnp.float32),
        "run_mean": gaussian(key_of[9], (C,), 1.0, 4.0, ((0, 2),), jnp.float32),
        "run_var": jnp.clip(jnp.exp(math.log(20.0) - 3.6888795 * jax.random.uniform(key_of[10], (C,), jnp.float32) ** shard_levels(key_of[10], (C,), ((0, 2),), -0.2, 0.2)), 0.5, 20.0),
        "cotangent": gaussian(key_of[11], (ROWS, FACE, C), 1.0, 6.0, ((0, 16), (2, 2)), jnp.float32),
    }


EPSILON = 1e-05
MOMENTUM = 0.1
HIGHEST = lax.Precision.HIGHEST

@jax.custom_vjp
def low(v):
    return lax.optimization_barrier(v.astype(jnp.bfloat16)).astype(jnp.float32)

@jax.custom_vjp
def low_back(v):
    return v

def low_keep(v):
    return (low(v), None)

def low_pass(kept, grad):
    return (grad,)

def back_keep(v):
    return (v, None)

def back_low(kept, grad):
    return (low(grad),)
low.defvjp(low_keep, low_pass)
low_back.defvjp(back_keep, back_low)

def pad_faces(values, edge_flip):
    next_ribbon = jnp.roll(values, -1, axis=1)
    prev_ribbon = jnp.roll(values, 1, axis=1)
    middle = jnp.concatenate([prev_ribbon[:, :, :, -1:, :], values, next_ribbon[:, :, :, :1, :]], axis=3)
    reversed_rim = (edge_flip == 1)[None, :, :, None, None]
    pole_rows = jnp.stack([next_ribbon[:, :, 0], next_ribbon[:, :, -1]], axis=2)
    pole_rows = jnp.where(reversed_rim, pole_rows[:, :, :, ::-1], pole_rows)
    edge_rows = jnp.stack([middle[:, :, 0], middle[:, :, -1]], axis=2)
    first_corner = 0.5 * (pole_rows[:, :, :, :1] + edge_rows[:, :, :, :1])
    last_corner = 0.5 * (pole_rows[:, :, :, -1:] + edge_rows[:, :, :, -1:])
    rim_rows = jnp.concatenate([first_corner, pole_rows, last_corner], axis=3)
    return jnp.concatenate([rim_rows[:, :, :1], middle, rim_rows[:, :, 1:]], axis=2)

def conv_three(padded, kernel):
    height = padded.shape[-3] - 2
    breadth = padded.shape[-2] - 2
    summed = jnp.zeros(padded.shape[:-3] + (height, breadth, kernel.shape[3]), jnp.float32)
    for row_tap in range(3):
        for col_tap in range(3):
            window = padded[..., row_tap:row_tap + height, col_tap:col_tap + breadth, :]
            summed = summed + jnp.einsum('...hwi,io->...hwo', window, kernel[row_tap, col_tap], precision=HIGHEST)
    return summed

def forward(features, w_first, b_first, w_second, b_second, w_skip, b_skip, sea_mask, edge_flip):
    sea_weight = sea_mask.astype(jnp.float32)[:, :, None]
    sea_count = jnp.sum(sea_weight)
    batch_mean = lax.optimization_barrier(jnp.sum(sea_weight * features, axis=(0, 1))) / sea_count
    centred = features - batch_mean
    batch_var = lax.optimization_barrier(jnp.sum(sea_weight * centred * centred, axis=(0, 1))) / sea_count
    scaled_in = sea_weight * centred * lax.rsqrt(batch_var + EPSILON)
    ribbons = scaled_in.reshape(SAMPLES, 4, 3 * FACE, FACE, C)
    pre_first = conv_three(pad_faces(ribbons, edge_flip), w_first) + b_first
    hidden = jax.nn.gelu(pre_first, approximate=False)
    pre_second = conv_three(pad_faces(hidden, edge_flip), w_second) + b_second
    skip_term = jnp.einsum('...i,io->...o', ribbons, w_skip, precision=HIGHEST)
    output = jax.nn.gelu(pre_second, approximate=False) + skip_term + b_skip
    return (output.reshape(ROWS, FACE, C), (batch_mean, batch_var, sea_count))

def reference(features, sea_mask, edge_flip, w_first, b_first, w_second, b_second, w_skip, b_skip, run_mean, run_var, cotangent):

    def residual_block(feat, wone, bone, wtwo, btwo, wres, bres):
        return forward(feat, wone, bone, wtwo, btwo, wres, bres, sea_mask, edge_flip)
    output, pullback, statistics = jax.vjp(residual_block, features, w_first, b_first, w_second, b_second, w_skip, b_skip, has_aux=True)
    gradients = pullback(cotangent)
    batch_mean, batch_var, sea_count = statistics
    new_mean = (1.0 - MOMENTUM) * run_mean + MOMENTUM * batch_mean
    new_var = (1.0 - MOMENTUM) * run_var + MOMENTUM * batch_var * sea_count / (sea_count - 1.0)
    return (output, gradients[0], gradients[1], gradients[2], gradients[3], gradients[4], gradients[5], gradients[6], new_mean, new_var)
```

```python
import functools

import jax
import jax.numpy as jnp
from jax import lax
from jax.experimental import pallas as pl
from jax.experimental.pallas import tpu as pltpu
from jax.sharding import PartitionSpec as P

EPSILON = 1e-05
MOMENTUM = 0.1
INV_ROOT_TWO_PI = 0.3989422804014327
SQRT_HALF = 0.7071067811865476
F32 = jnp.float32
BF16 = jnp.bfloat16
VMEM_LIMIT = 60 * 1024 * 1024


def split(value):
    high = value.astype(BF16)
    return high, (value - high.astype(F32)).astype(BF16)


def dot_split(a_high, a_low, b_high, b_low):
    total = jnp.dot(a_high, b_high, preferred_element_type=F32)
    total = total + jnp.dot(a_high, b_low, preferred_element_type=F32)
    return total + jnp.dot(a_low, b_high, preferred_element_type=F32)


def gelu_and_slope(u):
    cdf = 0.5 * (1.0 + lax.erf(u * SQRT_HALF))
    return u * cdf, cdf + u * jnp.exp(-0.5 * u * u) * INV_ROOT_TWO_PI


def put_shifts(high, low, block, value, left, right):
    breadth, depth = value.shape
    column = lax.broadcasted_iota(jnp.int32, (breadth, 1), 0)
    shifts = (
        jnp.where(column == 0, left, pltpu.roll(value, 1, 0)),
        value,
        jnp.where(column == breadth - 1, right, pltpu.roll(value, breadth - 1, 0)),
    )
    for tap, piece in enumerate(shifts):
        piece_high, piece_low = split(piece)
        high[pl.ds(block * breadth, breadth), tap * depth : (tap + 1) * depth] = piece_high
        low[pl.ds(block * breadth, breadth), tap * depth : (tap + 1) * depth] = piece_low


def conv_rows(high, low, w_high, w_low, first, rows, breadth):
    total = None
    for row_tap in range(3):
        window = pl.ds(pl.multiple_of((first + row_tap) * breadth, breadth), rows * breadth)
        part = dot_split(high[window, :], low[window, :], w_high[row_tap], w_low[row_tap])
        total = part if total is None else total + part
    return total


def put_padded(flags, x, left, right, pole, high, low, begin, count, top, bottom):
    breadth = x.shape[1]

    @pl.loop(0, count)
    def _(block):
        row = block + begin
        put_shifts(high, low, block, x[row], left[pl.ds(row, 1)], right[pl.ds(row, 1)])

    def put_pole(at, edge):
        corner_left = 0.5 * (pole[0:1] + left[edge : edge + 1])
        corner_right = 0.5 * (pole[breadth - 1 : breadth] + right[edge : edge + 1])
        put_shifts(high, low, at - begin, pole[...], corner_left, corner_right)

    @pl.when(flags[0] == 1)
    def _():
        put_pole(top, top + 1)

    @pl.when(flags[1] == 1)
    def _():
        put_pole(bottom, bottom - 1)


def first_kernel(flags, x, left, right, pole, w_high, w_low, bias, hidden, slope, high, low, *, tile):
    blocks, breadth = x.shape[0], x.shape[1]
    depth = hidden.shape[2]
    put_padded(flags, x, left, right, pole, high, low, 0, blocks, 3, blocks - 4)

    @pl.loop(0, (blocks - 2) // tile)
    def _(step):
        first = step * tile
        pre = conv_rows(high, low, w_high, w_low, first, tile, breadth) + bias[...]
        value, grad = gelu_and_slope(pre)
        hidden[pl.ds(first, tile)] = value.reshape(tile, breadth, depth)
        slope[pl.ds(first, tile)] = grad.reshape(tile, breadth, depth)


def second_kernel(
    flags, x, left, right, pole, w_high, w_low, bias, source, s_high, s_low, s_bias, out, slope, high, low, *, tile
):
    blocks, breadth = x.shape[0], x.shape[1]
    depth = out.shape[2]
    put_padded(flags, x, left, right, pole, high, low, 0, blocks, 2, blocks - 3)

    @pl.loop(0, (blocks - 2) // tile)
    def _(step):
        first = step * tile
        pre = conv_rows(high, low, w_high, w_low, first, tile, breadth) + bias[...]
        value, grad = gelu_and_slope(pre)
        skip_high, skip_low = split(source[pl.ds(first + 2, tile)].reshape(tile * breadth, -1))
        skip = dot_split(skip_high, skip_low, s_high[...], s_low[...]) + s_bias[...]
        out[pl.ds(first, tile)] = (value + skip).reshape(tile, breadth, depth)
        slope[pl.ds(first, tile)] = grad.reshape(tile, breadth, depth)


def back_conv(high, low, w_high, w_low, edge_first, edge_last, out, blocks, breadth, tile):
    depth = edge_first.shape[1]
    for tap in range(3):
        for edge, slot, base in ((edge_first, 2, blocks), (edge_last, 0, blocks + 3)):
            rows = pl.ds((base + tap) * breadth, breadth)
            edge_high, edge_low = split(edge[tap : tap + breadth])
            zero = jnp.zeros((breadth, 3 * depth), BF16)
            high[rows, :] = zero
            low[rows, :] = zero
            high[rows, slot * depth : (slot + 1) * depth] = edge_high
            low[rows, slot * depth : (slot + 1) * depth] = edge_low

    @pl.loop(0, (blocks + 4) // tile)
    def _(step):
        first = step * tile
        out[pl.ds(first, tile)] = conv_rows(high, low, w_high, w_low, first, tile, breadth).reshape(
            tile, breadth, depth
        )


def back_second_kernel(flags, cot, slope, w_high, w_low, out, grad, high, low, edge_first, edge_last, *, tile):
    blocks, breadth = cot.shape[0], cot.shape[1]
    edge_first[...] = jnp.zeros_like(edge_first)
    edge_last[...] = jnp.zeros_like(edge_last)

    @pl.loop(0, blocks)
    def _(block):
        outside = ((flags[0] == 1) & (block < 2)) | ((flags[1] == 1) & (block >= blocks - 2))
        value = cot[block] * slope[block] * jnp.where(outside, 0.0, 1.0)
        put_shifts(high, low, block, value, 0.0, 0.0)
        edge_first[pl.ds(block, 1)] = value[0:1]
        edge_last[pl.ds(block, 1)] = value[breadth - 1 : breadth]

        @pl.when((block >= 2) & (block < blocks - 2))
        def _():
            grad[block - 2] = value

    back_conv(high, low, w_high, w_low, edge_first, edge_last, out, blocks, breadth, tile)


def back_first_kernel(
    flags, upper, add_first, add_last, add_pole, slope, cot, w_high, w_low, s_high, s_low,
    out, grad, high, low, edge_first, edge_last, *, tile
):
    blocks, breadth, depth = cot.shape
    column = lax.broadcasted_iota(jnp.int32, (breadth, 1), 0)
    edge_first[...] = jnp.zeros_like(edge_first)
    edge_last[...] = jnp.zeros_like(edge_last)
    none = jnp.zeros((breadth, depth), F32)
    put_shifts(high, low, 0, none, 0.0, 0.0)
    put_shifts(high, low, blocks - 1, none, 0.0, 0.0)

    @pl.loop(1, blocks - 1)
    def _(block):
        row = block - 1
        outside = ((flags[0] == 1) & (block < 2)) | ((flags[1] == 1) & (block >= blocks - 2))
        edge = ((flags[0] == 1) & (block == 2)) | ((flags[1] == 1) & (block == blocks - 3))
        value = upper[row] + jnp.where(column == 0, add_first[pl.ds(row, 1)], 0.0)
        value = value + jnp.where(column == breadth - 1, add_last[pl.ds(row, 1)], 0.0)
        value = value + add_pole[...] * jnp.where(edge, 1.0, 0.0)
        value = value * slope[row + 2] * jnp.where(outside, 0.0, 1.0)
        put_shifts(high, low, block, value, 0.0, 0.0)
        edge_first[pl.ds(block, 1)] = value[0:1]
        edge_last[pl.ds(block, 1)] = value[breadth - 1 : breadth]

        @pl.when((block >= 2) & (block < blocks - 2))
        def _():
            grad[block - 2] = value

    back_conv(high, low, w_high, w_low, edge_first, edge_last, out, blocks, breadth, tile)

    @pl.loop(0, (blocks - 4) // tile)
    def _(step):
        first = step * tile
        cot_high, cot_low = split(cot[pl.ds(first + 2, tile)].reshape(tile * breadth, depth))
        skip = dot_split(cot_high, cot_low, s_high[...], s_low[...])
        out[pl.ds(first + 1, tile)] = out[pl.ds(first + 1, tile)] + skip.reshape(tile, breadth, depth)


def put_transposed(source, begin, rows, breadth, high, low, total, tile):
    depth = source.shape[2]
    total[...] = jnp.zeros_like(total)

    @pl.loop(0, rows // tile)
    def _(step):
        piece = source[pl.ds(begin + step * tile, tile)].reshape(tile * breadth, depth)
        total[...] += jnp.sum(piece, axis=0, keepdims=True)
        piece_high, piece_low = split(piece.T)
        window = pl.ds(pl.multiple_of(step * tile * breadth, tile * breadth), tile * breadth)
        high[:, window] = piece_high
        low[:, window] = piece_low


def put_weight_grad(out, at, grad, swap, depth):
    half = depth // 2
    out[at + (pl.ds(swap, half),)] = grad[:half]
    out[at + (pl.ds(half - swap, half),)] = grad[half:]


def weight_kernel(flags, x, left, right, pole, grad, *rest, begin, top, bottom, skip):
    if skip:
        cot, out, total, out_skip, total_skip, high, low, t_high, t_low = rest
    else:
        out, total, high, low, t_high, t_low = rest
    rows, breadth, depth = grad.shape
    put_padded(flags, x, left, right, pole, high, low, begin, rows + 2, top, bottom)
    put_transposed(grad, 0, rows, breadth, t_high, t_low, total, 4)
    swap = pl.multiple_of(flags[2] * (depth // 2), depth // 2)

    @pl.loop(0, 3)
    def _(row_tap):
        window = pl.ds(pl.multiple_of(row_tap * breadth, breadth), rows * breadth)
        for tap in range(3):
            lanes = slice(tap * depth, (tap + 1) * depth)
            part = dot_split(t_high[...], t_low[...], high[window, lanes], low[window, lanes])
            put_weight_grad(out, (row_tap, tap), part.T, swap, depth)

    if skip:
        put_transposed(cot, 2, rows, breadth, t_high, t_low, total_skip, 4)
        window, lanes = slice(breadth, breadth + rows * breadth), slice(depth, 2 * depth)
        part = dot_split(t_high[...], t_low[...], high[window, lanes], low[window, lanes])
        put_weight_grad(out_skip, (), part.T, swap, depth)


def call(kernel, shapes, scratch, flags, *operands):
    whole = pl.BlockSpec(memory_space=pltpu.VMEM)
    return pl.pallas_call(
        kernel,
        out_shape=[jax.ShapeDtypeStruct(shape, F32) for shape in shapes],
        in_specs=[pl.BlockSpec(memory_space=pltpu.SMEM)] + [whole] * len(operands),
        out_specs=[whole] * len(shapes),
        scratch_shapes=scratch,
        compiler_params=pltpu.CompilerParams(vmem_limit_bytes=VMEM_LIMIT),
    )(flags, *operands)


class Place:
    def __init__(self, mesh, rows, breadth):
        self.count = mesh.shape["pix"]
        self.strips = 3 * breadth // rows
        assert mesh.shape["ch"] == 2 and self.strips == 2
        self.pix = lax.axis_index("pix")
        self.side = lax.axis_index("ch")
        self.ribbon = self.pix // self.strips % 4
        self.strip = self.pix % self.strips
        self.half = self.side ^ self.strip
        self.at_top = (self.side == 0) & (self.strip == 0)
        self.at_bottom = (self.side == 0) & (self.strip == 1)
        self.at_pole = self.side == 0

    def ribbon_pairs(self, offset):
        pairs = []
        for index in range(self.count):
            sample, strip = index // (4 * self.strips), index % self.strips
            ribbon = (index // self.strips + offset) % 4
            pairs.append((index, (sample * 4 + ribbon) * self.strips + strip))
        return pairs

    def to_next(self, value):
        return lax.ppermute(value, "pix", self.ribbon_pairs(1))

    def to_prev(self, value):
        return lax.ppermute(value, "pix", self.ribbon_pairs(-1))

    def across(self, value):
        return lax.ppermute(value, "ch", [(0, 1), (1, 0)])

    def flip(self, value, bit):
        return lax.ppermute(value, "pix", [(i, i ^ bit) for i in range(self.count)])

    def bits(self):
        bit, out = 1, []
        while bit < self.count:
            out.append(bit)
            bit *= 2
        return out

    def ordered(self, mine, theirs, bit):
        upper = (self.pix & bit) != 0
        return jnp.where(upper, theirs, mine), jnp.where(upper, mine, theirs)

    def gathered(self, value):
        for bit in reversed(self.bits()):
            value = jnp.stack(self.ordered(value, self.flip(value, bit), bit))
        steps = len(self.bits())
        value = value.transpose(tuple(reversed(range(steps))) + tuple(range(steps, value.ndim)))
        return value.reshape((-1,) + value.shape[steps + 1 :])

    def reduced(self, value):
        for bit in self.bits():
            upper = (self.pix & bit) != 0
            size = value.shape[0] // 2
            low, high = value[:size], value[size:]
            value = jnp.where(upper, high, low) + self.flip(jnp.where(upper, low, high), bit)
        return value

    def spread(self, value):
        for bit in reversed(self.bits()):
            value = jnp.concatenate(self.ordered(value, self.flip(value, bit), bit), axis=0)
        return value

    def summed(self, value):
        for bit in self.bits():
            first, second = self.ordered(value, self.flip(value, bit), bit)
            value = first + second
        return value

    def halves(self, value, extra, size):
        length = size + extra
        mine = lax.dynamic_slice_in_dim(value, self.half * (size - extra), length, 0)
        theirs = lax.dynamic_slice_in_dim(value, (1 - self.half) * (size - extra), length, 0)
        return mine, theirs

    def join_rows(self, mine, theirs):
        return jnp.where(
            self.half == 0,
            jnp.concatenate([mine, theirs], axis=0),
            jnp.concatenate([theirs, mine], axis=0),
        )

    def outer_rows(self, value, extra):
        length = value.shape[0]
        edge = jnp.where(self.half == 0, value[:extra], value[length - extra :])
        return self.flip(edge, 1)

    def with_outer(self, value, extra):
        outer = self.outer_rows(value, extra)
        return jnp.where(
            self.half == 0,
            jnp.concatenate([outer, value], axis=0),
            jnp.concatenate([value, outer], axis=0),
        )

    def halo(self, value, first_row, last_row, flipped):
        pole = jnp.where(self.strip == 0, value[first_row], value[last_row])
        count = value.shape[0]
        ahead = self.to_prev(jnp.concatenate([value[:, 0], pole], axis=0))
        left = self.to_next(value[:, -1])
        pole = jnp.where(flipped, ahead[count:][::-1], ahead[count:])
        return left, ahead[:count], pole

    def halo_back(self, grad, rows, flipped):
        breadth = grad.shape[1]
        left, right = grad[rows + 4, : rows + 2], grad[rows + 7, : rows + 2]
        pole = jnp.where(self.strip == 0, grad[0], grad[rows + 1])
        corner = jnp.where(self.strip == 0, 0, rows + 1)
        inner = jnp.where(self.strip == 0, 1, rows)
        index = jnp.arange(rows + 2)[:, None]
        corners = []
        for name in range(2):
            rim = (left, right)[name]
            value = jnp.sum(jnp.where(index == corner, rim, 0.0), axis=0, keepdims=True)
            corners.append(0.5 * value * jnp.where(self.at_pole, 1.0, 0.0))
        left = left + jnp.where(index == inner, corners[0], 0.0)
        right = right + jnp.where(index == inner, corners[1], 0.0)
        column = jnp.arange(breadth)[:, None]
        pole = pole + jnp.where(column == 0, corners[0], 0.0)
        pole = pole + jnp.where(column == breadth - 1, corners[1], 0.0)
        pole = jnp.where(flipped, pole[::-1], pole)
        behind = self.to_next(jnp.concatenate([right, pole], axis=0))
        add_last = self.to_prev(left)
        add_pole = jnp.where(self.at_pole, behind[rows + 2 :], 0.0)
        return behind[: rows + 2], add_last, add_pole


def masked_stats(place, sea_weight, features):
    count = jnp.sum(sea_weight)
    mean = jnp.sum(sea_weight * features, axis=(0, 1)) / jnp.maximum(count, 1.0)
    centred = features - mean
    spread = jnp.sum(sea_weight * centred * centred, axis=(0, 1))
    state = jnp.stack([jnp.full_like(mean, count), mean, spread])
    for bit in place.bits():
        first, second = place.ordered(state, place.flip(state, bit), bit)
        total = first[0] + second[0]
        safe = jnp.maximum(total, 1.0)
        step = second[1] - first[1]
        state = jnp.stack(
            [
                total,
                (first[0] * first[1] + second[0] * second[1]) / safe,
                first[2] + second[2] + step * step * (first[0] * second[0] / safe),
            ]
        )
    return state[0], state[1], state[2] / state[0]


def bits_of(value):
    high = lax.reduce_precision(value, 8, 7)
    return high.astype(BF16), (value - high).astype(BF16)


def local(
    mesh, features, sea_mask, edge_flip, w_first, b_first, w_second, b_second, w_skip, b_skip,
    run_mean, run_var, cotangent,
):
    rows, breadth, own = features.shape
    place = Place(mesh, rows, breadth)
    size, depth = rows // 2, 2 * own
    flags = jnp.stack([place.at_top, place.at_bottom, place.side == 1]).astype(jnp.int32)
    flip_row = jnp.sum(jnp.where((jnp.arange(4) == place.ribbon)[:, None], edge_flip, 0), axis=0)
    flipped = jnp.where(place.strip == 0, flip_row[0], flip_row[1]) == 1

    packed = jnp.concatenate(
        [
            w_first.reshape(-1, own),
            w_second.reshape(-1, own),
            w_skip,
            b_first[None],
            b_second[None],
            b_skip[None],
        ],
        axis=0,
    )
    unit = 8 * place.count
    packed = jnp.pad(packed, ((0, -packed.shape[0] % unit), (0, 0)))
    share = packed.shape[0] // place.count
    other = place.across(lax.dynamic_slice_in_dim(packed, place.pix * share, share, 0))
    other = place.gathered(other)
    full = jnp.concatenate([packed, other], axis=1)

    def swapped(weights):
        return jnp.where(place.side == 0, weights, jnp.roll(weights, own, axis=-2))

    taps = 9 * depth
    first_full = swapped(full[:taps].reshape(3, 3, depth, depth))
    second_full = swapped(full[taps : 2 * taps].reshape(3, 3, depth, depth))
    skip_full = swapped(full[2 * taps : 2 * taps + depth])
    biases = full[2 * taps + depth : 2 * taps + depth + 3]

    def forward_weights(weights):
        return bits_of(weights.reshape(3, 3 * depth, depth))

    def backward_weights(weights):
        return bits_of(weights[::-1, ::-1].transpose(0, 1, 3, 2).reshape(3, 3 * depth, depth))

    mine, theirs = place.halves(features, 4, size)
    got = place.across(theirs)
    cot_mine, cot_theirs = place.halves(cotangent, 2, size)
    cot_got = place.across(cot_theirs)

    sea_weight = sea_mask.astype(F32)[:, :, None]
    sea_count, batch_mean, batch_var = masked_stats(place, sea_weight, features)
    inverse = lax.rsqrt(batch_var + EPSILON)
    moments = jnp.stack([batch_mean, inverse])
    moments = jnp.concatenate([moments, place.across(moments)], axis=1)

    weight_mine, _ = place.halves(sea_weight, 4, size)
    scaled = weight_mine * (jnp.concatenate([mine, got], axis=2) - moments[0]) * moments[1]
    scaled = place.with_outer(scaled, 4)
    x_left, x_right, x_pole = place.halo(scaled, 4, size + 3, flipped)

    def shift_scratch(blocks):
        return [pltpu.VMEM((blocks * breadth, 3 * depth), BF16) for _ in range(2)]

    def edges():
        return [pltpu.VMEM((breadth + 8, depth), F32) for _ in range(2)]

    def turned():
        return [pltpu.VMEM((depth, size * breadth), BF16) for _ in range(2)]

    hidden, slope_first = call(
        functools.partial(first_kernel, tile=9),
        [(size + 6, breadth, depth)] * 2,
        shift_scratch(size + 8),
        flags, scaled, x_left, x_right, x_pole, *forward_weights(first_full), biases[0:1],
    )
    h_left, h_right, h_pole = place.halo(hidden, 3, size + 2, flipped)
    out_rows, slope_second = call(
        functools.partial(second_kernel, tile=13),
        [(size + 4, breadth, depth)] * 2,
        shift_scratch(size + 6),
        flags, hidden, h_left, h_right, h_pole, *forward_weights(second_full), biases[1:2],
        scaled, *bits_of(skip_full), biases[2:3],
    )
    out_rows = out_rows[2 : size + 2]
    output = place.join_rows(out_rows[:, :, :own], place.across(out_rows[:, :, own:]))

    cot = place.with_outer(jnp.concatenate([cot_mine, cot_got], axis=2), 2)
    upper, grad_second = call(
        functools.partial(back_second_kernel, tile=8),
        [(size + 8, breadth, depth), (size, breadth, depth)],
        shift_scratch(size + 10) + edges(),
        flags, cot, slope_second, *backward_weights(second_full),
    )
    add_first, add_last, add_pole = place.halo_back(upper, size, flipped)
    gw_second, gb_second = call(
        functools.partial(weight_kernel, begin=2, top=2, bottom=size + 3, skip=False),
        [(3, 3, depth, depth), (1, depth)],
        shift_scratch(size + 2) + turned(),
        flags, hidden, h_left, h_right, h_pole, grad_second,
    )
    lower, grad_first = call(
        functools.partial(back_first_kernel, tile=8),
        [(size + 8, breadth, depth), (size, breadth, depth)],
        shift_scratch(size + 10) + edges(),
        flags, upper, add_first, add_last, add_pole, slope_first, cot,
        *backward_weights(first_full), *bits_of(skip_full.T),
    )
    add_first, add_last, add_pole = place.halo_back(lower, size, flipped)
    gw_first, gb_first, gw_skip, gb_skip = call(
        functools.partial(weight_kernel, begin=3, top=3, bottom=size + 4, skip=True),
        [(3, 3, depth, depth), (1, depth), (depth, depth), (1, depth)],
        shift_scratch(size + 2) + turned(),
        flags, scaled, x_left, x_right, x_pole, grad_first, cot,
    )

    column = jnp.arange(breadth)[None, :, None]
    row = jnp.arange(size)[:, None, None]
    edge = jnp.where(place.strip == 0, 0, size - 1)
    grad_in = lower[1 : size + 1]
    grad_in = grad_in + jnp.where(column == 0, add_first[1 : size + 1, None], 0.0)
    grad_in = grad_in + jnp.where(column == breadth - 1, add_last[1 : size + 1, None], 0.0)
    grad_in = grad_in + jnp.where(row == edge, add_pole[None], 0.0)
    own_weight = lax.dynamic_slice_in_dim(sea_weight, place.half * size, size, 0)
    first_sum = jnp.sum(own_weight * grad_in, axis=(0, 1))
    second_sum = jnp.sum(scaled[4 : size + 4] * grad_in, axis=(0, 1))
    sums = jnp.concatenate(
        [gb_first, gb_second, gb_skip, first_sum[None], second_sum[None]], axis=0
    )
    sums = place.summed(sums)
    sums = sums[:, :own] + place.across(sums[:, own:])
    grad_in = place.join_rows(grad_in[:, :, :own], place.across(grad_in[:, :, own:]))
    normed = (features - batch_mean) * inverse
    grad_features = (
        sea_weight * inverse * (grad_in - sums[3] / sea_count - normed * sums[4] / sea_count)
    )

    def all_summed(grad):
        part = place.reduced(grad)
        part = part[:, :own] + place.across(part[:, own:])
        return place.spread(part)

    gw_second = all_summed(
        jnp.concatenate([gw_second.reshape(taps, depth), gw_skip], axis=0)
    )
    gw_first = all_summed(gw_first.reshape(taps, depth))
    new_mean = (1.0 - MOMENTUM) * run_mean + MOMENTUM * batch_mean
    new_var = (1.0 - MOMENTUM) * run_var + MOMENTUM * batch_var * sea_count / (sea_count - 1.0)
    return (
        output,
        grad_features,
        gw_first.reshape(3, 3, depth, own),
        sums[0],
        gw_second[:taps].reshape(3, 3, depth, own),
        sums[1],
        gw_second[taps:],
        sums[2],
        new_mean,
        new_var,
    )


def solution(mesh):
    field, kernel, vector = P("pix", None, "ch"), P(None, None, None, "ch"), P("ch")
    placed = (
        field, P("pix", None), P(), kernel, vector, kernel, vector, P(None, "ch"), vector,
        vector, vector, field,
    )
    return jax.shard_map(
        functools.partial(local, mesh),
        mesh=mesh,
        in_specs=placed,
        out_specs=(
            field, field, kernel, vector, kernel, vector, P(None, "ch"), vector, vector, vector,
        ),
        check_vma=False,
    )
```

```python
import functools

import jax
import jax.numpy as jnp
from jax import lax
from jax.experimental import pallas as pl
from jax.experimental.pallas import tpu as pltpu
from jax.sharding import PartitionSpec as P

EPSILON = 1e-05
MOMENTUM = 0.1
INV_ROOT_TWO_PI = 0.3989422804014327
SQRT_HALF = 0.7071067811865476
F32 = jnp.float32
BF16 = jnp.bfloat16
VMEM_LIMIT = 60 * 1024 * 1024


def split(value):
    high = value.astype(BF16)
    return high, (value - high.astype(F32)).astype(BF16)


def dot_split(a_high, a_low, b_high, b_low):
    total = jnp.dot(a_high, b_high, preferred_element_type=F32)
    total = total + jnp.dot(a_high, b_low, preferred_element_type=F32)
    return total + jnp.dot(a_low, b_high, preferred_element_type=F32)


def gelu_and_slope(u):
    cdf = 0.5 * (1.0 + lax.erf(u * SQRT_HALF))
    return u * cdf, cdf + u * jnp.exp(-0.5 * u * u) * INV_ROOT_TWO_PI


def put_shifts(high, low, block, value, left, right):
    breadth, depth = value.shape
    column = lax.broadcasted_iota(jnp.int32, (breadth, 1), 0)
    shifts = (
        jnp.where(column == 0, left, pltpu.roll(value, 1, 0)),
        value,
        jnp.where(column == breadth - 1, right, pltpu.roll(value, breadth - 1, 0)),
    )
    for tap, piece in enumerate(shifts):
        piece_high, piece_low = split(piece)
        high[pl.ds(block * breadth, breadth), tap * depth : (tap + 1) * depth] = piece_high
        low[pl.ds(block * breadth, breadth), tap * depth : (tap + 1) * depth] = piece_low


def conv_rows(high, low, w_high, w_low, first, rows, breadth):
    total = None
    for row_tap in range(3):
        window = pl.ds(pl.multiple_of((first + row_tap) * breadth, breadth), rows * breadth)
        part = dot_split(high[window, :], low[window, :], w_high[row_tap], w_low[row_tap])
        total = part if total is None else total + part
    return total


AT_TOP, AT_BOTTOM, SIDE, HALF, FLIPPED, PIX = range(6)
NOT_SEA = 1e30


def put_padded(flags, x, left, ahead, pole, high, low, begin, count, top, bottom):
    rows, breadth = x.shape[0], x.shape[1]

    @pl.loop(0, count)
    def _(block):
        row = block + begin
        put_shifts(high, low, block, x[row], left[pl.ds(row, 1)], ahead[pl.ds(row, 1)])

    def put_pole(at, edge):
        @pl.when(flags[FLIPPED] == 1)
        def _():
            for column in range(breadth):
                pole[column : column + 1] = ahead[rows + breadth - 1 - column : rows + breadth - column]

        @pl.when(flags[FLIPPED] == 0)
        def _():
            pole[...] = ahead[rows : rows + breadth]

        corner_left = 0.5 * (pole[0:1] + left[edge : edge + 1])
        corner_right = 0.5 * (pole[breadth - 1 : breadth] + ahead[edge : edge + 1])
        put_shifts(high, low, at - begin, pole[...], corner_left, corner_right)

    @pl.when(flags[AT_TOP] == 1)
    def _():
        put_pole(top, top + 1)

    @pl.when(flags[AT_BOTTOM] == 1)
    def _():
        put_pole(bottom, bottom - 1)


def put_messages(flags, x, to_prev, to_next, first_row, last_row):
    rows, breadth = x.shape[0], x.shape[1]

    @pl.loop(0, rows)
    def _(row):
        to_prev[pl.ds(row, 1)] = x[row, 0:1]
        to_next[pl.ds(row, 1)] = x[row, breadth - 1 : breadth]

    to_prev[rows : rows + breadth] = x[jnp.where(flags[AT_BOTTOM] == 1, last_row, first_row)]


def first_kernel(
    flags, marked, got, halo_mine, halo_got, w_high, w_low, biases,
    scaled, x_left, x_ahead, hidden, slope, to_prev, to_next, pole, high, low, *, tile
):
    blocks, breadth, depth = scaled.shape
    own = depth // 2
    extra = blocks - got.shape[0]
    tail = halo_mine.shape[0] - 8
    start = flags[HALF] * (marked.shape[0] - got.shape[0])

    def normal(value, lanes):
        source = halo_mine if lanes.start == 0 else halo_got
        mean, inverse = source[tail : tail + 1], source[tail + 1 : tail + 2]
        return jnp.where(value > 0.1 * NOT_SEA, 0.0, (value - mean) * inverse)

    lower, upper = slice(0, own), slice(own, depth)
    main = jnp.where(flags[HALF] == 0, extra, 0)
    outer = jnp.where(flags[HALF] == 0, 0, blocks - extra)

    @pl.loop(0, got.shape[0])
    def _(row):
        scaled[main + row, :, lower] = normal(marked[start + row], lower)
        scaled[main + row, :, upper] = normal(got[row], upper)

    for row in range(extra):
        rows = slice(row * breadth, (row + 1) * breadth)
        scaled[outer + row, :, lower] = normal(halo_mine[rows], lower)
        scaled[outer + row, :, upper] = normal(halo_got[rows], upper)

    begin = extra * breadth
    for target, start, count in (
        (x_left, begin, blocks),
        (x_ahead, begin + blocks, blocks + breadth),
    ):
        rows = slice(start, start + count)
        target[:, lower] = normal(halo_mine[rows], lower)
        target[:, upper] = normal(halo_got[rows], upper)

    put_padded(flags, scaled, x_left, x_ahead, pole, high, low, 0, blocks, 3, blocks - 4)

    @pl.loop(0, (blocks - 2) // tile)
    def _(step):
        first = step * tile
        pre = conv_rows(high, low, w_high, w_low, first, tile, breadth) + biases[0:1]
        value, grad = gelu_and_slope(pre)
        hidden[pl.ds(first, tile)] = value.reshape(tile, breadth, depth)
        slope[pl.ds(first, tile)] = grad.reshape(tile, breadth, depth)

    put_messages(flags, hidden, to_prev, to_next, 3, blocks - 6)


def second_kernel(
    flags, x, left, ahead, w_high, w_low, biases, source, s_high, s_low,
    out_own, out_send, slope, pole, high, low, *, tile
):
    blocks, breadth, depth = x.shape
    own = depth // 2
    put_padded(flags, x, left, ahead, pole, high, low, 0, blocks, 2, blocks - 3)

    @pl.loop(0, (blocks - 2) // tile)
    def _(step):
        first = step * tile
        pre = conv_rows(high, low, w_high, w_low, first, tile, breadth) + biases[1:2]
        value, grad = gelu_and_slope(pre)
        slope[pl.ds(first, tile)] = grad.reshape(tile, breadth, depth)
        skip_high, skip_low = split(source[pl.ds(first + 2, tile)].reshape(tile * breadth, -1))
        skip = dot_split(skip_high, skip_low, s_high[...], s_low[...]) + biases[2:3]
        value = (value + skip).reshape(tile, breadth, depth)
        for block in range(tile):
            row = first + block - 2

            @pl.when((row >= 0) & (row < blocks - 6))
            def _():
                out_own[row] = value[block, :, :own]
                out_send[row] = value[block, :, own:]


def back_conv(flags, high, low, w_high, w_low, edge_first, edge_last, out, to_next, to_prev, blocks, breadth, tile):
    depth = edge_first.shape[1]
    for tap in range(3):
        for edge, slot, base in ((edge_first, 2, blocks), (edge_last, 0, blocks + 3)):
            rows = pl.ds((base + tap) * breadth, breadth)
            edge_high, edge_low = split(edge[tap : tap + breadth])
            zero = jnp.zeros((breadth, 3 * depth), BF16)
            high[rows, :] = zero
            low[rows, :] = zero
            high[rows, slot * depth : (slot + 1) * depth] = edge_high
            low[rows, slot * depth : (slot + 1) * depth] = edge_low

    @pl.loop(0, (blocks + 4) // tile)
    def _(step):
        first = step * tile
        out[pl.ds(first, tile)] = conv_rows(high, low, w_high, w_low, first, tile, breadth).reshape(
            tile, breadth, depth
        )

    count = blocks - 2
    to_prev[...] = out[blocks][:count]
    to_next[:count] = out[blocks + 3][:count]
    to_next[count:] = jnp.zeros((breadth, depth), F32)

    def put_pole(at, inner):
        corner_left = 0.5 * out[blocks][at : at + 1]
        corner_right = 0.5 * out[blocks + 3][at : at + 1]
        to_prev[inner : inner + 1] += corner_left
        to_next[inner : inner + 1] += corner_right
        column = lax.broadcasted_iota(jnp.int32, (breadth, 1), 0)
        row = out[at] + jnp.where(column == 0, corner_left, 0.0)
        row = row + jnp.where(column == breadth - 1, corner_right, 0.0)

        @pl.when(flags[FLIPPED] == 0)
        def _():
            to_next[count:] = row

        @pl.when(flags[FLIPPED] == 1)
        def _():
            for k in range(breadth):
                to_next[count + k : count + k + 1] = row[breadth - 1 - k : breadth - k]

    @pl.when(flags[AT_TOP] == 1)
    def _():
        put_pole(0, 1)

    @pl.when(flags[AT_BOTTOM] == 1)
    def _():
        put_pole(count - 1, count - 2)


def outside_pole(flags, block, blocks):
    return ((flags[AT_TOP] == 1) & (block < 2)) | ((flags[AT_BOTTOM] == 1) & (block >= blocks - 2))


def back_second_kernel(
    flags, cot_mine, cot_got, slope, w_high, w_low,
    out, grad, to_next, to_prev, high, low, edge_first, edge_last, *, tile
):
    blocks, breadth, depth = slope.shape
    edge_first[...] = jnp.zeros_like(edge_first)
    edge_last[...] = jnp.zeros_like(edge_last)

    @pl.loop(0, blocks)
    def _(block):
        outside = outside_pole(flags, block, blocks)
        value = jnp.concatenate([cot_mine[block], cot_got[block]], axis=1)
        value = value * slope[block] * jnp.where(outside, 0.0, 1.0)
        put_shifts(high, low, block, value, 0.0, 0.0)
        edge_first[pl.ds(block, 1)] = value[0:1]
        edge_last[pl.ds(block, 1)] = value[breadth - 1 : breadth]

        @pl.when((block >= 2) & (block < blocks - 2))
        def _():
            grad[block - 2] = value

    back_conv(
        flags, high, low, w_high, w_low, edge_first, edge_last, out, to_next, to_prev, blocks, breadth, tile
    )


def grad_first_kernel(flags, upper, behind, after, slope, grad):
    count, breadth, _ = grad.shape
    column = lax.broadcasted_iota(jnp.int32, (breadth, 1), 0)

    @pl.loop(0, count)
    def _(row):
        outside = ((flags[AT_TOP] == 1) & (row < 1)) | ((flags[AT_BOTTOM] == 1) & (row >= count - 1))
        edge = ((flags[AT_TOP] == 1) & (row == 1)) | ((flags[AT_BOTTOM] == 1) & (row == count - 2))
        value = upper[row] + jnp.where(column == 0, behind[pl.ds(row, 1)], 0.0)
        value = value + jnp.where(column == breadth - 1, after[pl.ds(row, 1)], 0.0)
        value = value + behind[count : count + breadth] * jnp.where(edge, 1.0, 0.0)
        grad[row] = value * slope[row + 2] * jnp.where(outside, 0.0, 1.0)


def back_first_kernel(
    flags, grad, cot_mine, cot_got, w_high, w_low, s_high, s_low,
    out_own, out_send, to_next, to_prev, out, high, low, edge_first, edge_last, *, tile
):
    blocks, breadth, own = cot_mine.shape
    depth = 2 * own
    edge_first[...] = jnp.zeros_like(edge_first)
    edge_last[...] = jnp.zeros_like(edge_last)
    none = jnp.zeros((breadth, depth), F32)
    put_shifts(high, low, 0, none, 0.0, 0.0)
    put_shifts(high, low, blocks - 1, none, 0.0, 0.0)

    @pl.loop(1, blocks - 1)
    def _(block):
        value = grad[block - 1]
        put_shifts(high, low, block, value, 0.0, 0.0)
        edge_first[pl.ds(block, 1)] = value[0:1]
        edge_last[pl.ds(block, 1)] = value[breadth - 1 : breadth]

    back_conv(
        flags, high, low, w_high, w_low, edge_first, edge_last, out, to_next, to_prev, blocks, breadth, tile
    )

    @pl.loop(0, (blocks - 4) // tile)
    def _(step):
        first = step * tile
        rows = pl.ds(first + 2, tile)
        cot = jnp.concatenate([cot_mine[rows], cot_got[rows]], axis=2).reshape(tile * breadth, depth)
        cot_high, cot_low = split(cot)
        skip = dot_split(cot_high, cot_low, s_high[...], s_low[...]).reshape(tile, breadth, depth)
        total = out[pl.ds(first + 1, tile)] + skip
        out_own[pl.ds(first, tile)] = total[:, :, :own]
        out_send[pl.ds(first, tile)] = total[:, :, own:]


def put_transposed(read, rows, breadth, high, low, total, tile):
    total[...] = jnp.zeros_like(total)

    @pl.loop(0, rows // tile)
    def _(step):
        piece = read(step * tile, tile)
        total[...] += jnp.sum(piece, axis=0, keepdims=True)
        piece_high, piece_low = split(piece.T)
        window = pl.ds(pl.multiple_of(step * tile * breadth, tile * breadth), tile * breadth)
        high[:, window] = piece_high
        low[:, window] = piece_low


def put_weight_grad(flags, parts, tap, grad):
    half = grad.shape[0] // 2
    first = (flags[SIDE] ^ flags[PIX]) & 1
    parts[first, tap] = grad[:half]
    parts[1 - first, tap] = grad[half:]


def weight_kernel(flags, x, left, ahead, grad, *rest, begin, top, bottom, skip, offset):
    if skip:
        source, cot_mine, cot_got, keep, send, total, total_skip, pole, high, low, t_high, t_low, parts, sems = rest
    else:
        behind, after, slope, keep, send, total, grad_out, pole, high, low, t_high, t_low, parts, sems = rest
        grad_first_kernel(flags, grad, behind, after, slope, grad_out)
        grad = grad_out
    rows, breadth, depth = grad.shape[0] - 2 * offset, grad.shape[1], grad.shape[2]
    put_padded(flags, x, left, ahead, pole, high, low, begin, rows + 2, top, bottom)

    def read_grad(first, count):
        return grad[pl.ds(first + offset, count)].reshape(count * breadth, depth)

    put_transposed(read_grad, rows, breadth, t_high, t_low, total, 4)
    @pl.loop(0, 3)
    def _(row_tap):
        window = pl.ds(pl.multiple_of(row_tap * breadth, breadth), rows * breadth)
        for tap in range(3):
            lanes = slice(tap * depth, (tap + 1) * depth)
            part = dot_split(t_high[...], t_low[...], high[window, lanes], low[window, lanes])
            put_weight_grad(flags, parts, row_tap * 3 + tap, part.T)

    if skip:
        def read_cot(first, count):
            window = pl.ds(first + 2, count)
            value = jnp.concatenate([cot_mine[window], cot_got[window]], axis=2)
            return value.reshape(count * breadth, depth)

        put_transposed(read_cot, rows, breadth, t_high, t_low, total_skip, 4)

        @pl.loop(0, rows)
        def _(row):
            row_high, row_low = split(source[row + 4])
            high[pl.ds(row * breadth, breadth), :depth] = row_high
            low[pl.ds(row * breadth, breadth), :depth] = row_low

        window, lanes = slice(0, rows * breadth), slice(0, depth)
        part = dot_split(t_high[...], t_low[...], high[window, lanes], low[window, lanes])
        put_weight_grad(flags, parts, 9, part.T)

    copies = [
        pltpu.make_async_copy(parts.at[k], (keep, send)[k], sems.at[k]) for k in range(2)
    ]
    for copy in copies:
        copy.start()
    for copy in copies:
        copy.wait()


def weights_kernel(flags, mine, *rest, steps, skip):
    shares, rest = rest[: steps + 1], rest[steps + 1 :]
    if skip:
        mine_skip, f_high, f_low, b_high, b_low, s_high, s_low, sb_high, sb_low, other = rest
    else:
        f_high, f_low, b_high, b_low, other = rest
    own = mine.shape[1]
    depth = 2 * own
    taps = mine.shape[0]
    count = 1 << steps
    share, share_skip = taps // count, depth // count
    unit = shares[0].shape[0]
    begin = share if skip else 0
    for piece in range(count):
        away = sum(1 << (steps - 1 - step) for step in range(steps) if piece >> step & 1)
        index = (flags[PIX] & (count - 1)) ^ away
        level = piece.bit_length()
        source = shares[level]
        at = (piece - (1 << (level - 1)) if level else 0) * unit + begin
        other[pl.ds(pl.multiple_of(index * share, 8), share)] = source[at : at + share]
        if skip:
            start = pl.multiple_of(taps + index * share_skip, 8)
            other[pl.ds(start, share_skip)] = source[at + share : at + share + share_skip]
    def both(first, second):
        return jnp.concatenate([first, second], axis=1)

    @pl.loop(0, 9)
    def _(tap):
        row_tap, column_tap = tap // 3, tap % 3
        back_row, back_column = 2 - row_tap, 2 - column_tap
        for part in range(2):
            at = pl.multiple_of(tap * depth + jnp.where(flags[SIDE] == part, 0, own), own)
            value = both(mine[pl.ds(at, own)], other[pl.ds(at, own)])
            value_high, value_low = split(value)
            place = pl.ds(pl.multiple_of(column_tap * depth + part * own, own), own)
            f_high[row_tap, place] = value_high
            f_low[row_tap, place] = value_low
            turned_high, turned_low = split(value.T)
            place = pl.ds(pl.multiple_of(back_column * depth, depth), depth)
            lanes = slice(part * own, (part + 1) * own)
            b_high[back_row, place, lanes] = turned_high
            b_low[back_row, place, lanes] = turned_low

    if skip:
        for part in range(2):
            at = pl.multiple_of(jnp.where(flags[SIDE] == part, 0, own), own)
            value = both(mine_skip[pl.ds(at, own)], other[pl.ds(pl.multiple_of(taps + at, own), own)])
            lanes = slice(part * own, (part + 1) * own)
            s_high[lanes], s_low[lanes] = split(value)
            sb_high[:, lanes], sb_low[:, lanes] = split(value.T)


def pre_kernel(flags, features, mask, marked, theirs, stats, inner, to_prev, to_next):
    rows, breadth, own = features.shape
    length = theirs.shape[0]
    start = (1 - flags[HALF]) * (rows - length)
    turned = mask[...].astype(F32)
    turned = jnp.concatenate([turned, jnp.zeros((breadth, 128 - rows), F32)], axis=1)
    none = jnp.zeros((8, own), F32)

    def fold(v):
        return jnp.sum(v.reshape(breadth // 8, 8, own), axis=0)

    def first(step, carry):
        count, total = carry
        base = step * 8
        sea_of = pltpu.roll(turned, 128 - base, 1)
        for k in range(8):
            row = base + k
            sea = jnp.broadcast_to(sea_of[:, k : k + 1], (breadth, own))
            value = features[row]
            land = jnp.where(sea > 0.5, value, NOT_SEA)
            marked[row] = land
            to_prev[pl.ds(row, 1)] = land[0:1]
            to_next[pl.ds(row, 1)] = land[breadth - 1 : breadth]
            count, total = count + fold(sea), total + fold(value * sea)
        return count, total

    count, total = lax.fori_loop(0, rows // 8, first, (none, none))
    count = jnp.sum(count, axis=0, keepdims=True)
    mean = jnp.sum(total, axis=0, keepdims=True) / jnp.maximum(count, 1.0)

    def second(step, squares):
        for k in range(8):
            value = marked[step * 8 + k]
            value = jnp.where(value > 0.1 * NOT_SEA, 0.0, value - mean)
            squares = squares + fold(value * value)
        return squares

    squares = lax.fori_loop(0, rows // 8, second, none)

    @pl.loop(0, length // 4)
    def _(step):
        theirs[pl.ds(step * 4, 4)] = marked[pl.ds(start + step * 4, 4)]

    stats[...] = jnp.zeros_like(stats)
    stats[0:1] = count
    stats[1:2] = mean
    stats[2:3] = jnp.sum(squares, axis=0, keepdims=True)
    strip = flags[SIDE] ^ flags[HALF]
    to_prev[rows:] = marked[strip * (rows - 1)]
    inner[...] = marked[pl.ds((1 - strip) * (rows - inner.shape[0]), inner.shape[0])]


def rims_kernel(flags, behind, ahead, core, stats, mine, theirs, wide):
    rows, own = behind.shape
    breadth = ahead.shape[0] - rows
    extra = (core.shape[0]) // (breadth + 2)
    length = rows // 2 + 2 * extra
    inner = extra * breadth
    at = inner
    for target in (mine, theirs):
        target[:inner] = core[:inner]
    for source, start in ((behind, inner + extra), (ahead, inner)):
        wide[:extra] = core[start : start + extra]
        wide[extra : extra + rows] = source[:rows]
        wide[extra + rows :] = core[start : start + extra]
        for target, half in ((mine, flags[HALF]), (theirs, 1 - flags[HALF])):
            target[at : at + length] = wide[pl.ds(pl.multiple_of(half * (rows // 2), 8), length)]
        at = at + length
    count, mean, squares = stats[0:1], stats[1:2], stats[2:3]
    inverse = lax.rsqrt(squares / count + EPSILON)
    for target in (mine, theirs):
        target[at : at + breadth] = ahead[rows:]
        target[at + breadth :] = jnp.zeros((8, own), F32)
        target[at + breadth : at + breadth + 1] = mean
        target[at + breadth + 1 : at + breadth + 2] = inverse


def final_kernel(flags, marked, lower, rims, stats, sums, *rest, other, parts):
    out, source, result, in_sems, out_sems = rest[-5:]
    rows, breadth, own = marked.shape
    size = rows // 2
    step = size // parts
    last = size + 2 + breadth
    count, mean = stats[0:1], stats[1:2]
    inverse = lax.rsqrt(stats[2:3] / count + EPSILON)
    first_mean, second_mean = sums[3:4] / count, sums[4:5] / count
    column = lax.broadcasted_iota(jnp.int32, (breadth, 1), 0)
    strip = flags[SIDE] ^ flags[HALF]
    edge = strip * (size - 1)
    half = 1 - flags[HALF] if other else flags[HALF]
    at_pole = flags[SIDE] == (1 if other else 0)

    def fetch(part):
        rows = pl.ds(half * size + part * step, step)
        return pltpu.make_async_copy(marked.at[rows], source.at[pl.ds(part * step, step)], in_sems.at[part])

    def store(part):
        rows = pl.ds(half * size + part * step, step)
        return pltpu.make_async_copy(result.at[pl.ds(part * step, step)], out.at[rows], out_sems.at[part])

    for part in range(parts):
        fetch(part).start()
    for part in range(parts):
        fetch(part).wait()

        @pl.loop(part * step, (part + 1) * step)
        def _(row):
            value = lower[row] + jnp.where(column == 0, rims[pl.ds(row + 1, 1)], 0.0)
            value = value + jnp.where(column == breadth - 1, rims[pl.ds(row + last + 1, 1)], 0.0)
            at_edge = jnp.where((row == edge) & at_pole, 1.0, 0.0)
            value = value + rims[size + 2 : last] * at_edge
            normed = (source[row] - mean) * inverse
            value = inverse * (value - first_mean - normed * second_mean)
            result[row] = jnp.where(source[row] > 0.1 * NOT_SEA, 0.0, value)

        store(part).start()
    for part in range(parts):
        store(part).wait()


def final_call(other, flags, marked, lower, rims, stats, sums, before=None):
    anywhere, whole = pl.BlockSpec(memory_space=pl.ANY), pl.BlockSpec(memory_space=pltpu.VMEM)
    parts = 4
    operands = [flags, marked, lower, rims, stats, sums] + ([before] if other else [])
    half = pltpu.VMEM(lower.shape, F32)
    return pl.pallas_call(
        functools.partial(final_kernel, other=other, parts=parts),
        out_shape=jax.ShapeDtypeStruct(marked.shape, F32),
        in_specs=[pl.BlockSpec(memory_space=pltpu.SMEM), anywhere] + [whole] * 4 + [anywhere] * other,
        out_specs=anywhere,
        scratch_shapes=[half, half, pltpu.SemaphoreType.DMA((parts,)), pltpu.SemaphoreType.DMA((parts,))],
        input_output_aliases={6: 0} if other else {},
        compiler_params=pltpu.CompilerParams(vmem_limit_bytes=VMEM_LIMIT),
        cost_estimate=pl.CostEstimate(flops=0, bytes_accessed=0, transcendentals=0),
        name="final_got" if other else "final_own",
    )(*operands)


def join_kernel(flags, mine, theirs, out, sems):
    size = mine.shape[0]
    one = pltpu.make_async_copy(mine, out.at[pl.ds(flags[HALF] * size, size)], sems.at[0])
    two = pltpu.make_async_copy(theirs, out.at[pl.ds((1 - flags[HALF]) * size, size)], sems.at[1])
    one.start()
    two.start()
    one.wait()
    two.wait()


def call_copy(kernel, shape, flags, *operands):
    anywhere = pl.BlockSpec(memory_space=pl.ANY)
    return pl.pallas_call(
        kernel,
        out_shape=[jax.ShapeDtypeStruct(shape, F32)],
        in_specs=[pl.BlockSpec(memory_space=pltpu.SMEM)]
        + [pl.BlockSpec(memory_space=pltpu.VMEM)] * len(operands),
        out_specs=[anywhere],
        scratch_shapes=[pltpu.SemaphoreType.DMA((len(operands),))],
        compiler_params=pltpu.CompilerParams(vmem_limit_bytes=VMEM_LIMIT),
        cost_estimate=pl.CostEstimate(flops=0, bytes_accessed=0, transcendentals=0),
        name="join",
    )(flags, *operands)


def call(kernel, shapes, scratch, flags, *operands, name=None, copied=0):
    whole = pl.BlockSpec(memory_space=pltpu.VMEM)
    shapes = [s if isinstance(s, jax.ShapeDtypeStruct) else jax.ShapeDtypeStruct(s, F32) for s in shapes]
    return pl.pallas_call(
        kernel,
        out_shape=shapes,
        in_specs=[pl.BlockSpec(memory_space=pltpu.SMEM)] + [whole] * len(operands),
        out_specs=[pl.BlockSpec(memory_space=pl.ANY)] * copied + [whole] * (len(shapes) - copied),
        scratch_shapes=scratch,
        compiler_params=pltpu.CompilerParams(vmem_limit_bytes=VMEM_LIMIT),
        cost_estimate=pl.CostEstimate(flops=0, bytes_accessed=0, transcendentals=0),
        name=name,
    )(flags, *operands)


class Place:
    def __init__(self, mesh, rows, breadth):
        self.count = mesh.shape["pix"]
        self.strips = 3 * breadth // rows
        assert mesh.shape["ch"] == 2 and self.strips == 2
        self.pix = lax.axis_index("pix")
        self.side = lax.axis_index("ch")
        self.ribbon = self.pix // self.strips % 4
        self.strip = self.pix % self.strips
        self.half = self.side ^ self.strip
        self.at_top = (self.side == 0) & (self.strip == 0)
        self.at_bottom = (self.side == 0) & (self.strip == 1)

    def ribbon_pairs(self, offset):
        pairs = []
        for index in range(self.count):
            sample, strip = index // (4 * self.strips), index % self.strips
            ribbon = (index // self.strips + offset) % 4
            pairs.append((index, (sample * 4 + ribbon) * self.strips + strip))
        return pairs

    def to_next(self, value):
        return lax.ppermute(value, "pix", self.ribbon_pairs(1))

    def to_prev(self, value):
        return lax.ppermute(value, "pix", self.ribbon_pairs(-1))

    def across(self, value):
        return lax.ppermute(value, "ch", [(0, 1), (1, 0)])

    def flip(self, value, bit):
        return lax.ppermute(value, "pix", [(i, i ^ bit) for i in range(self.count)])

    def bits(self):
        return [1 << step for step in range(self.count.bit_length() - 1)]

    def ordered(self, mine, theirs, bit):
        upper = (self.pix & bit) != 0
        return jnp.where(upper, theirs, mine), jnp.where(upper, mine, theirs)

    def near(self):
        return self.bits()[:3]

    def gathered(self, value):
        pieces = [value]
        for bit in reversed(self.near()):
            sent = pieces[0] if len(pieces) == 1 else jnp.concatenate(pieces, axis=0)
            pieces.append(self.flip(sent, bit))
        return pieces

    def members(self, bits):
        out = []
        for other in range(1, 1 << len(bits)):
            mask = sum(bit for step, bit in enumerate(bits) if other >> step & 1)
            out.append((other, [(i, i ^ mask) for i in range(self.count)]))
        return out

    def number(self, bits):
        total = 0
        for step, bit in enumerate(bits):
            total = total + (((self.pix & bit) != 0).astype(jnp.int32) << step)
        return total

    def shared(self, value, bits):
        me, length = self.number(bits), value.shape[0] >> len(bits)
        total = lax.dynamic_slice_in_dim(value, me * length, length, 0)
        parts = []
        for other, pairs in self.members(bits):
            piece = lax.dynamic_slice_in_dim(value, (me ^ other) * length, length, 0)
            parts.append(lax.ppermute(piece, "pix", pairs))
        for part in parts:
            total = total + part
        return total

    def spread(self, value, bits):
        parts = [value] + [lax.ppermute(value, "pix", pairs) for _, pairs in self.members(bits)]
        for step, bit in enumerate(bits):
            upper = (self.pix & bit) != 0
            parts = [
                jnp.where(upper, parts[k ^ (1 << step)], parts[k]) for k in range(len(parts))
            ]
        return jnp.concatenate(parts, axis=0)

    def groups(self):
        bits = self.bits()
        rest = [bits[k : k + 2] for k in range(2, len(bits), 2)]
        return [bits[:1], bits[1:2]] + rest

    def summed(self, value):
        for bit in self.bits():
            first, second = self.ordered(value, self.flip(value, bit), bit)
            value = first + second
        return value

    def part(self, value, half, start, length):
        return lax.dynamic_slice_in_dim(value, half * start, length, 0)

    def join_rows(self, mine, theirs):
        return jnp.where(
            self.half == 0,
            jnp.concatenate([mine, theirs], axis=0),
            jnp.concatenate([theirs, mine], axis=0),
        )

    def inner_rows(self, value, extra):
        edge = jnp.where(self.strip == 0, value[-extra:], value[:extra])
        return self.flip(edge, 1)


def merged_stats(place, state):
    for bit in place.bits():
        first, second = place.ordered(state, place.flip(state, bit), bit)
        total = first[0] + second[0]
        safe = jnp.maximum(total, 1.0)
        step = second[1] - first[1]
        state = jnp.stack(
            [
                total,
                (first[0] * first[1] + second[0] * second[1]) / safe,
                first[2] + second[2] + step * step * (first[0] * second[0] / safe),
            ]
            + [total] * 5
        )
    return state


def local(
    mesh, features, sea_mask, edge_flip, w_first, b_first, w_second, b_second, w_skip, b_skip,
    run_mean, run_var, cotangent,
):
    rows, breadth, own = features.shape
    place = Place(mesh, rows, breadth)
    size, depth = rows // 2, 2 * own
    taps = 9 * depth
    flip_row = jnp.sum(jnp.where((jnp.arange(4) == place.ribbon)[:, None], edge_flip, 0), axis=0)
    flipped = jnp.where(place.strip == 0, flip_row[0], flip_row[1]) == 1
    flags = jnp.stack(
        [
            jnp.where(flag, 1, 0).astype(jnp.int32)
            for flag in (place.at_top, place.at_bottom, place.side == 1, place.half == 1, flipped)
        ]
        + [place.pix.astype(jnp.int32)]
    )

    w_first, w_second = w_first.reshape(taps, own), w_second.reshape(taps, own)
    near = len(place.near())
    share, share_skip, number = taps >> near, depth >> near, place.number(place.near())
    biases = jnp.stack([b_first, b_second, b_skip])
    message = jnp.concatenate(
        [
            lax.dynamic_slice_in_dim(w_first, number * share, share, 0),
            lax.dynamic_slice_in_dim(w_second, number * share, share, 0),
            lax.dynamic_slice_in_dim(w_skip, number * share_skip, share_skip, 0),
            jnp.pad(biases, ((0, 5), (0, 0))),
        ]
    )
    message = place.across(message)
    features, message = lax.optimization_barrier((features, message))
    marked, theirs, stats, inner, to_prev, to_next = call(
        pre_kernel,
        [
            (rows, breadth, own), (size + 4, breadth, own), (8, own), (4, breadth, own),
            (rows + breadth, own), (rows, own),
        ],
        [], flags, features, sea_mask.T, name="pre",
    )
    got = place.across(theirs)
    biases = jnp.concatenate([biases, message[2 * share + share_skip :][:3]], axis=1)
    def neighbours(stats, inner, to_prev, to_next, message):
        shares = place.gathered(message[: 2 * share + share_skip])
        stats = merged_stats(place, stats)
        ahead, behind = place.to_prev(to_prev), place.to_next(to_next)

        def inner_part(value):
            return jnp.where(place.strip == 0, value[rows - 4 : rows], value[:4])

        core = jnp.concatenate(
            [inner.reshape(-1, own), inner_part(ahead), inner_part(behind)], axis=0
        )
        core = place.flip(core, 1)
        halo_mine, halo_theirs = call(
            rims_kernel, [(rim_rows, own)] * 2, [pltpu.VMEM((rows + 8, own), F32)],
            flags, behind, ahead, core, stats, name="rims",
        )
        return stats, halo_mine, halo_theirs, shares

    def block(steps, *operands):
        shapes = jax.eval_shape(steps, *operands)

        def nothing(*operands):
            return jax.tree.map(lambda leaf: jnp.zeros(leaf.shape, leaf.dtype), shapes)

        return lax.cond(edge_flip[0, 0] < 2, steps, nothing, *operands)

    rim_rows = 4 * breadth + 2 * (size + 8) + breadth + 8
    stats, halo_mine, halo_theirs, shares = block(neighbours, stats, inner, to_prev, to_next, message)
    kinds = [jax.ShapeDtypeStruct((3, 3 * depth, depth), BF16)] * 4
    first_weights = call(
        functools.partial(weights_kernel, steps=near, skip=False),
        kinds, [pltpu.VMEM((taps, own), F32)], flags, w_first, *shares,
        name="weights_first",
    )
    sea_count, batch_mean = stats[0], stats[1]
    batch_var = stats[2] / sea_count
    halo_theirs, got = lax.optimization_barrier((halo_theirs, got))
    halo_got = place.across(halo_theirs)

    extra = place.inner_rows(cotangent, 2)
    wide = jnp.concatenate([extra, cotangent, extra], axis=0)
    cot_mine = place.part(wide, place.half, size, size + 4)
    cot_theirs = place.part(wide, 1 - place.half, size, size + 4)
    cot_theirs, halo_got = lax.optimization_barrier((cot_theirs, halo_got))
    cot_got = place.across(cot_theirs)

    small = [jax.ShapeDtypeStruct((depth, depth), BF16)] * 4
    second_weights = call(
        functools.partial(weights_kernel, steps=near, skip=True),
        kinds + small, [pltpu.VMEM((taps + depth, own), F32)], flags,
        w_second, *shares, w_skip,
        name="weights_second",
    )

    def shift_scratch(blocks):
        return [pltpu.VMEM((blocks * breadth, 3 * depth), BF16) for _ in range(2)]

    def edges():
        return [pltpu.VMEM((breadth + 8, depth), F32) for _ in range(2)]

    def turned():
        return [pltpu.VMEM((depth, size * breadth), BF16) for _ in range(2)]

    def halves(count):
        return [pltpu.VMEM((2, count, own, depth), F32), pltpu.SemaphoreType.DMA((2,))]

    pole_row = [pltpu.VMEM((breadth, depth), F32)]

    scaled, x_left, x_ahead, hidden, slope_first, to_prev, to_next = call(
        functools.partial(first_kernel, tile=9),
        [
            (size + 8, breadth, depth), (size + 8, depth), (size + 8 + breadth, depth),
            (size + 6, breadth, depth), (size + 6, breadth, depth),
            (size + 6 + breadth, depth), (size + 6, depth),
        ],
        pole_row + shift_scratch(size + 8),
        flags, marked, got, halo_mine, halo_got, *first_weights[:2], biases,
        name="first",
    )
    h_ahead, h_left = place.to_prev(to_prev), place.to_next(to_next)
    out_own, out_send, slope_second = call(
        functools.partial(second_kernel, tile=4),
        [(size, breadth, own), (size, breadth, own), (size + 4, breadth, depth)],
        pole_row + shift_scratch(size + 6),
        flags, hidden, h_left, h_ahead, *second_weights[:2], biases, scaled, *second_weights[4:6],
        name="second",
    )
    out_got = place.across(out_send)

    rim_shapes = [(size + 2 + breadth, depth), (size + 2, depth)]
    upper, grad_second, to_next, to_prev = call(
        functools.partial(back_second_kernel, tile=8),
        [(size + 8, breadth, depth), (size, breadth, depth)] + rim_shapes,
        shift_scratch(size + 10) + edges(),
        flags, cot_mine, cot_got, slope_second, *second_weights[2:4],
        name="back_second",
    )
    groups = place.groups()

    def second_weights_grad(to_next, to_prev, grad_second):
        behind, after = place.to_next(to_next), place.to_prev(to_prev)
        grads = call(
            functools.partial(weight_kernel, begin=2, top=2, bottom=size + 3, skip=True, offset=0),
            [(10, own, depth)] * 2 + [(1, depth)] * 2,
            pole_row + shift_scratch(size + 2) + turned() + halves(10),
            flags, hidden, h_left, h_ahead, grad_second, scaled, cot_mine, cot_got,
            name="weight_second", copied=2,
        )
        return behind, after, *grads

    behind, after, keep, send, gb_second, gb_skip = block(
        second_weights_grad, to_next, to_prev, grad_second
    )
    out_got, send = lax.optimization_barrier((out_got, send))

    def first_weights_grad(keep, send, upper, behind, after):
        grads = call(
            functools.partial(weight_kernel, begin=3, top=3, bottom=size + 4, skip=False, offset=1),
            [(9, own, depth)] * 2 + [(1, depth), (size + 2, breadth, depth)],
            pole_row + shift_scratch(size + 2) + turned() + halves(9),
            flags, scaled, x_left, x_ahead, upper, behind, after, slope_first,
            name="weight_first", copied=2,
        )
        return (keep + place.flip(send, groups[0][0])).reshape(-1, depth), *grads

    gw_second, keep, send, gb_first, grad_first = block(
        first_weights_grad, keep, send, upper, behind, after
    )

    def input_grad(gw_second, keep, send, grad_first):
        grads = call(
            functools.partial(back_first_kernel, tile=8),
            [(size, breadth, own), (size, breadth, own)] + rim_shapes,
            [pltpu.VMEM((size + 8, breadth, depth), F32)] + shift_scratch(size + 10) + edges(),
            flags, grad_first, cot_mine, cot_got,
            *first_weights[2:4], *second_weights[6:8],
            name="back_first",
        )
        gw_first = (keep + place.flip(send, groups[0][0])).reshape(-1, depth)
        return place.shared(gw_second, groups[1]), gw_first, *grads

    gw_second, gw_first, lower_own, lower_send, to_next, to_prev = block(
        input_grad, gw_second, keep, send, grad_first
    )
    lower_got = place.across(lower_send)

    def last_sums(gw_second, gw_first, to_next, to_prev, lower_own, lower_send, out_own, out_got):
        behind, after = place.to_next(to_next), place.to_prev(to_prev)
        behind, after, gw_first, gw_second = lax.optimization_barrier((behind, after, gw_first, gw_second))
        adds = jnp.concatenate([behind, after], axis=0)
        adds_got = place.across(adds[:, own:])
        column = jnp.arange(breadth)[None, :, None]
        row = jnp.arange(size)[:, None, None]
        edge = jnp.where(place.strip == 0, 0, size - 1)
        at_pole = place.side == 0

        def with_rims(value, adds):
            last = size + 2 + breadth
            value = value + jnp.where(column == 0, adds[1 : size + 1, None], 0.0)
            value = value + jnp.where(column == breadth - 1, adds[last + 1 : last + 1 + size, None], 0.0)
            return value + jnp.where((row == edge) & at_pole, adds[None, size + 2 : last], 0.0)

        sea_weight = sea_mask.astype(F32)[:, :, None]
        own_weight = lax.dynamic_slice_in_dim(sea_weight, place.half * size, size, 0)
        source = scaled[4 : size + 4]
        parts = []
        for value, lanes in ((lower_own, slice(0, own)), (lower_send, slice(own, depth))):
            value = with_rims(value, adds[:, lanes])
            parts.append(
                jnp.stack(
                    [
                        jnp.sum(own_weight * value, axis=(0, 1)),
                        jnp.sum(source[:, :, lanes] * value, axis=(0, 1)),
                    ]
                )
            )
        zeros = jnp.zeros((3, depth), F32)
        sums = [gb_first, gb_second, gb_skip, jnp.concatenate(parts, axis=1), zeros]
        sums = place.summed(jnp.concatenate(sums, axis=0))
        sums = sums[:, :own] + place.across(sums[:, own:])

        def all_summed(grad, begin):
            for bits in groups[begin:]:
                grad = place.shared(grad, bits)
            grad = grad[:, :own] + place.across(grad[:, own:])
            for bits in reversed(groups[1:]):
                grad = place.spread(grad, bits)
            grad = grad.reshape(-1, own, own)
            other = place.flip(grad, groups[0][0])
            return jnp.concatenate(place.ordered(grad, other, groups[0][0]), axis=1)

        gw_second, gw_first = all_summed(gw_second, 2), all_summed(gw_first, 1)
        output, = call_copy(join_kernel, (rows, breadth, own), flags, out_own, out_got)
        adds_own = adds[:, :own]
        grad_half = final_call(0, flags, marked, lower_own, adds_own, stats, sums)
        return gw_second[:9], gw_second[9], gw_first, sums, adds_got, output, grad_half

    gw_second, gw_skip, gw_first, sums, adds_got, output, grad_half = last_sums(
        gw_second, gw_first, to_next, to_prev, lower_own, lower_send, out_own, out_got
    )
    late = (sums, gw_first, gw_second, gw_skip, grad_half, lower_got, adds_got)
    sums, gw_first, gw_second, gw_skip, grad_half, lower_got, adds_got = lax.optimization_barrier(late)
    grad_features = final_call(1, flags, marked, lower_got, adds_got, stats, sums, grad_half)
    new_mean = (1.0 - MOMENTUM) * run_mean + MOMENTUM * batch_mean
    new_var = (1.0 - MOMENTUM) * run_var + MOMENTUM * batch_var * sea_count / (sea_count - 1.0)
    return (
        output,
        grad_features,
        gw_first.reshape(3, 3, depth, own),
        sums[0],
        gw_second.reshape(3, 3, depth, own),
        sums[1],
        gw_skip,
        sums[2],
        new_mean,
        new_var,
    )


def solution(mesh):
    field, kernel, vector = P("pix", None, "ch"), P(None, None, None, "ch"), P("ch")
    placed = (
        field, P("pix", None), P(), kernel, vector, kernel, vector, P(None, "ch"), vector,
        vector, vector, field,
    )
    return jax.shard_map(
        functools.partial(local, mesh),
        mesh=mesh,
        in_specs=placed,
        out_specs=(
            field, field, kernel, vector, kernel, vector, P(None, "ch"), vector, vector, vector,
        ),
        check_vma=False,
    )
```

```python
import functools

import jax
import jax.numpy as jnp
from jax import lax
from jax.experimental import pallas as pl
from jax.experimental.pallas import tpu as pltpu
from jax.sharding import PartitionSpec as P

EPSILON = 1e-05
MOMENTUM = 0.1
INV_ROOT_TWO_PI = 0.3989422804014327
SQRT_HALF = 0.7071067811865476
F32 = jnp.float32
BF16 = jnp.bfloat16
VMEM_LIMIT = 60 * 1024 * 1024
LARGE = 512 * 1024


def split(value):
    high = value.astype(BF16)
    return high, (value - high.astype(F32)).astype(BF16)


def dot_split(a_high, a_low, b_high, b_low):
    total = jnp.dot(a_high, b_high, preferred_element_type=F32)
    total = total + jnp.dot(a_high, b_low, preferred_element_type=F32)
    return total + jnp.dot(a_low, b_high, preferred_element_type=F32)


def gelu_and_slope(u):
    cdf = 0.5 * (1.0 + lax.erf(u * SQRT_HALF))
    return u * cdf, cdf + u * jnp.exp(-0.5 * u * u) * INV_ROOT_TWO_PI


AT_TOP, AT_BOTTOM, SIDE, HALF, FLIPPED, PIX = range(6)
NOT_SEA = 1e30
LANES = 128


def lane_parts(depth):
    return [slice(start, start + LANES) for start in range(0, depth, LANES)]


def put_row(buffers, block, read, left, right, breadth, depth):
    high, low = buffers
    column = lax.broadcasted_iota(jnp.int32, (breadth, 1), 0)
    rows = slice(block * breadth, (block + 1) * breadth)
    for lanes in lane_parts(depth):
        value = read(lanes)
        shifts = (
            jnp.where(column == 0, left(lanes), pltpu.roll(value, 1, 0)),
            value,
            jnp.where(column == breadth - 1, right(lanes), pltpu.roll(value, breadth - 1, 0)),
        )
        for tap, piece in enumerate(shifts):
            place = slice(tap * depth + lanes.start, tap * depth + lanes.stop)
            high[rows, place], low[rows, place] = split(piece)


def conv_tile(buffers, w_high, w_low, total, tile, breadth):
    high, low = buffers
    value = None
    for row_tap in range(3):
        rows = slice(row_tap * breadth, (row_tap + tile) * breadth)
        part = dot_split(high[rows, :], low[rows, :], w_high[row_tap], w_low[row_tap])
        value = part if value is None else value + part
    total[...] = value


def pipeline(fill, multiply, finish, tiles, store=lambda tile: None):
    assert tiles % 2 == 0
    fill(0, 0, True)

    @pl.loop(0, tiles // 2)
    def _(step):
        tile = 2 * step
        fill(tile + 1, 1, True)
        multiply(0)
        finish(jnp.maximum(tile - 1, 0), 1)
        fill(jnp.minimum(tile + 2, tiles - 1), 0, tile + 2 < tiles)
        multiply(1)
        finish(tile, 0)

        @pl.when(step > 0)
        def _():
            store(tile - 1)

        store(tile)

    finish(tiles - 1, 1)
    store(tiles - 1)


def patch(flags, x, left, right, pole, top, bottom):
    breadth = x.shape[1]

    def put(at, edge):
        @pl.when(flags[FLIPPED] == 1)
        def _():
            for column in range(breadth):
                x[at, column : column + 1] = pole[breadth - 1 - column : breadth - column]

        @pl.when(flags[FLIPPED] == 0)
        def _():
            x[at] = pole[...]

        left[at : at + 1] = 0.5 * (x[at, 0:1] + left[edge : edge + 1])
        right[at : at + 1] = 0.5 * (x[at, breadth - 1 : breadth] + right[edge : edge + 1])

    @pl.when(flags[AT_TOP] == 1)
    def _():
        put(top, top + 1)

    @pl.when(flags[AT_BOTTOM] == 1)
    def _():
        put(bottom, bottom - 1)


def put_messages(flags, x, to_prev, to_next, first_row, last_row):
    rows, breadth = x.shape[0], x.shape[1]

    @pl.loop(0, rows)
    def _(row):
        to_prev[pl.ds(row, 1)] = x[row, 0:1]
        to_next[pl.ds(row, 1)] = x[row, breadth - 1 : breadth]

    to_prev[rows : rows + breadth] = x[jnp.where(flags[AT_BOTTOM] == 1, last_row, first_row)]


def first_kernel(
    traffic, flags, marked, got, halo_mine, halo_got, w_high, w_low, biases,
    scaled, x_left, x_right, hidden, slope, to_prev, to_next,
    pole, high0, low0, high1, low1, total0, total1, *, tile
):
    blocks, breadth, depth = scaled.shape
    own = depth // 2
    extra = blocks - got.shape[0]
    tail = halo_mine.shape[0] - 8
    start = flags[HALF] * (marked.shape[0] - got.shape[0])

    def normal(value, lanes):
        source = halo_mine if lanes.start == 0 else halo_got
        mean, inverse = source[tail : tail + 1], source[tail + 1 : tail + 2]
        return jnp.where(value > 0.1 * NOT_SEA, 0.0, (value - mean) * inverse)

    traffic.wait(0, 1)
    lower, upper = slice(0, own), slice(own, depth)
    main = jnp.where(flags[HALF] == 0, extra, 0)
    outer = jnp.where(flags[HALF] == 0, 0, blocks - extra)

    @pl.loop(0, got.shape[0])
    def _(row):
        scaled[main + row, :, lower] = normal(marked[start + row], lower)
        scaled[main + row, :, upper] = normal(got[row], upper)

    for row in range(extra):
        rows = slice(row * breadth, (row + 1) * breadth)
        scaled[outer + row, :, lower] = normal(halo_mine[rows], lower)
        scaled[outer + row, :, upper] = normal(halo_got[rows], upper)

    begin = extra * breadth
    for target, count in ((x_left, blocks), (x_right, blocks), (pole, breadth)):
        rows = slice(begin, begin + count)
        target[:, lower] = normal(halo_mine[rows], lower)
        target[:, upper] = normal(halo_got[rows], upper)
        begin = begin + count

    patch(flags, scaled, x_left, x_right, pole, 3, blocks - 4)
    traffic.store(0, 0, blocks)
    traffic.wait(4, 5)
    buffers, totals = ((high0, low0), (high1, low1)), (total0, total1)

    def fill(step, slot, fresh):
        for block in range(tile + 2):
            row = step * tile + block
            put_row(
                buffers[slot], block, lambda lanes: scaled[row, :, lanes],
                lambda lanes: x_left[pl.ds(row, 1)][:, lanes], lambda lanes: x_right[pl.ds(row, 1)][:, lanes],
                breadth, depth,
            )

    def finish(step, slot):
        for block in range(tile):
            for lanes in lane_parts(depth):
                pre = totals[slot][block * breadth : (block + 1) * breadth, lanes] + biases[0:1, lanes]
                value, grad = gelu_and_slope(pre)
                hidden[step * tile + block, :, lanes] = value
                slope[step * tile + block, :, lanes] = grad

    def store(step):
        traffic.store(3, step * tile, tile)
        traffic.store(4, step * tile, tile)

    pipeline(
        fill, lambda slot: conv_tile(buffers[slot], w_high, w_low, totals[slot], tile, breadth),
        finish, (blocks - 2) // tile, store,
    )
    put_messages(flags, hidden, to_prev, to_next, 3, blocks - 6)


def second_kernel(
    traffic, flags, x, left_in, ahead, w_high, w_low, biases, source, s_high, s_low,
    out_own, out_send, slope,
    left, right, high0, low0, high1, low1, total0, total1, skip0, skip1, sum0, sum1, *, tile
):
    blocks, breadth, depth = x.shape
    own = depth // 2
    left[...] = left_in[...]
    right[...] = ahead[:blocks]
    traffic.wait(0)
    patch(flags, x, left, right, ahead[blocks:], 2, blocks - 3)
    traffic.wait(3, 4, 6)
    buffers, totals, skips = ((high0, low0), (high1, low1)), (total0, total1), (skip0, skip1)
    sums = (sum0, sum1)

    def fill(step, slot, fresh):
        for block in range(tile + 2):
            row = step * tile + block
            put_row(
                buffers[slot], block, lambda lanes: x[row, :, lanes],
                lambda lanes: left[pl.ds(row, 1)][:, lanes], lambda lanes: right[pl.ds(row, 1)][:, lanes],
                breadth, depth,
            )
        for block in range(tile):
            rows = slice(block * breadth, (block + 1) * breadth)
            for lanes in lane_parts(depth):
                value = source[step * tile + block + 2, :, lanes]
                place = slice(depth + lanes.start, depth + lanes.stop)
                skips[slot][rows, lanes], skips[slot][rows, place] = split(value)

    def multiply(slot):
        conv_tile(buffers[slot], w_high, w_low, totals[slot], tile, breadth)
        skip = skips[slot]
        sums[slot][...] = dot_split(skip[:, :depth], skip[:, depth:], s_high[...], s_low[...])

    def finish(step, slot):
        for block in range(tile):
            row = step * tile + block
            rows = slice(block * breadth, (block + 1) * breadth)
            for lanes in lane_parts(depth):
                pre = totals[slot][rows, lanes] + biases[1:2, lanes]
                value, grad = gelu_and_slope(pre)
                slope[row, :, lanes] = grad
                value = value + sums[slot][rows, lanes] + biases[2:3, lanes]
                if lanes.stop <= own:
                    out_own[row, :, lanes] = value
                else:
                    out_send[row, :, lanes.start - own : lanes.stop - own] = value

    def store(step):
        for result in range(3):
            traffic.store(result, step * tile, tile)

    pipeline(fill, multiply, finish, (blocks - 2) // tile, store)


def edge_products(edges, w_high, w_low, slot, count):
    depth = edges.shape[0] * LANES
    total = None
    for tap in range(3):
        rows = slice(slot * depth, (slot + 1) * depth)
        pieces = [edges[part, tap : tap + count] for part in range(edges.shape[0])]
        edge_high, edge_low = split(jnp.concatenate(pieces, axis=1))
        part = dot_split(edge_high, edge_low, w_high[tap, rows], w_low[tap, rows])
        total = part if total is None else total + part
    return total


def put_rims(flags, to_next, to_prev, first_rim, last_rim, top, bottom):
    count, breadth = to_prev.shape[0], top.shape[0]
    to_prev[...] = first_rim[:count]
    to_next[:count] = last_rim[:count]
    to_next[count:] = jnp.zeros((breadth, to_next.shape[1]), F32)
    column = lax.broadcasted_iota(jnp.int32, (breadth, 1), 0)

    def put(row, at, inner):
        corner_first, corner_last = 0.5 * first_rim[at : at + 1], 0.5 * last_rim[at : at + 1]
        to_prev[inner : inner + 1] += corner_first
        to_next[inner : inner + 1] += corner_last
        row = row[...] + jnp.where(column == 0, corner_first, 0.0)
        row = row + jnp.where(column == breadth - 1, corner_last, 0.0)

        @pl.when(flags[FLIPPED] == 0)
        def _():
            to_next[count:] = row

        @pl.when(flags[FLIPPED] == 1)
        def _():
            for k in range(breadth):
                to_next[count + k : count + k + 1] = row[breadth - 1 - k : breadth - k]

    @pl.when(flags[AT_TOP] == 1)
    def _():
        put(top, 0, 1)

    @pl.when(flags[AT_BOTTOM] == 1)
    def _():
        put(bottom, count - 1, count - 2)


def back_second_kernel(
    traffic, flags, cot_mine, cot_got, slope, w_high, w_low,
    out, grad, to_next, to_prev,
    high0, low0, high1, low1, total0, total1, edge_first, edge_last, *, tile
):
    blocks, breadth, depth = slope.shape
    own = depth // 2
    traffic.wait(0, 1, 2)
    edge_first[...] = jnp.zeros_like(edge_first)
    edge_last[...] = jnp.zeros_like(edge_last)
    buffers, totals = ((high0, low0), (high1, low1)), (total0, total1)

    def fill(step, slot, fresh):
        for block in range(tile + 2):
            row = jnp.minimum(step * tile + block, blocks - 1)
            outside = (flags[AT_TOP] == 1) & (row < 2) | (flags[AT_BOTTOM] == 1) & (row >= blocks - 2)
            inside = jnp.where(outside, 0.0, 1.0)

            def read(lanes):
                cot = cot_mine[row] if lanes.stop <= own else cot_got[row]
                value = cot * slope[row, :, lanes] * inside
                grad[row, :, lanes] = value
                edge_first[lanes.start // LANES, pl.ds(row, 1)] = value[0:1]
                edge_last[lanes.start // LANES, pl.ds(row, 1)] = value[breadth - 1 : breadth]
                return value

            put_row(buffers[slot], block, read, lambda lanes: 0.0, lambda lanes: 0.0, breadth, depth)

    def finish(step, slot):
        for block in range(tile):
            out[step * tile + block] = totals[slot][block * breadth : (block + 1) * breadth]

    traffic.wait(3, 4)
    pipeline(
        fill, lambda slot: conv_tile(buffers[slot], w_high, w_low, totals[slot], tile, breadth),
        finish, blocks // tile, lambda step: traffic.store(0, step * tile, tile),
    )
    traffic.store(1, 0, blocks)
    rows = blocks + 4
    first_rim = edge_products(edge_first, w_high, w_low, 2, rows)
    last_rim = edge_products(edge_last, w_high, w_low, 0, rows)
    put_rims(flags, to_next, to_prev, first_rim, last_rim, out[0], out[blocks - 3])


def back_first_kernel(
    traffic, flags, grad, cot_mine, cot_got, w_high, w_low, s_high, s_low, *rest, tile, part
):
    if part:
        before_first, before_last, before_top, out_own, out_send, to_next, to_prev = rest[:7]
    else:
        out_own, out_send, rim_first, rim_last, top = rest[:5]
    high0, low0, high1, low1, total0, total1, skip0, skip1, edge_first, edge_last, result = rest[-11:]
    count, breadth, depth = grad.shape
    own = depth // 2
    begin = part * ((count - 2) // 2)
    blocks = result.shape[0]
    edge_first[...] = jnp.zeros_like(edge_first)
    edge_last[...] = jnp.zeros_like(edge_last)
    buffers, totals, skips = ((high0, low0), (high1, low1)), (total0, total1), (skip0, skip1)
    traffic.wait(0, 1, 2)

    def fill(step, slot, fresh):
        for block in range(tile + 2):
            at = step * tile + block
            row = begin + at - 1
            inside = jnp.where((row >= 0) & (row < count), 1.0, 0.0)
            row = jnp.clip(row, 0, count - 1)

            def read(lanes):
                value = grad[row, :, lanes] * inside
                edge_first[lanes.start // LANES, pl.ds(at, 1)] = value[0:1]
                edge_last[lanes.start // LANES, pl.ds(at, 1)] = value[breadth - 1 : breadth]
                return value

            put_row(buffers[slot], block, read, lambda lanes: 0.0, lambda lanes: 0.0, breadth, depth)
        for block in range(tile):
            row = begin + step * tile + block
            inside = jnp.where((row >= 1) & (row < count - 1), 1.0, 0.0)
            rows = slice(block * breadth, (block + 1) * breadth)
            for lanes in lane_parts(depth):
                cot = cot_mine[row + 1] if lanes.stop <= own else cot_got[row + 1]
                place = slice(depth + lanes.start, depth + lanes.stop)
                skips[slot][rows, lanes], skips[slot][rows, place] = split(cot * inside)

    def multiply(slot):
        conv_tile(buffers[slot], w_high, w_low, totals[slot], tile, breadth)
        skip = skips[slot]
        totals[slot][...] += dot_split(skip[:, :depth], skip[:, depth:], s_high[...], s_low[...])

    def finish(step, slot):
        for block in range(tile):
            result[step * tile + block] = totals[slot][block * breadth : (block + 1) * breadth]

    traffic.wait(3, 4)
    pipeline(fill, multiply, finish, blocks // tile)

    @pl.loop(0, out_own.shape[0])
    def _(row):
        out_own[row] = result[row + 1, :, :own]
        out_send[row] = result[row + 1, :, own:]

    traffic.store(0 if part == 0 else 0, 0, out_own.shape[0])
    traffic.store(1, 0, out_own.shape[0])
    rows = blocks + 6
    first_rim = edge_products(edge_first, w_high, w_low, 2, rows)
    last_rim = edge_products(edge_last, w_high, w_low, 0, rows)
    if part == 0:
        rim_first[...], rim_last[...] = first_rim, last_rim
        top[...] = result[0]
    else:
        joined = [
            jnp.concatenate([before[: begin + 1], now[1 : begin + 2]], axis=0)
            for before, now in ((before_first, first_rim), (before_last, last_rim))
        ]
        put_rims(flags, to_next, to_prev, *joined, before_top[...], result[blocks - 1])


def weight_kernel(traffic, flags, x, *rest, tile, first):
    if first:
        left, right, upper, behind, after, slope, cot_mine, cot_got = rest[:8]
        parts, _, total, total_skip, grad_out = rest[8:13]
        rest, begin = rest[13:], 3
    else:
        left_in, ahead, grad = rest[:3]
        parts, _, total = rest[3:6]
        left, right = rest[-2:]
        rest, begin = rest[6:-2], 2
    high0, low0, high1, low1, t0, t1, acc = rest[:7]
    buffers, turned = ((high0, low0), (high1, low1)), (t0, t1)
    breadth, depth = x.shape[1:]
    own = depth // 2
    taps = acc.shape[0]
    rows = x.shape[0] - 2 * begin - 2
    pixels = tile * breadth
    traffic.wait(0)
    if first:
        count = rows + 2
        column = lax.broadcasted_iota(jnp.int32, (breadth, 1), 0)
        traffic.wait(3, 6, 7, 8)
        total_skip[...] = jnp.zeros_like(total_skip)

        def read(row, lanes):
            at = row + 1
            edge = (flags[AT_TOP] == 1) & (row == 0) | (flags[AT_BOTTOM] == 1) & (row == rows - 1)
            value = upper[at, :, lanes] + jnp.where(column == 0, behind[pl.ds(at, 1)][:, lanes], 0.0)
            value = value + jnp.where(column == breadth - 1, after[pl.ds(at, 1)][:, lanes], 0.0)
            value = value + behind[count : count + breadth, lanes] * jnp.where(edge, 1.0, 0.0)
            value = value * slope[at + 2, :, lanes]
            grad_out[at, :, lanes] = value
            return value

        for row, pole in ((-1, AT_TOP), (rows, AT_BOTTOM)):
            for lanes in lane_parts(depth):
                value = read(row, lanes)
                grad_out[row + 1, :, lanes] = value * jnp.where(flags[pole] == 1, 0.0, 1.0)
    else:
        left[...] = left_in[...]
        right[...] = ahead[: x.shape[0]]
        patch(flags, x, left, right, ahead[x.shape[0] :], 2, x.shape[0] - 3)
        traffic.wait(3)

        def read(row, lanes):
            return grad[row + 2, :, lanes]

    acc[...] = jnp.zeros_like(acc)
    total[...] = jnp.zeros_like(total)

    def turn(slot, place, lanes, value):
        value_high, value_low = split(value.T)
        turned[slot][place, lanes] = value_high
        turned[slot][place + 1, lanes] = value_low

    def fill(step, slot, fresh):
        once = jnp.where(fresh, 1.0, 0.0)
        for block in range(tile + 2):
            row = step * tile + block + begin
            put_row(
                buffers[slot], block, lambda lanes: x[row, :, lanes],
                lambda lanes: left[pl.ds(row, 1)][:, lanes], lambda lanes: right[pl.ds(row, 1)][:, lanes],
                breadth, depth,
            )
        for lanes in lane_parts(depth):
            value = jnp.concatenate([read(step * tile + block, lanes) for block in range(tile)], axis=0)
            total[:, lanes] += jnp.sum(value, axis=0, keepdims=True) * once
            turn(slot, 0, lanes, value)
            if first:
                source = cot_mine if lanes.stop <= own else cot_got
                value = source[pl.ds(step * tile + 2, tile)].reshape(pixels, LANES)
                total_skip[:, lanes] += jnp.sum(value, axis=0, keepdims=True) * once
                turn(slot, 2, lanes, value)

    def multiply(slot):
        high, low = buffers[slot]
        for tap in range(taps):
            row_tap, column_tap, place = (tap // 3, tap % 3, 0) if tap < 9 else (1, 1, 2)
            window = slice(row_tap * breadth, row_tap * breadth + pixels)
            lanes = slice(column_tap * depth, (column_tap + 1) * depth)
            acc[tap] += dot_split(
                turned[slot][place], turned[slot][place + 1], high[window, lanes], low[window, lanes]
            )

    pipeline(fill, multiply, lambda step, slot: None, rows // tile)
    half = depth // 2
    mine = (flags[SIDE] ^ flags[PIX]) & 1
    for tap in range(taps):
        value = acc[tap].T
        parts[mine, tap] = value[:half]
        parts[1 - mine, tap] = value[half:]


def weights_kernel(traffic, flags, mine, *rest, steps, skip):
    shares, rest = rest[: steps + 1], rest[steps + 1 :]
    if skip:
        mine_skip, f_high, f_low, b_high, b_low, s_high, s_low, sb_high, sb_low, other = rest
    else:
        f_high, f_low, b_high, b_low, other = rest
    own = mine.shape[1]
    depth = 2 * own
    taps = mine.shape[0]
    count = 1 << steps
    traffic.wait(*traffic.ins)
    share, share_skip = taps // count, depth // count
    unit = shares[0].shape[0]
    begin = share if skip else 0
    for piece in range(count):
        away = sum(1 << (steps - 1 - step) for step in range(steps) if piece >> step & 1)
        index = (flags[PIX] & (count - 1)) ^ away
        level = piece.bit_length()
        source = shares[level]
        at = (piece - (1 << (level - 1)) if level else 0) * unit + begin
        other[pl.ds(pl.multiple_of(index * share, 8), share)] = source[at : at + share]
        if skip:
            start = pl.multiple_of(taps + index * share_skip, 8)
            other[pl.ds(start, share_skip)] = source[at + share : at + share + share_skip]
    def both(first, second):
        return jnp.concatenate([first, second], axis=1)

    @pl.loop(0, 9)
    def _(tap):
        row_tap, column_tap = tap // 3, tap % 3
        back_row, back_column = 2 - row_tap, 2 - column_tap
        for part in range(2):
            at = pl.multiple_of(tap * depth + jnp.where(flags[SIDE] == part, 0, own), own)
            value = both(mine[pl.ds(at, own)], other[pl.ds(at, own)])
            value_high, value_low = split(value)
            place = pl.ds(pl.multiple_of(column_tap * depth + part * own, own), own)
            f_high[row_tap, place] = value_high
            f_low[row_tap, place] = value_low
            turned_high, turned_low = split(value.T)
            place = pl.ds(pl.multiple_of(back_column * depth, depth), depth)
            lanes = slice(part * own, (part + 1) * own)
            b_high[back_row, place, lanes] = turned_high
            b_low[back_row, place, lanes] = turned_low

    if skip:
        for part in range(2):
            at = pl.multiple_of(jnp.where(flags[SIDE] == part, 0, own), own)
            value = both(mine_skip[pl.ds(at, own)], other[pl.ds(pl.multiple_of(taps + at, own), own)])
            lanes = slice(part * own, (part + 1) * own)
            s_high[lanes], s_low[lanes] = split(value)
            sb_high[:, lanes], sb_low[:, lanes] = split(value.T)


def pre_kernel(traffic, flags, features, mask, marked, theirs, stats, inner, to_prev, to_next):
    rows, breadth, own = features.shape
    length = theirs.shape[0]
    traffic.wait(0)
    start = (1 - flags[HALF]) * (rows - length)
    turned = mask[...].astype(F32)
    turned = jnp.concatenate([turned, jnp.zeros((breadth, 128 - rows), F32)], axis=1)
    none = jnp.zeros((8, own), F32)

    def fold(v):
        return jnp.sum(v.reshape(breadth // 8, 8, own), axis=0)

    def first(step, carry):
        count, total = carry
        base = step * 8
        sea_of = pltpu.roll(turned, 128 - base, 1)
        for k in range(8):
            row = base + k
            sea = jnp.broadcast_to(sea_of[:, k : k + 1], (breadth, own))
            value = features[row]
            land = jnp.where(sea > 0.5, value, NOT_SEA)
            marked[row] = land
            to_prev[pl.ds(row, 1)] = land[0:1]
            to_next[pl.ds(row, 1)] = land[breadth - 1 : breadth]
            count, total = count + fold(sea), total + fold(value * sea)
        return count, total

    count, total = lax.fori_loop(0, rows // 8, first, (none, none))
    count = jnp.sum(count, axis=0, keepdims=True)
    mean = jnp.sum(total, axis=0, keepdims=True) / jnp.maximum(count, 1.0)

    def second(step, squares):
        for k in range(8):
            value = marked[step * 8 + k]
            value = jnp.where(value > 0.1 * NOT_SEA, 0.0, value - mean)
            squares = squares + fold(value * value)
        return squares

    squares = lax.fori_loop(0, rows // 8, second, none)

    @pl.loop(0, length // 4)
    def _(step):
        theirs[pl.ds(step * 4, 4)] = marked[pl.ds(start + step * 4, 4)]

    stats[...] = jnp.zeros_like(stats)
    stats[0:1] = count
    stats[1:2] = mean
    stats[2:3] = jnp.sum(squares, axis=0, keepdims=True)
    strip = flags[SIDE] ^ flags[HALF]
    to_prev[rows:] = marked[strip * (rows - 1)]
    inner[...] = marked[pl.ds((1 - strip) * (rows - inner.shape[0]), inner.shape[0])]


def rims_kernel(traffic, flags, behind, ahead, core, stats, mine, theirs, wide):
    rows, own = behind.shape
    breadth = ahead.shape[0] - rows
    extra = (core.shape[0]) // (breadth + 2)
    length = rows // 2 + 2 * extra
    inner = extra * breadth
    at = inner
    for target in (mine, theirs):
        target[:inner] = core[:inner]
    for source, start in ((behind, inner + extra), (ahead, inner)):
        wide[:extra] = core[start : start + extra]
        wide[extra : extra + rows] = source[:rows]
        wide[extra + rows :] = core[start : start + extra]
        for target, half in ((mine, flags[HALF]), (theirs, 1 - flags[HALF])):
            target[at : at + length] = wide[pl.ds(pl.multiple_of(half * (rows // 2), 8), length)]
        at = at + length
    count, mean, squares = stats[0:1], stats[1:2], stats[2:3]
    inverse = lax.rsqrt(squares / count + EPSILON)
    for target in (mine, theirs):
        target[at : at + breadth] = ahead[rows:]
        target[at + breadth :] = jnp.zeros((8, own), F32)
        target[at + breadth : at + breadth + 1] = mean
        target[at + breadth + 1 : at + breadth + 2] = inverse


def final_kernel(flags, marked, lower_upper, lower_lower, rims, stats, sums, *rest, other, parts):
    out, source, result, in_sems, out_sems = rest[-5:]
    rows, breadth, own = marked.shape
    size = rows // 2
    step = size // parts
    last = size + 2 + breadth
    count, mean = stats[0:1], stats[1:2]
    inverse = lax.rsqrt(stats[2:3] / count + EPSILON)
    first_mean, second_mean = sums[3:4] / count, sums[4:5] / count
    column = lax.broadcasted_iota(jnp.int32, (breadth, 1), 0)
    strip = flags[SIDE] ^ flags[HALF]
    edge = strip * (size - 1)
    half = 1 - flags[HALF] if other else flags[HALF]
    at_pole = flags[SIDE] == (1 if other else 0)

    def fetch(part):
        rows = pl.ds(half * size + part * step, step)
        return pltpu.make_async_copy(marked.at[rows], source.at[pl.ds(part * step, step)], in_sems.at[part])

    def store(part):
        rows = pl.ds(half * size + part * step, step)
        return pltpu.make_async_copy(result.at[pl.ds(part * step, step)], out.at[rows], out_sems.at[part])

    for part in range(parts):
        fetch(part).start()
    for part in range(parts):
        fetch(part).wait()

        lower = lower_upper if part < parts // 2 else lower_lower

        @pl.loop(part * step, (part + 1) * step)
        def _(row):
            value = lower[row % (size // 2)] + jnp.where(column == 0, rims[pl.ds(row + 1, 1)], 0.0)
            value = value + jnp.where(column == breadth - 1, rims[pl.ds(row + last + 1, 1)], 0.0)
            at_edge = jnp.where((row == edge) & at_pole, 1.0, 0.0)
            value = value + rims[size + 2 : last] * at_edge
            normed = (source[row] - mean) * inverse
            value = inverse * (value - first_mean - normed * second_mean)
            result[row] = jnp.where(source[row] > 0.1 * NOT_SEA, 0.0, value)

        store(part).start()
    for part in range(parts):
        store(part).wait()


def final_call(other, flags, marked, lower, rims, stats, sums, before=None):
    anywhere, whole = pl.BlockSpec(memory_space=pl.ANY), pl.BlockSpec(memory_space=pltpu.VMEM)
    parts = 4
    operands = [flags, marked, *lower, rims, stats, sums] + ([before] if other else [])
    half = pltpu.VMEM((marked.shape[0] // 2,) + marked.shape[1:], F32)
    return pl.pallas_call(
        functools.partial(final_kernel, other=other, parts=parts),
        out_shape=jax.ShapeDtypeStruct(marked.shape, F32),
        in_specs=[pl.BlockSpec(memory_space=pltpu.SMEM), anywhere] + [whole] * 5 + [anywhere] * other,
        out_specs=anywhere,
        scratch_shapes=[half, half, pltpu.SemaphoreType.DMA((parts,)), pltpu.SemaphoreType.DMA((parts,))],
        input_output_aliases={7: 0} if other else {},
        compiler_params=pltpu.CompilerParams(vmem_limit_bytes=VMEM_LIMIT),
        cost_estimate=pl.CostEstimate(flops=0, bytes_accessed=0, transcendentals=0),
        name="final_got" if other else "final_own",
    )(*operands)


def join_kernel(flags, mine, theirs, out, sems):
    size = out.shape[0] // 2
    skip = (mine.shape[0] - size) // 2
    copies = []
    for place, source in enumerate((mine, theirs)):
        half = flags[HALF] if place == 0 else 1 - flags[HALF]
        target = out.at[pl.ds(half * size, size)]
        copies.append(pltpu.make_async_copy(source.at[pl.ds(skip, size)], target, sems.at[place]))
    for copy in copies:
        copy.start()
    for copy in copies:
        copy.wait()


def call_copy(kernel, shape, flags, *operands):
    anywhere = pl.BlockSpec(memory_space=pl.ANY)
    return pl.pallas_call(
        kernel,
        out_shape=[jax.ShapeDtypeStruct(shape, F32)],
        in_specs=[pl.BlockSpec(memory_space=pltpu.SMEM)]
        + [pl.BlockSpec(memory_space=pltpu.VMEM)] * len(operands),
        out_specs=[anywhere],
        scratch_shapes=[pltpu.SemaphoreType.DMA((len(operands),))],
        compiler_params=pltpu.CompilerParams(vmem_limit_bytes=VMEM_LIMIT),
        cost_estimate=pl.CostEstimate(flops=0, bytes_accessed=0, transcendentals=0),
        name="join",
    )(flags, *operands)


class Traffic:
    def __init__(self, ins, outs):
        self.ins, self.outs, self.parts = ins, outs, {}
        for copy in ins.values():
            copy.start()

    def wait(self, *places):
        for place in places:
            self.ins.pop(place).wait()

    def store(self, place, start, count):
        source, target, sem = self.outs[place]
        rows = pl.ds(start, count)
        pltpu.make_async_copy(source.at[rows], target.at[rows], sem).start()
        self.parts[place] = True

    def finish(self):
        for place in self.outs:
            if place not in self.parts:
                pltpu.make_async_copy(*self.outs[place]).start()
        for place in self.outs:
            pltpu.make_async_copy(*self.outs[place]).wait()


def call(kernel, shapes, scratch, flags, *operands, name=None, paired=False):
    shapes = [s if isinstance(s, jax.ShapeDtypeStruct) else jax.ShapeDtypeStruct(s, F32) for s in shapes]

    def large(a):
        return a.size * a.dtype.itemsize >= LARGE

    inside, outside = [large(a) for a in operands], [large(a) for a in shapes]
    buffers = [pltpu.VMEM(a.shape, a.dtype) for a in list(operands) + shapes[2 * paired :] if large(a)]
    if paired:
        buffers.append(pltpu.VMEM((2,) + shapes[0].shape, F32))
    sems = [pltpu.SemaphoreType.DMA((max(1, sum(group)),)) for group in (inside, outside)]
    anywhere, whole = pl.BlockSpec(memory_space=pl.ANY), pl.BlockSpec(memory_space=pltpu.VMEM)

    def body(flags, *refs):
        refs = list(refs)
        given = len(operands) + len(shapes)
        rest, (in_sems, out_sems) = refs[given : len(refs) - 2], refs[-2:]
        held, extra = rest[: len(buffers)], rest[len(buffers) :]
        ins, outs, seen = {}, {}, []
        for place, is_large in enumerate(inside):
            if is_large:
                buffer = held.pop(0)
                ins[place] = pltpu.make_async_copy(refs[place], buffer, in_sems.at[len(ins)])
                seen.append(buffer)
            else:
                seen.append(refs[place])
        for place, is_large in enumerate(outside):
            ref = refs[len(operands) + place]
            if paired and place < 2:
                outs[place] = (held[-1].at[place], ref, out_sems.at[len(outs)])
                seen.append(held[-1])
            elif is_large:
                buffer = held.pop(0)
                outs[place] = (buffer, ref, out_sems.at[len(outs)])
                seen.append(buffer)
            else:
                seen.append(ref)
        traffic = Traffic(ins, outs)
        kernel(traffic, flags, *seen, *extra)
        assert not traffic.ins
        traffic.finish()

    return pl.pallas_call(
        body,
        out_shape=shapes,
        in_specs=[pl.BlockSpec(memory_space=pltpu.SMEM)] + [anywhere if k else whole for k in inside],
        out_specs=[anywhere if k else whole for k in outside],
        scratch_shapes=buffers + list(scratch) + sems,
        compiler_params=pltpu.CompilerParams(vmem_limit_bytes=VMEM_LIMIT),
        cost_estimate=pl.CostEstimate(flops=0, bytes_accessed=0, transcendentals=0),
        name=name,
    )(flags, *operands)


class Place:
    def __init__(self, mesh, rows, breadth):
        self.count = mesh.shape["pix"]
        self.strips = 3 * breadth // rows
        assert mesh.shape["ch"] == 2 and self.strips == 2
        self.pix = lax.axis_index("pix")
        self.side = lax.axis_index("ch")
        self.ribbon = self.pix // self.strips % 4
        self.strip = self.pix % self.strips
        self.half = self.side ^ self.strip
        self.at_top = (self.side == 0) & (self.strip == 0)
        self.at_bottom = (self.side == 0) & (self.strip == 1)

    def ribbon_pairs(self, offset):
        pairs = []
        for index in range(self.count):
            sample, strip = index // (4 * self.strips), index % self.strips
            ribbon = (index // self.strips + offset) % 4
            pairs.append((index, (sample * 4 + ribbon) * self.strips + strip))
        return pairs

    def to_next(self, value):
        return lax.ppermute(value, "pix", self.ribbon_pairs(1))

    def to_prev(self, value):
        return lax.ppermute(value, "pix", self.ribbon_pairs(-1))

    def across(self, value):
        return lax.ppermute(value, "ch", [(0, 1), (1, 0)])

    def flip(self, value, bit):
        return lax.ppermute(value, "pix", [(i, i ^ bit) for i in range(self.count)])

    def bits(self):
        return [1 << step for step in range(self.count.bit_length() - 1)]

    def ordered(self, mine, theirs, bit):
        upper = (self.pix & bit) != 0
        return jnp.where(upper, theirs, mine), jnp.where(upper, mine, theirs)

    def near(self):
        return self.bits()[:3]

    def gathered(self, value):
        pieces = [value]
        for bit in reversed(self.near()):
            sent = pieces[0] if len(pieces) == 1 else jnp.concatenate(pieces, axis=0)
            pieces.append(self.flip(sent, bit))
        return pieces

    def members(self, bits):
        out = []
        for other in range(1, 1 << len(bits)):
            mask = sum(bit for step, bit in enumerate(bits) if other >> step & 1)
            out.append((other, [(i, i ^ mask) for i in range(self.count)]))
        return out

    def number(self, bits):
        total = 0
        for step, bit in enumerate(bits):
            total = total + (((self.pix & bit) != 0).astype(jnp.int32) << step)
        return total

    def shared(self, values, bits):
        me, length = self.number(bits), values[0].shape[0] >> len(bits)

        def share(number):
            pieces = [lax.dynamic_slice_in_dim(value, number * length, length, 0) for value in values]
            return functools.reduce(jnp.add, pieces)

        total = share(me)
        parts = []
        for other, pairs in self.members(bits):
            piece = share(me ^ other)
            parts.append(lax.ppermute(piece, "pix", pairs))
        for part in parts:
            total = total + part
        return total

    def spread(self, value, bits):
        parts = [value] + [lax.ppermute(value, "pix", pairs) for _, pairs in self.members(bits)]
        for step, bit in enumerate(bits):
            upper = (self.pix & bit) != 0
            parts = [
                jnp.where(upper, parts[k ^ (1 << step)], parts[k]) for k in range(len(parts))
            ]
        return jnp.concatenate(parts, axis=0)

    def groups(self):
        bits = self.bits()
        rest = [bits[k : k + 2] for k in range(2, len(bits), 2)]
        return [bits[:1], bits[1:2]] + rest

    def summed(self, value):
        for bit in self.bits():
            first, second = self.ordered(value, self.flip(value, bit), bit)
            value = first + second
        return value

    def part(self, value, half, start, length):
        return lax.dynamic_slice_in_dim(value, half * start, length, 0)

    def join_rows(self, mine, theirs):
        return jnp.where(
            self.half == 0,
            jnp.concatenate([mine, theirs], axis=0),
            jnp.concatenate([theirs, mine], axis=0),
        )

    def inner_rows(self, value, extra):
        edge = jnp.where(self.strip == 0, value[-extra:], value[:extra])
        return self.flip(edge, 1)


def merged_stats(place, state):
    for bit in place.bits():
        first, second = place.ordered(state, place.flip(state, bit), bit)
        total = first[0] + second[0]
        safe = jnp.maximum(total, 1.0)
        step = second[1] - first[1]
        state = jnp.stack(
            [
                total,
                (first[0] * first[1] + second[0] * second[1]) / safe,
                first[2] + second[2] + step * step * (first[0] * second[0] / safe),
            ]
            + [total] * 5
        )
    return state


def local(
    mesh, features, sea_mask, edge_flip, w_first, b_first, w_second, b_second, w_skip, b_skip,
    run_mean, run_var, cotangent,
):
    rows, breadth, own = features.shape
    place = Place(mesh, rows, breadth)
    size, depth = rows // 2, 2 * own
    taps = 9 * depth
    flip_row = jnp.sum(jnp.where((jnp.arange(4) == place.ribbon)[:, None], edge_flip, 0), axis=0)
    flipped = jnp.where(place.strip == 0, flip_row[0], flip_row[1]) == 1
    flags = jnp.stack(
        [
            jnp.where(flag, 1, 0).astype(jnp.int32)
            for flag in (place.at_top, place.at_bottom, place.side == 1, place.half == 1, flipped)
        ]
        + [place.pix.astype(jnp.int32)]
    )

    w_first, w_second = w_first.reshape(taps, own), w_second.reshape(taps, own)
    near = len(place.near())
    share, share_skip, number = taps >> near, depth >> near, place.number(place.near())
    biases = jnp.stack([b_first, b_second, b_skip])
    message = jnp.concatenate(
        [
            lax.dynamic_slice_in_dim(w_first, number * share, share, 0),
            lax.dynamic_slice_in_dim(w_second, number * share, share, 0),
            lax.dynamic_slice_in_dim(w_skip, number * share_skip, share_skip, 0),
            jnp.pad(biases, ((0, 5), (0, 0))),
        ]
    )
    features, message = lax.optimization_barrier((features, message))
    message = place.across(message)
    marked, theirs, stats, inner, to_prev, to_next = call(
        pre_kernel,
        [
            (rows, breadth, own), (size + 4, breadth, own), (8, own), (4, breadth, own),
            (rows + breadth, own), (rows, own),
        ],
        [], flags, features, sea_mask.T, name="pre",
    )
    theirs, message = lax.optimization_barrier((theirs, message))
    got = place.across(theirs)
    biases = jnp.concatenate([biases, message[2 * share + share_skip :][:3]], axis=1)
    def neighbours(stats, inner, to_prev, to_next, message):
        shares = place.gathered(message[: 2 * share + share_skip])
        stats = merged_stats(place, stats)
        ahead, behind = place.to_prev(to_prev), place.to_next(to_next)

        def inner_part(value):
            return jnp.where(place.strip == 0, value[rows - 4 : rows], value[:4])

        core = jnp.concatenate(
            [inner.reshape(-1, own), inner_part(ahead), inner_part(behind)], axis=0
        )
        core = place.flip(core, 1)
        halo_mine, halo_theirs = call(
            rims_kernel, [(rim_rows, own)] * 2, [pltpu.VMEM((rows + 8, own), F32)],
            flags, behind, ahead, core, stats, name="rims",
        )
        return stats, halo_mine, halo_theirs, shares

    def block(steps, *operands):
        shapes = jax.eval_shape(steps, *operands)

        def nothing(*operands):
            return jax.tree.map(lambda leaf: jnp.zeros(leaf.shape, leaf.dtype), shapes)

        return lax.cond(edge_flip[0, 0] < 2, steps, nothing, *operands)

    rim_rows = 4 * breadth + 2 * (size + 8) + breadth + 8
    stats, halo_mine, halo_theirs, shares = block(neighbours, stats, inner, to_prev, to_next, message)
    kinds = [jax.ShapeDtypeStruct((3, 3 * depth, depth), BF16)] * 4
    first_weights = call(
        functools.partial(weights_kernel, steps=near, skip=False),
        kinds, [pltpu.VMEM((taps, own), F32)], flags, w_first, *shares,
        name="weights_first",
    )
    sea_count, batch_mean = stats[0], stats[1]
    batch_var = stats[2] / sea_count
    halo_theirs, got = lax.optimization_barrier((halo_theirs, got))
    halo_got = place.across(halo_theirs)

    extra = place.inner_rows(cotangent, 2)
    wide = jnp.concatenate([extra, cotangent, extra], axis=0)
    cot_mine = place.part(wide, place.half, size, size + 4)
    cot_theirs = place.part(wide, 1 - place.half, size, size + 4)
    cot_theirs, halo_got = lax.optimization_barrier((cot_theirs, halo_got))
    cot_got = place.across(cot_theirs)

    small = [jax.ShapeDtypeStruct((depth, depth), BF16)] * 4
    second_weights = call(
        functools.partial(weights_kernel, steps=near, skip=True),
        kinds + small, [pltpu.VMEM((taps + depth, own), F32)], flags,
        w_second, *shares, w_skip,
        name="weights_second",
    )

    def buffers(tile):
        return [pltpu.VMEM(((tile + 2) * breadth, 3 * depth), BF16) for _ in range(4)]

    def pair(count, width, kind=F32):
        return [pltpu.VMEM((count, width), kind) for _ in range(2)]

    def edges(count):
        return [pltpu.VMEM((depth // LANES, count, LANES), F32) for _ in range(2)]

    def conv_scratch(tile):
        return buffers(tile) + pair(tile * breadth, depth)

    def first_conv(got, halo_got):
        return call(
            functools.partial(first_kernel, tile=9),
            [
                (size + 8, breadth, depth), (size + 8, depth), (size + 8, depth),
                (size + 6, breadth, depth), (size + 6, breadth, depth),
                (size + 6 + breadth, depth), (size + 6, depth),
            ],
            [pltpu.VMEM((breadth, depth), F32)] + conv_scratch(9),
            flags, marked, got, halo_mine, halo_got, *first_weights[:2], biases,
            name="first",
        )

    scaled, x_left, x_right, hidden, slope_first, to_prev, to_next = block(first_conv, got, halo_got)
    h_ahead, h_left = place.to_prev(to_prev), place.to_next(to_next)
    h_left, cot_got = lax.optimization_barrier((h_left, cot_got))
    out_own, out_send, slope_second = call(
        functools.partial(second_kernel, tile=13),
        [(size + 4, breadth, own), (size + 4, breadth, own), (size + 4, breadth, depth)],
        pair(size + 6, depth) + conv_scratch(13) + pair(13 * breadth, 2 * depth, BF16)
        + pair(13 * breadth, depth),
        flags, hidden, h_left, h_ahead, *second_weights[:2], biases, scaled, *second_weights[4:6],
        name="second",
    )
    out_got = place.across(out_send)

    rim_shapes = [(size + 2 + breadth, depth), (size + 2, depth)]
    upper, grad_second, to_next, to_prev = call(
        functools.partial(back_second_kernel, tile=13),
        [(size + 4, breadth, depth), (size + 4, breadth, depth)] + rim_shapes,
        conv_scratch(13) + edges(breadth),
        flags, cot_mine, cot_got, slope_second, *second_weights[2:4],
        name="back_second",
    )
    groups = place.groups()

    def weight_scratch(kinds, taps):
        turned = [pltpu.VMEM((kinds, depth, 12 * breadth), BF16) for _ in range(2)]
        return buffers(12) + turned + [pltpu.VMEM((taps, depth, depth), F32)]

    def second_weights_grad(to_next, to_prev, grad_second):
        behind, after = place.to_next(to_next), place.to_prev(to_prev)
        grads = call(
            functools.partial(weight_kernel, tile=12, first=False),
            [(9, own, depth)] * 2 + [(1, depth)],
            weight_scratch(2, 9) + pair(size + 6, depth),
            flags, hidden, h_left, h_ahead, grad_second,
            name="weight_second", paired=True,
        )
        return behind, after, *grads

    behind, after, keep, send, gb_second = block(
        second_weights_grad, to_next, to_prev, grad_second
    )
    out_got, send = lax.optimization_barrier((out_got, send))

    def first_weights_grad(keep, send, upper, behind, after):
        grads = call(
            functools.partial(weight_kernel, tile=12, first=True),
            [(10, own, depth)] * 2 + [(1, depth)] * 2 + [(size + 2, breadth, depth)],
            weight_scratch(4, 10),
            flags, scaled, x_left, x_right, upper, behind, after, slope_first, cot_mine, cot_got,
            name="weight_first", paired=True,
        )
        return place.flip(send, groups[0][0]), *grads

    gw_second = [keep]
    other, keep, send, gb_first, gb_skip, grad_first = block(
        first_weights_grad, keep, send, upper, behind, after
    )
    gw_second = [value.reshape(-1, depth) for value in (*gw_second, other)]

    def input_grad(part, *before):
        shapes = [(size // 2, breadth, own)] * 2
        shapes += rim_shapes if part else [(32, depth)] * 2 + [(breadth, depth)]
        scratch = conv_scratch(13) + pair(13 * breadth, 2 * depth, BF16) + edges(40)
        return call(
            functools.partial(back_first_kernel, tile=13, part=part),
            shapes, scratch + [pltpu.VMEM((26, breadth, depth), F32)],
            flags, grad_first, cot_mine, cot_got, *first_weights[2:4], *second_weights[6:8], *before,
            name="back_first_%d" % part,
        )

    def upper_half(send, grad_first, *gw_second):
        return place.shared(gw_second, groups[1]), place.flip(send, groups[0][0]), *input_grad(0)

    gw_second, other, own_upper, send_upper, *before = block(upper_half, send, grad_first, *gw_second)
    gw_first = [value.reshape(-1, depth) for value in (keep, other)]
    got_upper = place.across(send_upper)

    def lower_half(gw_second, keep, other, *before):
        for bits in groups[2:]:
            gw_second = place.shared((gw_second,), bits)
        return gw_second, place.shared((keep, other), groups[1]), *input_grad(1, *before)

    gw_second, gw_first, own_lower, send_lower, to_next, to_prev = block(
        lower_half, gw_second, *gw_first, *before
    )
    got_lower = place.across(send_lower)
    lower_own, lower_send, lower_got = (own_upper, own_lower), (send_upper, send_lower), (got_upper, got_lower)

    def last_sums(gw_second, gw_first, to_next, to_prev, lower_own, lower_send, out_own, out_got):
        behind, after = place.to_next(to_next), place.to_prev(to_prev)
        gate = (gw_first, gw_second, got_upper)
        gw_first, gw_second, _ = lax.optimization_barrier(gate)
        for bits in groups[2:]:
            gw_first = place.shared((gw_first,), bits)
        gate = (gw_first, lower_own, lower_send, out_own, got_lower)
        gw_first, lower_own, lower_send, out_own, _ = lax.optimization_barrier(gate)
        adds = jnp.concatenate([behind, after], axis=0)
        adds_got = place.across(adds[:, own:])
        column = jnp.arange(breadth)[None, :, None]
        row = jnp.arange(size)[:, None, None]
        edge = jnp.where(place.strip == 0, 0, size - 1)
        at_pole = place.side == 0

        def with_rims(value, adds):
            last = size + 2 + breadth
            value = value + jnp.where(column == 0, adds[1 : size + 1, None], 0.0)
            value = value + jnp.where(column == breadth - 1, adds[last + 1 : last + 1 + size, None], 0.0)
            return value + jnp.where((row == edge) & at_pole, adds[None, size + 2 : last], 0.0)

        sea_weight = sea_mask.astype(F32)[:, :, None]
        own_weight = lax.dynamic_slice_in_dim(sea_weight, place.half * size, size, 0)
        source = scaled[4 : size + 4]
        parts = []
        for value, lanes in ((lower_own, slice(0, own)), (lower_send, slice(own, depth))):
            value = with_rims(jnp.concatenate(value, axis=0), adds[:, lanes])
            parts.append(
                jnp.stack(
                    [
                        jnp.sum(own_weight * value, axis=(0, 1)),
                        jnp.sum(source[:, :, lanes] * value, axis=(0, 1)),
                    ]
                )
            )
        zeros = jnp.zeros((3, depth), F32)
        sums = [gb_first, gb_second, gb_skip, jnp.concatenate(parts, axis=1), zeros]
        sums = place.summed(jnp.concatenate(sums, axis=0))

        def collected(grad):
            grad = grad[:, :own] + place.across(grad[:, own:])
            for bits in reversed(groups[1:]):
                grad = place.spread(grad, bits)
            grad = grad.reshape(-1, own, own)
            other = place.flip(grad, groups[0][0])
            return jnp.concatenate(place.ordered(grad, other, groups[0][0]), axis=1)

        gw_second, gw_first = collected(gw_second), collected(gw_first)
        sums = sums[:, :own] + place.across(sums[:, own:])
        output, = call_copy(join_kernel, (rows, breadth, own), flags, out_own, out_got)
        adds_own = adds[:, :own]
        grad_half = final_call(0, flags, marked, lower_own, adds_own, stats, sums)
        return gw_second, gw_first[9], gw_first[:9], sums, adds_got, output, grad_half

    gw_second, gw_skip, gw_first, sums, adds_got, output, grad_half = last_sums(
        gw_second, gw_first, to_next, to_prev, lower_own, lower_send, out_own, out_got
    )
    late = (sums, gw_first, gw_second, gw_skip, grad_half, lower_got, adds_got)
    sums, gw_first, gw_second, gw_skip, grad_half, lower_got, adds_got = lax.optimization_barrier(late)
    grad_features = final_call(1, flags, marked, lower_got, adds_got, stats, sums, grad_half)
    new_mean = (1.0 - MOMENTUM) * run_mean + MOMENTUM * batch_mean
    new_var = (1.0 - MOMENTUM) * run_var + MOMENTUM * batch_var * sea_count / (sea_count - 1.0)
    return (
        output,
        grad_features,
        gw_first.reshape(3, 3, depth, own),
        sums[0],
        gw_second.reshape(3, 3, depth, own),
        sums[1],
        gw_skip,
        sums[2],
        new_mean,
        new_var,
    )


def solution(mesh):
    field, kernel, vector = P("pix", None, "ch"), P(None, None, None, "ch"), P("ch")
    placed = (
        field, P("pix", None), P(), kernel, vector, kernel, vector, P(None, "ch"), vector,
        vector, vector, field,
    )
    return jax.shard_map(
        functools.partial(local, mesh),
        mesh=mesh,
        in_specs=placed,
        out_specs=(
            field, field, kernel, vector, kernel, vector, P(None, "ch"), vector, vector, vector,
        ),
        check_vma=False,
    )
```

```python
import functools

import jax
import jax.numpy as jnp
from jax import lax
from jax.experimental import pallas as pl
from jax.experimental.pallas import tpu as pltpu
from jax.sharding import PartitionSpec as P

EPSILON = 1e-05
MOMENTUM = 0.1
INV_ROOT_TWO_PI = 0.3989422804014327
SQRT_HALF = 0.7071067811865476
F32 = jnp.float32
BF16 = jnp.bfloat16
VMEM_LIMIT = 60 * 1024 * 1024
LARGE = 512 * 1024


def split(value):
    high = value.astype(BF16)
    return high, (value - high.astype(F32)).astype(BF16)


def dot_split(a_high, a_low, b_high, b_low):
    total = jnp.dot(a_high, b_high, preferred_element_type=F32)
    total = total + jnp.dot(a_high, b_low, preferred_element_type=F32)
    return total + jnp.dot(a_low, b_high, preferred_element_type=F32)


def gelu_and_slope(u):
    cdf = 0.5 * (1.0 + lax.erf(u * SQRT_HALF))
    return u * cdf, cdf + u * jnp.exp(-0.5 * u * u) * INV_ROOT_TWO_PI


AT_TOP, AT_BOTTOM, SIDE, HALF, FLIPPED, PIX = range(6)
NOT_SEA = 1e30
LANES = 128


def lane_parts(depth):
    return [slice(start, start + LANES) for start in range(0, depth, LANES)]


def put_row(buffers, block, read, left, right, breadth, depth):
    high, low = buffers
    column = lax.broadcasted_iota(jnp.int32, (breadth, 1), 0)
    rows = slice(block * breadth, (block + 1) * breadth)
    for lanes in lane_parts(depth):
        value = read(lanes)
        shifts = (
            jnp.where(column == 0, left(lanes), pltpu.roll(value, 1, 0)),
            value,
            jnp.where(column == breadth - 1, right(lanes), pltpu.roll(value, breadth - 1, 0)),
        )
        for tap, piece in enumerate(shifts):
            place = slice(tap * depth + lanes.start, tap * depth + lanes.stop)
            high[rows, place], low[rows, place] = split(piece)


def conv_tile(buffers, w_high, w_low, total, tile, breadth):
    high, low = buffers
    value = None
    for row_tap in range(3):
        rows = slice(row_tap * breadth, (row_tap + tile) * breadth)
        part = dot_split(high[rows, :], low[rows, :], w_high[row_tap], w_low[row_tap])
        value = part if value is None else value + part
    total[...] = value


def pipeline(fill, multiply, finish, tiles, store=lambda tile: None):
    assert tiles % 2 == 0
    fill(0, 0, True)

    @pl.loop(0, tiles // 2)
    def _(step):
        tile = 2 * step
        fill(tile + 1, 1, True)
        multiply(0)
        finish(jnp.maximum(tile - 1, 0), 1)
        fill(jnp.minimum(tile + 2, tiles - 1), 0, tile + 2 < tiles)
        multiply(1)
        finish(tile, 0)

        @pl.when(step > 0)
        def _():
            store(tile - 1)

        store(tile)

    finish(tiles - 1, 1)
    store(tiles - 1)


def patch(flags, x, left, right, pole, top, bottom):
    breadth = x.shape[1]

    def put(at, edge):
        @pl.when(flags[FLIPPED] == 1)
        def _():
            for column in range(breadth):
                x[at, column : column + 1] = pole[breadth - 1 - column : breadth - column]

        @pl.when(flags[FLIPPED] == 0)
        def _():
            x[at] = pole[...]

        left[at : at + 1] = 0.5 * (x[at, 0:1] + left[edge : edge + 1])
        right[at : at + 1] = 0.5 * (x[at, breadth - 1 : breadth] + right[edge : edge + 1])

    @pl.when(flags[AT_TOP] == 1)
    def _():
        put(top, top + 1)

    @pl.when(flags[AT_BOTTOM] == 1)
    def _():
        put(bottom, bottom - 1)


def put_messages(flags, x, to_prev, to_next, first_row, last_row):
    rows, breadth = x.shape[0], x.shape[1]

    @pl.loop(0, rows)
    def _(row):
        to_prev[pl.ds(row, 1)] = x[row, 0:1]
        to_next[pl.ds(row, 1)] = x[row, breadth - 1 : breadth]

    to_prev[rows : rows + breadth] = x[jnp.where(flags[AT_BOTTOM] == 1, last_row, first_row)]


def first_kernel(
    traffic, flags, marked, got, halo_mine, halo_got, w_high, w_low, biases,
    scaled, x_left, x_right, hidden, slope, to_prev, to_next,
    pole, high0, low0, high1, low1, total0, total1, *, tile
):
    blocks, breadth, depth = scaled.shape
    own = depth // 2
    extra = blocks - got.shape[0]
    tail = halo_mine.shape[0] - 8
    start = flags[HALF] * (marked.shape[0] - got.shape[0])

    def normal(value, lanes):
        source = halo_mine if lanes.start == 0 else halo_got
        mean, inverse = source[tail : tail + 1], source[tail + 1 : tail + 2]
        return jnp.where(value > 0.1 * NOT_SEA, 0.0, (value - mean) * inverse)

    traffic.wait(0, 1)
    lower, upper = slice(0, own), slice(own, depth)
    main = jnp.where(flags[HALF] == 0, extra, 0)
    outer = jnp.where(flags[HALF] == 0, 0, blocks - extra)

    @pl.loop(0, got.shape[0])
    def _(row):
        scaled[main + row, :, lower] = normal(marked[start + row], lower)
        scaled[main + row, :, upper] = normal(got[row], upper)

    for row in range(extra):
        rows = slice(row * breadth, (row + 1) * breadth)
        scaled[outer + row, :, lower] = normal(halo_mine[rows], lower)
        scaled[outer + row, :, upper] = normal(halo_got[rows], upper)

    begin = extra * breadth
    for target, count in ((x_left, blocks), (x_right, blocks), (pole, breadth)):
        rows = slice(begin, begin + count)
        target[:, lower] = normal(halo_mine[rows], lower)
        target[:, upper] = normal(halo_got[rows], upper)
        begin = begin + count

    patch(flags, scaled, x_left, x_right, pole, 3, blocks - 4)
    traffic.store(0, 0, blocks)
    traffic.wait(4, 5)
    buffers, totals = ((high0, low0), (high1, low1)), (total0, total1)

    def fill(step, slot, fresh):
        for block in range(tile + 2):
            row = step * tile + block
            put_row(
                buffers[slot], block, lambda lanes: scaled[row, :, lanes],
                lambda lanes: x_left[pl.ds(row, 1)][:, lanes], lambda lanes: x_right[pl.ds(row, 1)][:, lanes],
                breadth, depth,
            )

    def finish(step, slot):
        for block in range(tile):
            for lanes in lane_parts(depth):
                pre = totals[slot][block * breadth : (block + 1) * breadth, lanes] + biases[0:1, lanes]
                value, grad = gelu_and_slope(pre)
                hidden[step * tile + block, :, lanes] = value
                slope[step * tile + block, :, lanes] = grad

    def store(step):
        traffic.store(3, step * tile, tile)
        traffic.store(4, step * tile, tile)

    pipeline(
        fill, lambda slot: conv_tile(buffers[slot], w_high, w_low, totals[slot], tile, breadth),
        finish, (blocks - 2) // tile, store,
    )
    put_messages(flags, hidden, to_prev, to_next, 3, blocks - 6)


def second_kernel(
    traffic, flags, x, left_in, ahead, w_high, w_low, biases, source, s_high, s_low,
    out_own, out_send, slope,
    left, right, high0, low0, high1, low1, total0, total1, skip0, skip1, sum0, sum1, *, tile
):
    blocks, breadth, depth = x.shape
    own = depth // 2
    left[...] = left_in[...]
    right[...] = ahead[:blocks]
    traffic.wait(0)
    patch(flags, x, left, right, ahead[blocks:], 2, blocks - 3)
    traffic.wait(3, 4, 6)
    buffers, totals, skips = ((high0, low0), (high1, low1)), (total0, total1), (skip0, skip1)
    sums = (sum0, sum1)

    def fill(step, slot, fresh):
        for block in range(tile + 2):
            row = step * tile + block
            put_row(
                buffers[slot], block, lambda lanes: x[row, :, lanes],
                lambda lanes: left[pl.ds(row, 1)][:, lanes], lambda lanes: right[pl.ds(row, 1)][:, lanes],
                breadth, depth,
            )
        for block in range(tile):
            rows = slice(block * breadth, (block + 1) * breadth)
            for lanes in lane_parts(depth):
                value = source[step * tile + block + 2, :, lanes]
                place = slice(depth + lanes.start, depth + lanes.stop)
                skips[slot][rows, lanes], skips[slot][rows, place] = split(value)

    def multiply(slot):
        conv_tile(buffers[slot], w_high, w_low, totals[slot], tile, breadth)
        skip = skips[slot]
        sums[slot][...] = dot_split(skip[:, :depth], skip[:, depth:], s_high[...], s_low[...])

    def finish(step, slot):
        for block in range(tile):
            row = step * tile + block
            rows = slice(block * breadth, (block + 1) * breadth)
            for lanes in lane_parts(depth):
                pre = totals[slot][rows, lanes] + biases[1:2, lanes]
                value, grad = gelu_and_slope(pre)
                slope[row, :, lanes] = grad
                value = value + sums[slot][rows, lanes] + biases[2:3, lanes]
                if lanes.stop <= own:
                    out_own[row, :, lanes] = value
                else:
                    out_send[row, :, lanes.start - own : lanes.stop - own] = value

    def store(step):
        for result in range(3):
            traffic.store(result, step * tile, tile)

    pipeline(fill, multiply, finish, (blocks - 2) // tile, store)


def edge_products(edges, w_high, w_low, slot, count):
    depth = edges.shape[0] * LANES
    total = None
    for tap in range(3):
        rows = slice(slot * depth, (slot + 1) * depth)
        pieces = [edges[part, tap : tap + count] for part in range(edges.shape[0])]
        edge_high, edge_low = split(jnp.concatenate(pieces, axis=1))
        part = dot_split(edge_high, edge_low, w_high[tap, rows], w_low[tap, rows])
        total = part if total is None else total + part
    return total


def put_rims(flags, to_next, to_prev, first_rim, last_rim, top, bottom):
    count, breadth = to_prev.shape[0], top.shape[0]
    to_prev[...] = first_rim[:count]
    to_next[:count] = last_rim[:count]
    to_next[count:] = jnp.zeros((breadth, to_next.shape[1]), F32)
    column = lax.broadcasted_iota(jnp.int32, (breadth, 1), 0)

    def put(row, at, inner):
        corner_first, corner_last = 0.5 * first_rim[at : at + 1], 0.5 * last_rim[at : at + 1]
        to_prev[inner : inner + 1] += corner_first
        to_next[inner : inner + 1] += corner_last
        row = row[...] + jnp.where(column == 0, corner_first, 0.0)
        row = row + jnp.where(column == breadth - 1, corner_last, 0.0)

        @pl.when(flags[FLIPPED] == 0)
        def _():
            to_next[count:] = row

        @pl.when(flags[FLIPPED] == 1)
        def _():
            for k in range(breadth):
                to_next[count + k : count + k + 1] = row[breadth - 1 - k : breadth - k]

    @pl.when(flags[AT_TOP] == 1)
    def _():
        put(top, 0, 1)

    @pl.when(flags[AT_BOTTOM] == 1)
    def _():
        put(bottom, count - 1, count - 2)


def back_second_kernel(
    traffic, flags, cot_mine, cot_got, slope, w_high, w_low,
    out, grad, to_next, to_prev,
    high0, low0, high1, low1, total0, total1, edge_first, edge_last, *, tile
):
    blocks, breadth, depth = slope.shape
    own = depth // 2
    traffic.wait(0, 1, 2)
    edge_first[...] = jnp.zeros_like(edge_first)
    edge_last[...] = jnp.zeros_like(edge_last)
    buffers, totals = ((high0, low0), (high1, low1)), (total0, total1)

    def fill(step, slot, fresh):
        for block in range(tile + 2):
            row = jnp.minimum(step * tile + block, blocks - 1)
            outside = (flags[AT_TOP] == 1) & (row < 2) | (flags[AT_BOTTOM] == 1) & (row >= blocks - 2)
            inside = jnp.where(outside, 0.0, 1.0)

            def read(lanes):
                cot = cot_mine[row] if lanes.stop <= own else cot_got[row]
                value = cot * slope[row, :, lanes] * inside
                grad[row, :, lanes] = value
                edge_first[lanes.start // LANES, pl.ds(row, 1)] = value[0:1]
                edge_last[lanes.start // LANES, pl.ds(row, 1)] = value[breadth - 1 : breadth]
                return value

            put_row(buffers[slot], block, read, lambda lanes: 0.0, lambda lanes: 0.0, breadth, depth)

    def finish(step, slot):
        for block in range(tile):
            out[step * tile + block] = totals[slot][block * breadth : (block + 1) * breadth]

    traffic.wait(3, 4)
    pipeline(
        fill, lambda slot: conv_tile(buffers[slot], w_high, w_low, totals[slot], tile, breadth),
        finish, blocks // tile, lambda step: traffic.store(0, step * tile, tile),
    )
    traffic.store(1, 0, blocks)
    rows = blocks + 4
    first_rim = edge_products(edge_first, w_high, w_low, 2, rows)
    last_rim = edge_products(edge_last, w_high, w_low, 0, rows)
    put_rims(flags, to_next, to_prev, first_rim, last_rim, out[0], out[blocks - 3])


def back_first_kernel(
    traffic, flags, grad, cot_mine, cot_got, w_high, w_low, s_high, s_low, *rest, tile, part
):
    if part:
        before_first, before_last, before_top, out_own, out_send, to_next, to_prev = rest[:7]
    else:
        out_own, out_send, rim_first, rim_last, top = rest[:5]
    high0, low0, high1, low1, total0, total1, skip0, skip1, edge_first, edge_last, result = rest[-11:]
    count, breadth, depth = grad.shape
    own = depth // 2
    begin = part * ((count - 2) // 2)
    blocks = result.shape[0]
    edge_first[...] = jnp.zeros_like(edge_first)
    edge_last[...] = jnp.zeros_like(edge_last)
    buffers, totals, skips = ((high0, low0), (high1, low1)), (total0, total1), (skip0, skip1)
    traffic.wait(0, 1, 2)

    def fill(step, slot, fresh):
        for block in range(tile + 2):
            at = step * tile + block
            row = begin + at - 1
            inside = jnp.where((row >= 0) & (row < count), 1.0, 0.0)
            row = jnp.clip(row, 0, count - 1)

            def read(lanes):
                value = grad[row, :, lanes] * inside
                edge_first[lanes.start // LANES, pl.ds(at, 1)] = value[0:1]
                edge_last[lanes.start // LANES, pl.ds(at, 1)] = value[breadth - 1 : breadth]
                return value

            put_row(buffers[slot], block, read, lambda lanes: 0.0, lambda lanes: 0.0, breadth, depth)
        for block in range(tile):
            row = begin + step * tile + block
            inside = jnp.where((row >= 1) & (row < count - 1), 1.0, 0.0)
            rows = slice(block * breadth, (block + 1) * breadth)
            for lanes in lane_parts(depth):
                cot = cot_mine[row + 1] if lanes.stop <= own else cot_got[row + 1]
                place = slice(depth + lanes.start, depth + lanes.stop)
                skips[slot][rows, lanes], skips[slot][rows, place] = split(cot * inside)

    def multiply(slot):
        conv_tile(buffers[slot], w_high, w_low, totals[slot], tile, breadth)
        skip = skips[slot]
        totals[slot][...] += dot_split(skip[:, :depth], skip[:, depth:], s_high[...], s_low[...])

    def finish(step, slot):
        for block in range(tile):
            result[step * tile + block] = totals[slot][block * breadth : (block + 1) * breadth]

    traffic.wait(3, 4)
    pipeline(fill, multiply, finish, blocks // tile)

    @pl.loop(0, out_own.shape[0])
    def _(row):
        out_own[row] = result[row + 1, :, :own]
        out_send[row] = result[row + 1, :, own:]

    traffic.store(0 if part == 0 else 0, 0, out_own.shape[0])
    traffic.store(1, 0, out_own.shape[0])
    rows = blocks + 6
    first_rim = edge_products(edge_first, w_high, w_low, 2, rows)
    last_rim = edge_products(edge_last, w_high, w_low, 0, rows)
    if part == 0:
        rim_first[...], rim_last[...] = first_rim, last_rim
        top[...] = result[0]
    else:
        joined = [
            jnp.concatenate([before[: begin + 1], now[1 : begin + 2]], axis=0)
            for before, now in ((before_first, first_rim), (before_last, last_rim))
        ]
        put_rims(flags, to_next, to_prev, *joined, before_top[...], result[blocks - 1])


def weight_kernel(traffic, flags, x, *rest, tile, first):
    if first:
        left, right, upper, behind, after, slope, cot_mine, cot_got = rest[:8]
        parts, _, total, total_skip, grad_out = rest[8:13]
        rest, begin = rest[13:], 3
    else:
        left_in, ahead, grad = rest[:3]
        parts, _, total = rest[3:6]
        left, right = rest[-2:]
        rest, begin = rest[6:-2], 2
    high0, low0, high1, low1, t0, t1, acc = rest[:7]
    buffers, turned = ((high0, low0), (high1, low1)), (t0, t1)
    breadth, depth = x.shape[1:]
    own = depth // 2
    taps = acc.shape[0]
    rows = x.shape[0] - 2 * begin - 2
    pixels = tile * breadth
    traffic.wait(0)
    if first:
        count = rows + 2
        column = lax.broadcasted_iota(jnp.int32, (breadth, 1), 0)
        traffic.wait(3, 6, 7, 8)
        total_skip[...] = jnp.zeros_like(total_skip)

        def read(row, lanes):
            at = row + 1
            edge = (flags[AT_TOP] == 1) & (row == 0) | (flags[AT_BOTTOM] == 1) & (row == rows - 1)
            value = upper[at, :, lanes] + jnp.where(column == 0, behind[pl.ds(at, 1)][:, lanes], 0.0)
            value = value + jnp.where(column == breadth - 1, after[pl.ds(at, 1)][:, lanes], 0.0)
            value = value + behind[count : count + breadth, lanes] * jnp.where(edge, 1.0, 0.0)
            value = value * slope[at + 2, :, lanes]
            grad_out[at, :, lanes] = value
            return value

        for row, pole in ((-1, AT_TOP), (rows, AT_BOTTOM)):
            for lanes in lane_parts(depth):
                value = read(row, lanes)
                grad_out[row + 1, :, lanes] = value * jnp.where(flags[pole] == 1, 0.0, 1.0)
    else:
        left[...] = left_in[...]
        right[...] = ahead[: x.shape[0]]
        patch(flags, x, left, right, ahead[x.shape[0] :], 2, x.shape[0] - 3)
        traffic.wait(3)

        def read(row, lanes):
            return grad[row + 2, :, lanes]

    acc[...] = jnp.zeros_like(acc)
    total[...] = jnp.zeros_like(total)

    def turn(slot, place, lanes, value):
        value_high, value_low = split(value.T)
        turned[slot][place, lanes] = value_high
        turned[slot][place + 1, lanes] = value_low

    def fill(step, slot, fresh):
        once = jnp.where(fresh, 1.0, 0.0)
        for block in range(tile + 2):
            row = step * tile + block + begin
            put_row(
                buffers[slot], block, lambda lanes: x[row, :, lanes],
                lambda lanes: left[pl.ds(row, 1)][:, lanes], lambda lanes: right[pl.ds(row, 1)][:, lanes],
                breadth, depth,
            )
        for lanes in lane_parts(depth):
            value = jnp.concatenate([read(step * tile + block, lanes) for block in range(tile)], axis=0)
            total[:, lanes] += jnp.sum(value, axis=0, keepdims=True) * once
            turn(slot, 0, lanes, value)
            if first:
                source = cot_mine if lanes.stop <= own else cot_got
                value = source[pl.ds(step * tile + 2, tile)].reshape(pixels, LANES)
                total_skip[:, lanes] += jnp.sum(value, axis=0, keepdims=True) * once
                turn(slot, 2, lanes, value)

    def multiply(slot):
        high, low = buffers[slot]
        for tap in range(taps):
            row_tap, column_tap, place = (tap // 3, tap % 3, 0) if tap < 9 else (1, 1, 2)
            window = slice(row_tap * breadth, row_tap * breadth + pixels)
            lanes = slice(column_tap * depth, (column_tap + 1) * depth)
            acc[tap] += dot_split(
                turned[slot][place], turned[slot][place + 1], high[window, lanes], low[window, lanes]
            )

    pipeline(fill, multiply, lambda step, slot: None, rows // tile)
    half = depth // 2
    mine = (flags[SIDE] ^ flags[PIX]) & 1
    for tap in range(taps):
        value = acc[tap].T
        parts[mine, tap] = value[:half]
        parts[1 - mine, tap] = value[half:]


def weights_kernel(traffic, flags, mine, *rest, steps, skip):
    shares, rest = rest[: steps + 1], rest[steps + 1 :]
    if skip:
        mine_skip, f_high, f_low, b_high, b_low, s_high, s_low, sb_high, sb_low, other = rest
    else:
        f_high, f_low, b_high, b_low, other = rest
    own = mine.shape[1]
    depth = 2 * own
    taps = mine.shape[0]
    count = 1 << steps
    traffic.wait(*traffic.ins)
    share, share_skip = taps // count, depth // count
    unit = shares[0].shape[0]
    begin = share if skip else 0
    for piece in range(count):
        away = sum(1 << (steps - 1 - step) for step in range(steps) if piece >> step & 1)
        index = (flags[PIX] & (count - 1)) ^ away
        level = piece.bit_length()
        source = shares[level]
        at = (piece - (1 << (level - 1)) if level else 0) * unit + begin
        other[pl.ds(pl.multiple_of(index * share, 8), share)] = source[at : at + share]
        if skip:
            start = pl.multiple_of(taps + index * share_skip, 8)
            other[pl.ds(start, share_skip)] = source[at + share : at + share + share_skip]
    def both(first, second):
        return jnp.concatenate([first, second], axis=1)

    def one_tap(row_tap, column_tap):
        tap, back_row, back_column = row_tap * 3 + column_tap, 2 - row_tap, 2 - column_tap
        for part in range(2):
            at = pl.multiple_of(tap * depth + jnp.where(flags[SIDE] == part, 0, own), own)
            value = both(mine[pl.ds(at, own)], other[pl.ds(at, own)])
            value_high, value_low = split(value)
            place = pl.ds(pl.multiple_of(column_tap * depth + part * own, own), own)
            f_high[row_tap, place] = value_high
            f_low[row_tap, place] = value_low
            turned_high, turned_low = split(value.T)
            place = pl.ds(pl.multiple_of(back_column * depth, depth), depth)
            lanes = slice(part * own, (part + 1) * own)
            b_high[back_row, place, lanes] = turned_high
            b_low[back_row, place, lanes] = turned_low

    for row_tap in range(3):
        pl.loop(0, 3)(functools.partial(one_tap, row_tap))
        for result in range(4):
            traffic.store(result, row_tap if result < 2 else 2 - row_tap, 1)

    if skip:
        for part in range(2):
            at = pl.multiple_of(jnp.where(flags[SIDE] == part, 0, own), own)
            value = both(mine_skip[pl.ds(at, own)], other[pl.ds(pl.multiple_of(taps + at, own), own)])
            lanes = slice(part * own, (part + 1) * own)
            s_high[lanes], s_low[lanes] = split(value)
            sb_high[:, lanes], sb_low[:, lanes] = split(value.T)


def pre_kernel(traffic, flags, features, mask, marked, theirs, stats, inner, to_prev, to_next):
    rows, breadth, own = features.shape
    length = theirs.shape[0]
    traffic.wait(0)
    start = (1 - flags[HALF]) * (rows - length)
    turned = mask[...].astype(F32)
    turned = jnp.concatenate([turned, jnp.zeros((breadth, 128 - rows), F32)], axis=1)
    none = jnp.zeros((8, own), F32)

    def fold(v):
        return jnp.sum(v.reshape(breadth // 8, 8, own), axis=0)

    def first(step, carry):
        count, total = carry
        base = step * 8
        sea_of = pltpu.roll(turned, 128 - base, 1)
        for k in range(8):
            row = base + k
            sea = jnp.broadcast_to(sea_of[:, k : k + 1], (breadth, own))
            value = features[row]
            land = jnp.where(sea > 0.5, value, NOT_SEA)
            marked[row] = land
            to_prev[pl.ds(row, 1)] = land[0:1]
            to_next[pl.ds(row, 1)] = land[breadth - 1 : breadth]
            count, total = count + fold(sea), total + fold(value * sea)
        return count, total

    count, total = lax.fori_loop(0, rows // 8, first, (none, none))
    count = jnp.sum(count, axis=0, keepdims=True)
    mean = jnp.sum(total, axis=0, keepdims=True) / jnp.maximum(count, 1.0)

    def second(step, squares):
        for k in range(8):
            value = marked[step * 8 + k]
            value = jnp.where(value > 0.1 * NOT_SEA, 0.0, value - mean)
            squares = squares + fold(value * value)
        return squares

    @pl.loop(0, length // 4)
    def _(step):
        theirs[pl.ds(step * 4, 4)] = marked[pl.ds(start + step * 4, 4)]

    traffic.store(1, 0, length)
    traffic.store(0, 0, rows)
    squares = lax.fori_loop(0, rows // 8, second, none)

    stats[...] = jnp.zeros_like(stats)
    stats[0:1] = count
    stats[1:2] = mean
    stats[2:3] = jnp.sum(squares, axis=0, keepdims=True)
    strip = flags[SIDE] ^ flags[HALF]
    to_prev[rows:] = marked[strip * (rows - 1)]
    inner[...] = marked[pl.ds((1 - strip) * (rows - inner.shape[0]), inner.shape[0])]


def cot_kernel(traffic, flags, cot, extra, mine, early, late):
    rows, more, count = cot.shape[0], extra.shape[0], mine.shape[0]
    traffic.wait(0)

    def put(target, begin, half):
        length = target.shape[0]

        @pl.loop(0, length)
        def _(row):
            target[row] = cot[jnp.clip(begin + row - more + half * (rows // 2), 0, rows - 1)]

        if begin == 0:

            @pl.when(half == 0)
            def _():
                target[:more] = extra[...]

        if begin + length == count:

            @pl.when(half == 1)
            def _():
                target[length - more :] = extra[...]

    put(early, 0, 1 - flags[HALF])
    put(late, early.shape[0], 1 - flags[HALF])
    put(mine, 0, flags[HALF])


def rims_kernel(traffic, flags, behind, ahead, core, stats, mine, theirs, wide):
    rows, own = behind.shape
    breadth = ahead.shape[0] - rows
    extra = (core.shape[0]) // (breadth + 2)
    length = rows // 2 + 2 * extra
    inner = extra * breadth
    at = inner
    for target in (mine, theirs):
        target[:inner] = core[:inner]
    for source, start in ((behind, inner + extra), (ahead, inner)):
        wide[:extra] = core[start : start + extra]
        wide[extra : extra + rows] = source[:rows]
        wide[extra + rows :] = core[start : start + extra]
        for target, half in ((mine, flags[HALF]), (theirs, 1 - flags[HALF])):
            target[at : at + length] = wide[pl.ds(pl.multiple_of(half * (rows // 2), 8), length)]
        at = at + length
    count, mean, squares = stats[0:1], stats[1:2], stats[2:3]
    inverse = lax.rsqrt(squares / count + EPSILON)
    for target in (mine, theirs):
        target[at : at + breadth] = ahead[rows:]
        target[at + breadth :] = jnp.zeros((8, own), F32)
        target[at + breadth : at + breadth + 1] = mean
        target[at + breadth + 1 : at + breadth + 2] = inverse


def gather_kernel(flags, second_mine, second_other, first_mine, first_other, second, first, skip, sems):
    half = second_mine.shape[1]
    here = (flags[PIX] & 1) * half
    copies = []
    for place, (mine, start) in enumerate(
        (
            (second_mine, here), (second_other, half - here),
            (first_mine, here), (first_other, half - here),
        )
    ):
        rows = pl.ds(pl.multiple_of(start, half), half)
        target = second if place < 2 else first
        copies.append(pltpu.make_async_copy(mine.at[pl.ds(0, 9)], target.at[:, rows], sems.at[place]))
        if place >= 2:
            copies.append(pltpu.make_async_copy(mine.at[9], skip.at[rows], sems.at[place + 2]))
    for copy in copies:
        copy.start()
    for copy in copies:
        copy.wait()


def gather_call(flags, *operands):
    anywhere, whole = pl.BlockSpec(memory_space=pl.ANY), pl.BlockSpec(memory_space=pltpu.VMEM)
    half, own = operands[0].shape[1:]
    shapes = [(9, 2 * half, own), (9, 2 * half, own), (2 * half, own)]
    return pl.pallas_call(
        gather_kernel,
        out_shape=[jax.ShapeDtypeStruct(shape, F32) for shape in shapes],
        in_specs=[pl.BlockSpec(memory_space=pltpu.SMEM)] + [whole] * 4,
        out_specs=[anywhere] * 3,
        scratch_shapes=[pltpu.SemaphoreType.DMA((6,))],
        compiler_params=pltpu.CompilerParams(vmem_limit_bytes=VMEM_LIMIT),
        cost_estimate=pl.CostEstimate(flops=0, bytes_accessed=12_000_000, transcendentals=0),
        name="gather",
    )(flags, *operands)


def final_kernel(flags, marked, lower_upper, lower_lower, rims, stats, sums, *rest, other, parts):
    out, source, result, in_sems, out_sems = rest[-5:]
    rows, breadth, own = marked.shape
    size = rows // 2
    step = size // parts
    last = size + 2 + breadth
    count, mean = stats[0:1], stats[1:2]
    inverse = lax.rsqrt(stats[2:3] / count + EPSILON)
    first_mean, second_mean = sums[3:4] / count, sums[4:5] / count
    column = lax.broadcasted_iota(jnp.int32, (breadth, 1), 0)
    strip = flags[SIDE] ^ flags[HALF]
    edge = strip * (size - 1)
    half = 1 - flags[HALF] if other else flags[HALF]
    at_pole = flags[SIDE] == (1 if other else 0)

    def fetch(part):
        rows = pl.ds(half * size + part * step, step)
        return pltpu.make_async_copy(marked.at[rows], source.at[pl.ds(part * step, step)], in_sems.at[part])

    def store(part):
        rows = pl.ds(half * size + part * step, step)
        return pltpu.make_async_copy(result.at[pl.ds(part * step, step)], out.at[rows], out_sems.at[part])

    for part in range(parts):
        fetch(part).start()
    for part in range(parts):
        fetch(part).wait()

        lower = lower_upper if part < parts // 2 else lower_lower

        @pl.loop(part * step, (part + 1) * step)
        def _(row):
            value = lower[row % (size // 2)] + jnp.where(column == 0, rims[pl.ds(row + 1, 1)], 0.0)
            value = value + jnp.where(column == breadth - 1, rims[pl.ds(row + last + 1, 1)], 0.0)
            at_edge = jnp.where((row == edge) & at_pole, 1.0, 0.0)
            value = value + rims[size + 2 : last] * at_edge
            normed = (source[row] - mean) * inverse
            value = inverse * (value - first_mean - normed * second_mean)
            result[row] = jnp.where(source[row] > 0.1 * NOT_SEA, 0.0, value)

        store(part).start()
    for part in range(parts):
        store(part).wait()


def final_call(other, flags, marked, lower, rims, stats, sums, before=None):
    anywhere, whole = pl.BlockSpec(memory_space=pl.ANY), pl.BlockSpec(memory_space=pltpu.VMEM)
    parts = 4
    operands = [flags, marked, *lower, rims, stats, sums] + ([before] if other else [])
    half = pltpu.VMEM((marked.shape[0] // 2,) + marked.shape[1:], F32)
    return pl.pallas_call(
        functools.partial(final_kernel, other=other, parts=parts),
        out_shape=jax.ShapeDtypeStruct(marked.shape, F32),
        in_specs=[pl.BlockSpec(memory_space=pltpu.SMEM), anywhere] + [whole] * 5 + [anywhere] * other,
        out_specs=anywhere,
        scratch_shapes=[half, half, pltpu.SemaphoreType.DMA((parts,)), pltpu.SemaphoreType.DMA((parts,))],
        input_output_aliases={7: 0} if other else {},
        compiler_params=pltpu.CompilerParams(vmem_limit_bytes=VMEM_LIMIT),
        cost_estimate=pl.CostEstimate(flops=0, bytes_accessed=4 * marked.size * 3, transcendentals=0),
        name="final_got" if other else "final_own",
    )(*operands)


def join_kernel(flags, mine, theirs, out, sems):
    size = out.shape[0] // 2
    skip = (mine.shape[0] - size) // 2
    copies = []
    for place, source in enumerate((mine, theirs)):
        half = flags[HALF] if place == 0 else 1 - flags[HALF]
        target = out.at[pl.ds(half * size, size)]
        copies.append(pltpu.make_async_copy(source.at[pl.ds(skip, size)], target, sems.at[place]))
    for copy in copies:
        copy.start()
    for copy in copies:
        copy.wait()


def call_copy(kernel, shape, flags, *operands):
    anywhere = pl.BlockSpec(memory_space=pl.ANY)
    return pl.pallas_call(
        kernel,
        out_shape=[jax.ShapeDtypeStruct(shape, F32)],
        in_specs=[pl.BlockSpec(memory_space=pltpu.SMEM)]
        + [pl.BlockSpec(memory_space=pltpu.VMEM)] * len(operands),
        out_specs=[anywhere],
        scratch_shapes=[pltpu.SemaphoreType.DMA((len(operands),))],
        compiler_params=pltpu.CompilerParams(vmem_limit_bytes=VMEM_LIMIT),
        cost_estimate=pl.CostEstimate(flops=0, bytes_accessed=0, transcendentals=0),
        name="join",
    )(flags, *operands)


class Traffic:
    def __init__(self, ins, outs):
        self.ins, self.outs, self.parts = ins, outs, {}
        for copies in ins.values():
            for copy in copies:
                copy.start()

    def wait(self, *places):
        for place in places:
            for copy in self.ins.pop(place):
                copy.wait()

    def store(self, place, start, count):
        source, target, sem = self.outs[place]
        rows = pl.ds(start, count)
        pltpu.make_async_copy(source.at[rows], target.at[rows], sem).start()
        self.parts[place] = True

    def finish(self):
        for place in self.outs:
            if place not in self.parts:
                pltpu.make_async_copy(*self.outs[place]).start()
        for place in self.outs:
            pltpu.make_async_copy(*self.outs[place]).wait()


def call(kernel, shapes, scratch, flags, *operands, name=None, paired=False):
    shapes = [s if isinstance(s, jax.ShapeDtypeStruct) else jax.ShapeDtypeStruct(s, F32) for s in shapes]

    operands = [operand if isinstance(operand, tuple) else (operand,) for operand in operands]
    wholes = [
        jax.ShapeDtypeStruct((sum(part.shape[0] for part in parts),) + parts[0].shape[1:], parts[0].dtype)
        for parts in operands
    ]
    counts = [len(parts) for parts in operands]
    operands = [part for parts in operands for part in parts]

    def large(a):
        return a.size * a.dtype.itemsize >= LARGE

    inside, outside = [large(a) for a in wholes], [large(a) for a in shapes]
    split_up = [is_large for is_large, count in zip(inside, counts) for _ in range(count)]
    buffers = [pltpu.VMEM(a.shape, a.dtype) for a in wholes + shapes[2 * paired :] if large(a)]
    if paired:
        buffers.append(pltpu.VMEM((2,) + shapes[0].shape, F32))
    sems = [pltpu.SemaphoreType.DMA((max(1, sum(group)),)) for group in (split_up, outside)]
    anywhere, whole = pl.BlockSpec(memory_space=pl.ANY), pl.BlockSpec(memory_space=pltpu.VMEM)

    def body(flags, *refs):
        refs = list(refs)
        given = len(operands) + len(shapes)
        rest, (in_sems, out_sems) = refs[given : len(refs) - 2], refs[-2:]
        held, extra = rest[: len(buffers)], rest[len(buffers) :]
        ins, outs, seen, sources, started = {}, {}, [], refs[: len(operands)], 0
        for place, is_large in enumerate(inside):
            parts = [sources.pop(0) for _ in range(counts[place])]
            if not is_large:
                seen.append(parts[0])
                continue
            buffer, row = held.pop(0), 0
            ins[place] = []
            for part in parts:
                target = buffer.at[pl.ds(row, part.shape[0])] if len(parts) > 1 else buffer
                ins[place].append(pltpu.make_async_copy(part, target, in_sems.at[started]))
                row, started = row + part.shape[0], started + 1
            seen.append(buffer)
        for place, is_large in enumerate(outside):
            ref = refs[len(operands) + place]
            if paired and place < 2:
                outs[place] = (held[-1].at[place], ref, out_sems.at[len(outs)])
                seen.append(held[-1])
            elif is_large:
                buffer = held.pop(0)
                outs[place] = (buffer, ref, out_sems.at[len(outs)])
                seen.append(buffer)
            else:
                seen.append(ref)
        traffic = Traffic(ins, outs)
        kernel(traffic, flags, *seen, *extra)
        assert not traffic.ins
        traffic.finish()

    return pl.pallas_call(
        body,
        out_shape=shapes,
        in_specs=[pl.BlockSpec(memory_space=pltpu.SMEM)] + [anywhere if k else whole for k in split_up],
        out_specs=[anywhere if k else whole for k in outside],
        scratch_shapes=buffers + list(scratch) + sems,
        compiler_params=pltpu.CompilerParams(vmem_limit_bytes=VMEM_LIMIT),
        cost_estimate=pl.CostEstimate(flops=0, bytes_accessed=0, transcendentals=0),
        name=name,
    )(flags, *operands)


class Place:
    def __init__(self, mesh, rows, breadth):
        self.count = mesh.shape["pix"]
        self.strips = 3 * breadth // rows
        assert mesh.shape["ch"] == 2 and self.strips == 2
        self.pix = lax.axis_index("pix")
        self.side = lax.axis_index("ch")
        self.ribbon = self.pix // self.strips % 4
        self.strip = self.pix % self.strips
        self.half = self.side ^ self.strip
        self.at_top = (self.side == 0) & (self.strip == 0)
        self.at_bottom = (self.side == 0) & (self.strip == 1)

    def ribbon_pairs(self, offset):
        pairs = []
        for index in range(self.count):
            sample, strip = index // (4 * self.strips), index % self.strips
            ribbon = (index // self.strips + offset) % 4
            pairs.append((index, (sample * 4 + ribbon) * self.strips + strip))
        return pairs

    def to_next(self, value):
        return lax.ppermute(value, "pix", self.ribbon_pairs(1))

    def to_prev(self, value):
        return lax.ppermute(value, "pix", self.ribbon_pairs(-1))

    def across(self, value):
        return lax.ppermute(value, "ch", [(0, 1), (1, 0)])

    def flip(self, value, bit):
        return lax.ppermute(value, "pix", [(i, i ^ bit) for i in range(self.count)])

    def bits(self):
        return [1 << step for step in range(self.count.bit_length() - 1)]

    def ordered(self, mine, theirs, bit):
        upper = (self.pix & bit) != 0
        return jnp.where(upper, theirs, mine), jnp.where(upper, mine, theirs)

    def near(self):
        return self.bits()[:3]

    def members(self, bits):
        out = []
        for other in range(1, 1 << len(bits)):
            mask = sum(bit for step, bit in enumerate(bits) if other >> step & 1)
            out.append((other, [(i, i ^ mask) for i in range(self.count)]))
        return out

    def number(self, bits):
        total = 0
        for step, bit in enumerate(bits):
            total = total + (((self.pix & bit) != 0).astype(jnp.int32) << step)
        return total

    def shared(self, values, bits):
        me, length = self.number(bits), values[0].shape[0] >> len(bits)

        def share(number):
            pieces = [lax.dynamic_slice_in_dim(value, number * length, length, 0) for value in values]
            return functools.reduce(jnp.add, pieces)

        total = share(me)
        parts = []
        for other, pairs in self.members(bits):
            piece = share(me ^ other)
            parts.append(lax.ppermute(piece, "pix", pairs))
        for part in parts:
            total = total + part
        return total

    def spread(self, value, bits):
        parts = [value] + [lax.ppermute(value, "pix", pairs) for _, pairs in self.members(bits)]
        for step, bit in enumerate(bits):
            upper = (self.pix & bit) != 0
            parts = [
                jnp.where(upper, parts[k ^ (1 << step)], parts[k]) for k in range(len(parts))
            ]
        return jnp.concatenate(parts, axis=0)

    def groups(self):
        bits = self.bits()
        rest = [bits[k : k + 2] for k in range(2, len(bits), 2)]
        return [bits[:1], bits[1:2]] + rest

    def summed(self, value):
        for bit in self.bits():
            first, second = self.ordered(value, self.flip(value, bit), bit)
            value = first + second
        return value

    def part(self, value, half, start, length):
        return lax.dynamic_slice_in_dim(value, half * start, length, 0)

    def join_rows(self, mine, theirs):
        return jnp.where(
            self.half == 0,
            jnp.concatenate([mine, theirs], axis=0),
            jnp.concatenate([theirs, mine], axis=0),
        )

    def inner_rows(self, value, extra):
        edge = jnp.where(self.strip == 0, value[-extra:], value[:extra])
        return self.flip(edge, 1)


def merged_stats(place, state):
    for bit in place.bits():
        first, second = place.ordered(state, place.flip(state, bit), bit)
        total = first[0] + second[0]
        safe = jnp.maximum(total, 1.0)
        step = second[1] - first[1]
        state = jnp.stack(
            [
                total,
                (first[0] * first[1] + second[0] * second[1]) / safe,
                first[2] + second[2] + step * step * (first[0] * second[0] / safe),
            ]
            + [total] * 5
        )
    return state


def local(
    mesh, features, sea_mask, edge_flip, w_first, b_first, w_second, b_second, w_skip, b_skip,
    run_mean, run_var, cotangent,
):
    rows, breadth, own = features.shape
    place = Place(mesh, rows, breadth)
    size, depth = rows // 2, 2 * own
    taps = 9 * depth
    flip_row = jnp.sum(jnp.where((jnp.arange(4) == place.ribbon)[:, None], edge_flip, 0), axis=0)
    flipped = jnp.where(place.strip == 0, flip_row[0], flip_row[1]) == 1
    flags = jnp.stack(
        [
            jnp.where(flag, 1, 0).astype(jnp.int32)
            for flag in (place.at_top, place.at_bottom, place.side == 1, place.half == 1, flipped)
        ]
        + [place.pix.astype(jnp.int32)]
    )

    w_first, w_second = w_first.reshape(taps, own), w_second.reshape(taps, own)
    near = len(place.near())
    share, share_skip, number = taps >> near, depth >> near, place.number(place.near())
    biases = jnp.stack([b_first, b_second, b_skip])
    message = jnp.concatenate(
        [
            lax.dynamic_slice_in_dim(w_first, number * share, share, 0),
            lax.dynamic_slice_in_dim(w_second, number * share, share, 0),
            lax.dynamic_slice_in_dim(w_skip, number * share_skip, share_skip, 0),
            jnp.pad(biases, ((0, 5), (0, 0))),
        ]
    )
    features, message = lax.optimization_barrier((features, message))
    message = place.across(message)
    marked, theirs, stats, inner, to_prev, to_next = call(
        pre_kernel,
        [
            (rows, breadth, own), (size + 4, breadth, own), (8, own), (4, breadth, own),
            (rows + breadth, own), (rows, own),
        ],
        [], flags, features, sea_mask.T, name="pre",
    )
    theirs, message = lax.optimization_barrier((theirs, message))
    got = place.across(theirs)
    biases = jnp.concatenate([biases, message[2 * share + share_skip :][:3]], axis=1)
    cot_inner = place.inner_rows(cotangent, 2)

    def neighbours(stats, inner, to_prev, to_next, message):
        mine = message[: 2 * share + share_skip]
        bits = place.near()
        ahead, behind = place.to_prev(to_prev), place.to_next(to_next)
        shares = [mine, place.flip(mine, bits[2])]
        shares[1], ahead, behind = lax.optimization_barrier((shares[1], ahead, behind))
        shares.append(place.flip(jnp.concatenate(shares, axis=0), bits[1]))

        def inner_part(value):
            return jnp.where(place.strip == 0, value[rows - 4 : rows], value[:4])

        core = jnp.concatenate(
            [inner.reshape(-1, own), inner_part(ahead), inner_part(behind)], axis=0
        )
        core = place.flip(core, 1)
        stats = merged_stats(place, stats)
        halo_mine, halo_theirs = call(
            rims_kernel, [(rim_rows, own)] * 2, [pltpu.VMEM((rows + 8, own), F32)],
            flags, behind, ahead, core, stats, name="rims",
        )
        late = size // 6
        cot_mine, cot_early, cot_late = call(
            cot_kernel, [(size + 4, breadth, own), (size + 4 - late, breadth, own), (late, breadth, own)],
            [], flags, cotangent, cot_inner, name="cot",
        )
        gate = (shares[2], halo_theirs, cot_early)
        shares[2], halo_theirs, cot_early = lax.optimization_barrier(gate)
        halo_got = place.across(halo_theirs)
        shares.append(place.flip(jnp.concatenate(shares, axis=0), bits[0]))
        first_weights = call(
            functools.partial(weights_kernel, steps=near, skip=False),
            kinds, [pltpu.VMEM((taps, own), F32)], flags, w_first, *shares,
            name="weights_first",
        )
        return stats, halo_mine, halo_got, cot_mine, cot_early, cot_late, shares, first_weights

    def block(steps, *operands):
        shapes = jax.eval_shape(steps, *operands)

        def nothing(*operands):
            return jax.tree.map(lambda leaf: jnp.zeros(leaf.shape, leaf.dtype), shapes)

        return lax.cond(edge_flip[0, 0] < 2, steps, nothing, *operands)

    rim_rows = 4 * breadth + 2 * (size + 8) + breadth + 8
    kinds = [jax.ShapeDtypeStruct((3, 3 * depth, depth), BF16)] * 4
    stats, halo_mine, halo_got, cot_mine, cot_early, cot_late, shares, first_weights = block(
        neighbours, stats, inner, to_prev, to_next, message
    )
    sea_count, batch_mean = stats[0], stats[1]
    batch_var = stats[2] / sea_count
    cot_early, got = lax.optimization_barrier((cot_early, got))
    cot_got = place.across(cot_early)

    small = [jax.ShapeDtypeStruct((depth, depth), BF16)] * 4
    second_weights = call(
        functools.partial(weights_kernel, steps=near, skip=True),
        kinds + small, [pltpu.VMEM((taps + depth, own), F32)], flags,
        w_second, *shares, w_skip,
        name="weights_second",
    )

    def buffers(tile):
        return [pltpu.VMEM(((tile + 2) * breadth, 3 * depth), BF16) for _ in range(4)]

    def pair(count, width, kind=F32):
        return [pltpu.VMEM((count, width), kind) for _ in range(2)]

    def edges(count):
        return [pltpu.VMEM((depth // LANES, count, LANES), F32) for _ in range(2)]

    def conv_scratch(tile):
        return buffers(tile) + pair(tile * breadth, depth)

    def first_conv(got, halo_got):
        return call(
            functools.partial(first_kernel, tile=9),
            [
                (size + 8, breadth, depth), (size + 8, depth), (size + 8, depth),
                (size + 6, breadth, depth), (size + 6, breadth, depth),
                (size + 6 + breadth, depth), (size + 6, depth),
            ],
            [pltpu.VMEM((breadth, depth), F32)] + conv_scratch(9),
            flags, marked, got, halo_mine, halo_got, *first_weights[:2], biases,
            name="first",
        )

    scaled, x_left, x_right, hidden, slope_first, to_prev, to_next = block(first_conv, got, halo_got)
    h_ahead, h_left = place.to_prev(to_prev), place.to_next(to_next)
    h_left, cot_got = lax.optimization_barrier((h_left, cot_got))
    cot_got = (cot_got, place.across(cot_late))
    out_own, out_send, slope_second = call(
        functools.partial(second_kernel, tile=13),
        [(size + 4, breadth, own), (size + 4, breadth, own), (size + 4, breadth, depth)],
        pair(size + 6, depth) + conv_scratch(13) + pair(13 * breadth, 2 * depth, BF16)
        + pair(13 * breadth, depth),
        flags, hidden, h_left, h_ahead, *second_weights[:2], biases, scaled, *second_weights[4:6],
        name="second",
    )
    out_send, _ = lax.optimization_barrier((out_send, cot_got[1]))
    out_got = place.across(out_send)

    rim_shapes = [(size + 2 + breadth, depth), (size + 2, depth)]
    upper, grad_second, to_next, to_prev = call(
        functools.partial(back_second_kernel, tile=13),
        [(size + 4, breadth, depth), (size + 4, breadth, depth)] + rim_shapes,
        conv_scratch(13) + edges(breadth),
        flags, cot_mine, cot_got, slope_second, *second_weights[2:4],
        name="back_second",
    )
    groups = place.groups()

    def weight_scratch(kinds, taps):
        turned = [pltpu.VMEM((kinds, depth, 12 * breadth), BF16) for _ in range(2)]
        return buffers(12) + turned + [pltpu.VMEM((taps, depth, depth), F32)]

    def second_weights_grad(to_next, to_prev, grad_second):
        behind, after = place.to_next(to_next), place.to_prev(to_prev)
        grads = call(
            functools.partial(weight_kernel, tile=12, first=False),
            [(9, own, depth)] * 2 + [(1, depth)],
            weight_scratch(2, 9) + pair(size + 6, depth),
            flags, hidden, h_left, h_ahead, grad_second,
            name="weight_second", paired=True,
        )
        return behind, after, *grads

    behind, after, keep, send, gb_second = block(
        second_weights_grad, to_next, to_prev, grad_second
    )
    out_got, send = lax.optimization_barrier((out_got, send))

    def first_weights_grad(keep, send, upper, behind, after):
        grads = call(
            functools.partial(weight_kernel, tile=12, first=True),
            [(10, own, depth)] * 2 + [(1, depth)] * 2 + [(size + 2, breadth, depth)],
            weight_scratch(4, 10),
            flags, scaled, x_left, x_right, upper, behind, after, slope_first, cot_mine, cot_got,
            name="weight_first", paired=True,
        )
        return place.flip(send, groups[0][0]), *grads

    gw_second = [keep]
    other, keep, send, gb_first, gb_skip, grad_first = block(
        first_weights_grad, keep, send, upper, behind, after
    )
    gw_second = [value.reshape(-1, depth) for value in (*gw_second, other)]

    def input_grad(part, *before):
        shapes = [(size // 2, breadth, own)] * 2
        shapes += rim_shapes if part else [(32, depth)] * 2 + [(breadth, depth)]
        scratch = conv_scratch(13) + pair(13 * breadth, 2 * depth, BF16) + edges(40)
        return call(
            functools.partial(back_first_kernel, tile=13, part=part),
            shapes, scratch + [pltpu.VMEM((26, breadth, depth), F32)],
            flags, grad_first, cot_mine, cot_got, *first_weights[2:4], *second_weights[6:8], *before,
            name="back_first_%d" % part,
        )

    def upper_half(send, grad_first, *gw_second):
        return place.shared(gw_second, groups[1]), place.flip(send, groups[0][0]), *input_grad(0)

    gw_second, other, own_upper, send_upper, *before = block(upper_half, send, grad_first, *gw_second)
    gw_first = [value.reshape(-1, depth) for value in (keep, other)]
    got_upper = place.across(send_upper)

    def lower_half(gw_second, keep, other, *before):
        for bits in groups[2:]:
            gw_second = place.shared((gw_second,), bits)
        return gw_second, place.shared((keep, other), groups[1]), *input_grad(1, *before)

    gw_second, gw_first, own_lower, send_lower, to_next, to_prev = block(
        lower_half, gw_second, *gw_first, *before
    )
    got_lower = place.across(send_lower)
    lower_own, lower_send, lower_got = (own_upper, own_lower), (send_upper, send_lower), (got_upper, got_lower)

    def after_products(gw_first, gw_second, to_next, to_prev, out_own, out_got):
        behind, after = place.to_next(to_next), place.to_prev(to_prev)
        for bits in groups[2:]:
            gw_first = place.shared((gw_first,), bits)
        gw_second = gw_second[:, :own] + place.across(gw_second[:, own:])
        output, = call_copy(join_kernel, (rows, breadth, own), flags, out_own, out_got)
        return behind, after, gw_first, gw_second, output

    gw_first, gw_second, got_upper = lax.optimization_barrier((gw_first, gw_second, got_upper))
    behind, after, gw_first, gw_second, output = block(
        after_products, gw_first, gw_second, to_next, to_prev, out_own, out_got
    )

    def last_sums(gw_second, gw_first, behind, after, lower_own, lower_send):
        adds = jnp.concatenate([behind, after], axis=0)
        adds_got = place.across(adds[:, own:])
        column = jnp.arange(breadth)[None, :, None]
        row = jnp.arange(size)[:, None, None]
        edge = jnp.where(place.strip == 0, 0, size - 1)
        at_pole = place.side == 0

        def with_rims(value, adds):
            last = size + 2 + breadth
            value = value + jnp.where(column == 0, adds[1 : size + 1, None], 0.0)
            value = value + jnp.where(column == breadth - 1, adds[last + 1 : last + 1 + size, None], 0.0)
            return value + jnp.where((row == edge) & at_pole, adds[None, size + 2 : last], 0.0)

        sea_weight = sea_mask.astype(F32)[:, :, None]
        own_weight = lax.dynamic_slice_in_dim(sea_weight, place.half * size, size, 0)
        source = scaled[4 : size + 4]
        parts = []
        for value, lanes in ((lower_own, slice(0, own)), (lower_send, slice(own, depth))):
            value = with_rims(jnp.concatenate(value, axis=0), adds[:, lanes])
            parts.append(
                jnp.stack(
                    [
                        jnp.sum(own_weight * value, axis=(0, 1)),
                        jnp.sum(source[:, :, lanes] * value, axis=(0, 1)),
                    ]
                )
            )
        zeros = jnp.zeros((3, depth), F32)
        sums = [gb_first, gb_second, gb_skip, jnp.concatenate(parts, axis=1), zeros]
        sums = place.summed(jnp.concatenate(sums, axis=0))

        def collected(grad):
            for bits in reversed(groups[1:]):
                grad = place.spread(grad, bits)
            grad = grad.reshape(-1, own, own)
            return grad, place.flip(grad, groups[0][0])

        gw_first, _ = lax.optimization_barrier((gw_first, got_lower))
        gw_first = gw_first[:, :own] + place.across(gw_first[:, own:])
        gw_second, gw_first, gw_skip = gather_call(flags, *collected(gw_second), *collected(gw_first))
        sums = sums[:, :own] + place.across(sums[:, own:])
        adds_own = adds[:, :own]
        grad_half = final_call(0, flags, marked, lower_own, adds_own, stats, sums)
        return gw_second, gw_skip, gw_first, sums, adds_got, grad_half

    gw_second, gw_skip, gw_first, sums, adds_got, grad_half = last_sums(
        gw_second, gw_first, behind, after, lower_own, lower_send
    )
    late = (sums, gw_first, gw_second, gw_skip, grad_half, lower_got, adds_got)
    sums, gw_first, gw_second, gw_skip, grad_half, lower_got, adds_got = lax.optimization_barrier(late)
    grad_features = final_call(1, flags, marked, lower_got, adds_got, stats, sums, grad_half)
    new_mean = (1.0 - MOMENTUM) * run_mean + MOMENTUM * batch_mean
    new_var = (1.0 - MOMENTUM) * run_var + MOMENTUM * batch_var * sea_count / (sea_count - 1.0)
    return (
        output,
        grad_features,
        gw_first.reshape(3, 3, depth, own),
        sums[0],
        gw_second.reshape(3, 3, depth, own),
        sums[1],
        gw_skip,
        sums[2],
        new_mean,
        new_var,
    )


def solution(mesh):
    field, kernel, vector = P("pix", None, "ch"), P(None, None, None, "ch"), P("ch")
    placed = (
        field, P("pix", None), P(), kernel, vector, kernel, vector, P(None, "ch"), vector,
        vector, vector, field,
    )
    return jax.shard_map(
        functools.partial(local, mesh),
        mesh=mesh,
        in_specs=placed,
        out_specs=(
            field, field, kernel, vector, kernel, vector, P(None, "ch"), vector, vector, vector,
        ),
        check_vma=False,
    )
```

```python
import functools

import jax
import jax.numpy as jnp
from jax import lax
from jax.experimental import pallas as pl
from jax.experimental.pallas import tpu as pltpu
from jax.sharding import PartitionSpec as P

EPSILON = 1e-05
MOMENTUM = 0.1
INV_ROOT_TWO_PI = 0.3989422804014327
SQRT_HALF = 0.7071067811865476
F32 = jnp.float32
BF16 = jnp.bfloat16
VMEM_LIMIT = 60 * 1024 * 1024
LARGE = 512 * 1024


def split(value):
    high = value.astype(BF16)
    return high, (value - high.astype(F32)).astype(BF16)


def dot_split(a_high, a_low, b_high, b_low):
    total = jnp.dot(a_high, b_high, preferred_element_type=F32)
    total = total + jnp.dot(a_high, b_low, preferred_element_type=F32)
    return total + jnp.dot(a_low, b_high, preferred_element_type=F32)


def gelu_and_slope(u):
    cdf = 0.5 * (1.0 + lax.erf(u * SQRT_HALF))
    return u * cdf, cdf + u * jnp.exp(-0.5 * u * u) * INV_ROOT_TWO_PI


AT_TOP, AT_BOTTOM, SIDE, HALF, FLIPPED, PIX = range(6)
NOT_SEA = 1e30
LANES = 128


def lane_parts(depth):
    return [slice(start, start + LANES) for start in range(0, depth, LANES)]


def put_row(buffers, block, read, left, right, breadth, depth):
    high, low = buffers
    column = lax.broadcasted_iota(jnp.int32, (breadth, 1), 0)
    rows = block_rows(block, breadth)
    for lanes in lane_parts(depth):
        value = read(lanes)
        shifts = (
            jnp.where(column == 0, left(lanes), pltpu.roll(value, 1, 0)),
            value,
            jnp.where(column == breadth - 1, right(lanes), pltpu.roll(value, breadth - 1, 0)),
        )
        for tap, piece in enumerate(shifts):
            place = slice(tap * depth + lanes.start, tap * depth + lanes.stop)
            high[rows, place], low[rows, place] = split(piece)


def conv_tile(buffers, w_high, w_low, total, tile, breadth):
    high, low = buffers
    value = None
    for row_tap in range(3):
        rows = slice(row_tap * breadth, (row_tap + tile) * breadth)
        part = dot_split(high[rows, :], low[rows, :], w_high[row_tap], w_low[row_tap])
        value = part if value is None else value + part
    total[...] = value


def block_rows(block, breadth):
    start = block * breadth
    return pl.ds(start if isinstance(start, int) else pl.multiple_of(start, breadth), breadth)


def pipeline(fills, multiply, finish, tiles, tile, store=lambda tile: None, more=lambda *step: None):
    def fill(step, slot, fresh):
        for count, lay in fills:
            for block in range(count):
                lay(step, slot, block)
        more(step, slot, fresh)

    def finish_all(step, slot):
        for block in range(tile):
            finish(step, slot, block)

    for count, lay in fills:
        pl.loop(0, count)(functools.partial(lay, 0, 0))
    more(0, 0, True)

    @pl.loop(0, (tiles + 1) // 2)
    def _(step):
        now = 2 * step
        fill(jnp.minimum(now + 1, tiles - 1), 1, now + 1 < tiles)
        multiply(0)
        finish_all(jnp.maximum(now - 1, 0), 1)
        fill(jnp.minimum(now + 2, tiles - 1), 0, now + 2 < tiles)
        multiply(1)
        finish_all(now, 0)

        @pl.when(step > 0)
        def _():
            store(now - 1)

        store(now)

    if tiles % 2 == 0:
        pl.loop(0, tile)(functools.partial(finish, tiles - 1, 1))
        store(tiles - 1)


def in_turn(fills, multiply, finish, tiles, tile):
    @pl.loop(0, tiles)
    def _(step):
        for count, lay in fills:
            pl.loop(0, count)(functools.partial(lay, step, 0))
        multiply(0)
        pl.loop(0, tile)(functools.partial(finish, step, 0))


def patch(flags, x, left, right, pole, top, bottom):
    breadth = x.shape[1]

    def put(at, edge):
        @pl.when(flags[FLIPPED] == 1)
        def _():
            for column in range(breadth):
                x[at, column : column + 1] = pole[breadth - 1 - column : breadth - column]

        @pl.when(flags[FLIPPED] == 0)
        def _():
            x[at] = pole[...]

        left[at : at + 1] = 0.5 * (x[at, 0:1] + left[edge : edge + 1])
        right[at : at + 1] = 0.5 * (x[at, breadth - 1 : breadth] + right[edge : edge + 1])

    @pl.when(flags[AT_TOP] == 1)
    def _():
        put(top, top + 1)

    @pl.when(flags[AT_BOTTOM] == 1)
    def _():
        put(bottom, bottom - 1)


def put_messages(flags, x, to_prev, to_next, first_row, last_row):
    rows, breadth = x.shape[0], x.shape[1]

    @pl.loop(0, rows)
    def _(row):
        to_prev[pl.ds(row, 1)] = x[row, 0:1]
        to_next[pl.ds(row, 1)] = x[row, breadth - 1 : breadth]

    to_prev[rows : rows + breadth] = x[jnp.where(flags[AT_BOTTOM] == 1, last_row, first_row)]


def first_kernel(
    traffic, flags, marked, got, halo_mine, halo_got, w_high, w_low, biases,
    scaled, x_left, x_right, hidden, slope, to_prev, to_next,
    pole, high0, low0, high1, low1, total0, total1, *, tile
):
    blocks, breadth, depth = scaled.shape
    own = depth // 2
    extra = blocks - got.shape[0]
    tail = halo_mine.shape[0] - 8
    start = flags[HALF] * (marked.shape[0] - got.shape[0])

    def normal(value, lanes):
        source = halo_mine if lanes.start == 0 else halo_got
        mean, inverse = source[tail : tail + 1], source[tail + 1 : tail + 2]
        return jnp.where(value > 0.1 * NOT_SEA, 0.0, (value - mean) * inverse)

    traffic.wait(0, 1)
    lower, upper = slice(0, own), slice(own, depth)
    main = jnp.where(flags[HALF] == 0, extra, 0)
    outer = jnp.where(flags[HALF] == 0, 0, blocks - extra)

    @pl.loop(0, got.shape[0])
    def _(row):
        scaled[main + row, :, lower] = normal(marked[start + row], lower)
        scaled[main + row, :, upper] = normal(got[row], upper)

    for row in range(extra):
        rows = slice(row * breadth, (row + 1) * breadth)
        scaled[outer + row, :, lower] = normal(halo_mine[rows], lower)
        scaled[outer + row, :, upper] = normal(halo_got[rows], upper)

    begin = extra * breadth
    for target, count in ((x_left, blocks), (x_right, blocks), (pole, breadth)):
        rows = slice(begin, begin + count)
        target[:, lower] = normal(halo_mine[rows], lower)
        target[:, upper] = normal(halo_got[rows], upper)
        begin = begin + count

    patch(flags, scaled, x_left, x_right, pole, 3, blocks - 4)
    traffic.store(0, 0, blocks)
    traffic.wait(4, 5)
    buffers, totals = ((high0, low0), (high1, low1)), (total0, total1)

    def fill(step, slot, block):
        row = jnp.minimum(step * tile + block, blocks - 1)
        put_row(
            buffers[slot], block, lambda lanes: scaled[row, :, lanes],
            lambda lanes: x_left[pl.ds(row, 1)][:, lanes], lambda lanes: x_right[pl.ds(row, 1)][:, lanes],
            breadth, depth,
        )

    def finish(step, slot, block):
        for lanes in lane_parts(depth):
            pre = totals[slot][block_rows(block, breadth), lanes] + biases[0:1, lanes]
            value, grad = gelu_and_slope(pre)
            hidden[step * tile + block, :, lanes] = value
            slope[step * tile + block, :, lanes] = grad

    def store(step):
        traffic.store(3, step * tile, tile)
        traffic.store(4, step * tile, tile)

    pipeline(
        [(tile + 2, fill)],
        lambda slot: conv_tile(buffers[slot], w_high, w_low, totals[slot], tile, breadth),
        finish, hidden.shape[0] // tile, tile, store,
    )
    put_messages(flags, hidden, to_prev, to_next, 3, blocks - 6)


def second_kernel(
    traffic, flags, x, left_in, ahead, w_high, w_low, biases, source, s_high, s_low,
    out_own, out_send, slope,
    left, right, high0, low0, high1, low1, total0, total1, skip0, skip1, sum0, sum1, *, tile
):
    blocks, breadth, depth = x.shape
    own = depth // 2
    left[...] = left_in[...]
    right[...] = ahead[:blocks]
    traffic.wait(0)
    patch(flags, x, left, right, ahead[blocks:], 2, blocks - 3)
    traffic.wait(3, 4, 6)
    buffers, totals, skips = ((high0, low0), (high1, low1)), (total0, total1), (skip0, skip1)
    sums = (sum0, sum1)

    def fill(step, slot, block):
        row = jnp.minimum(step * tile + block, blocks - 1)
        put_row(
            buffers[slot], block, lambda lanes: x[row, :, lanes],
            lambda lanes: left[pl.ds(row, 1)][:, lanes], lambda lanes: right[pl.ds(row, 1)][:, lanes],
            breadth, depth,
        )

    def fill_skip(step, slot, block):
        row = jnp.minimum(step * tile + block + 2, source.shape[0] - 1)
        rows = block_rows(block, breadth)
        for lanes in lane_parts(depth):
            place = slice(depth + lanes.start, depth + lanes.stop)
            skips[slot][rows, lanes], skips[slot][rows, place] = split(source[row, :, lanes])

    def multiply(slot):
        conv_tile(buffers[slot], w_high, w_low, totals[slot], tile, breadth)
        skip = skips[slot]
        sums[slot][...] = dot_split(skip[:, :depth], skip[:, depth:], s_high[...], s_low[...])

    def finish(step, slot, block):
        row = step * tile + block
        rows = block_rows(block, breadth)
        for lanes in lane_parts(depth):
            pre = totals[slot][rows, lanes] + biases[1:2, lanes]
            value, grad = gelu_and_slope(pre)
            slope[row, :, lanes] = grad
            value = value + sums[slot][rows, lanes] + biases[2:3, lanes]
            if lanes.stop <= own:
                out_own[row, :, lanes] = value
            else:
                out_send[row, :, lanes.start - own : lanes.stop - own] = value

    def store(step):
        for result in range(3):
            traffic.store(result, step * tile, tile)

    pipeline([(tile + 2, fill), (tile, fill_skip)], multiply, finish, slope.shape[0] // tile, tile, store)


def edge_products(edges, w_high, w_low, slot, count):
    depth = edges.shape[0] * LANES
    total = None
    for tap in range(3):
        rows = slice(slot * depth, (slot + 1) * depth)
        pieces = [edges[part, tap : tap + count] for part in range(edges.shape[0])]
        edge_high, edge_low = split(jnp.concatenate(pieces, axis=1))
        part = dot_split(edge_high, edge_low, w_high[tap, rows], w_low[tap, rows])
        total = part if total is None else total + part
    return total


def put_rims(flags, to_next, to_prev, first_rim, last_rim, top, bottom):
    count, breadth = to_prev.shape[0], top.shape[0]
    to_prev[...] = first_rim[:count]
    to_next[:count] = last_rim[:count]
    to_next[count:] = jnp.zeros((breadth, to_next.shape[1]), F32)
    column = lax.broadcasted_iota(jnp.int32, (breadth, 1), 0)

    def put(row, at, inner):
        corner_first, corner_last = 0.5 * first_rim[at : at + 1], 0.5 * last_rim[at : at + 1]
        to_prev[inner : inner + 1] += corner_first
        to_next[inner : inner + 1] += corner_last
        row = row[...] + jnp.where(column == 0, corner_first, 0.0)
        row = row + jnp.where(column == breadth - 1, corner_last, 0.0)

        @pl.when(flags[FLIPPED] == 0)
        def _():
            to_next[count:] = row

        @pl.when(flags[FLIPPED] == 1)
        def _():
            for k in range(breadth):
                to_next[count + k : count + k + 1] = row[breadth - 1 - k : breadth - k]

    @pl.when(flags[AT_TOP] == 1)
    def _():
        put(top, 0, 1)

    @pl.when(flags[AT_BOTTOM] == 1)
    def _():
        put(bottom, count - 1, count - 2)


def back_second_kernel(
    traffic, flags, cot_mine, cot_got, slope, w_high, w_low,
    out, grad, to_next, to_prev,
    high0, low0, high1, low1, total0, total1, edge_first, edge_last, *, tile
):
    blocks, breadth, depth = slope.shape
    own = depth // 2
    traffic.wait(0, 1, 2)
    edge_first[...] = jnp.zeros_like(edge_first)
    edge_last[...] = jnp.zeros_like(edge_last)
    buffers, totals = ((high0, low0), (high1, low1)), (total0, total1)

    def fill(step, slot, block):
        row = jnp.minimum(step * tile + block, blocks - 1)
        outside = (flags[AT_TOP] == 1) & (row < 2) | (flags[AT_BOTTOM] == 1) & (row >= blocks - 2)
        inside = jnp.where(outside, 0.0, 1.0)

        def read(lanes):
            cot = cot_mine[row] if lanes.stop <= own else cot_got[row]
            value = cot * slope[row, :, lanes] * inside
            grad[row, :, lanes] = value
            edge_first[lanes.start // LANES, pl.ds(row, 1)] = value[0:1]
            edge_last[lanes.start // LANES, pl.ds(row, 1)] = value[breadth - 1 : breadth]
            return value

        put_row(buffers[slot], block, read, lambda lanes: 0.0, lambda lanes: 0.0, breadth, depth)

    def finish(step, slot, block):
        out[step * tile + block] = totals[slot][block_rows(block, breadth), :]

    traffic.wait(3, 4)
    pipeline(
        [(tile + 2, fill)],
        lambda slot: conv_tile(buffers[slot], w_high, w_low, totals[slot], tile, breadth),
        finish, out.shape[0] // tile, tile, lambda step: traffic.store(0, step * tile, tile),
    )
    traffic.store(1, 0, blocks)
    rows = blocks + 4
    first_rim = edge_products(edge_first, w_high, w_low, 2, rows)
    last_rim = edge_products(edge_last, w_high, w_low, 0, rows)
    put_rims(flags, to_next, to_prev, first_rim, last_rim, out[0], out[blocks - 3])


def back_first_kernel(
    traffic, flags, grad, cot_mine, cot_got, w_high, w_low, s_high, s_low, *rest, tile, part
):
    if part:
        before_first, before_last, before_top, out_own, out_send, to_next, to_prev = rest[:7]
    else:
        out_own, out_send, rim_first, rim_last, top = rest[:5]
    high0, low0, high1, low1, total0, total1, skip0, skip1, edge_first, edge_last, result = rest[-11:]
    count, breadth, depth = grad.shape
    own = depth // 2
    begin = part * ((count - 2) // 2)
    blocks = out_own.shape[0] + 2
    edge_first[...] = jnp.zeros_like(edge_first)
    edge_last[...] = jnp.zeros_like(edge_last)
    buffers, totals, skips = ((high0, low0), (high1, low1)), (total0, total1), (skip0, skip1)
    traffic.wait(0, 1, 2)

    def fill(step, slot, block):
        at = step * tile + block
        row = begin + at - 1
        inside = jnp.where((row >= 0) & (row < count), 1.0, 0.0)
        row = jnp.clip(row, 0, count - 1)

        def read(lanes):
            value = grad[row, :, lanes] * inside
            edge_first[lanes.start // LANES, pl.ds(at, 1)] = value[0:1]
            edge_last[lanes.start // LANES, pl.ds(at, 1)] = value[breadth - 1 : breadth]
            return value

        put_row(buffers[slot], block, read, lambda lanes: 0.0, lambda lanes: 0.0, breadth, depth)

    def fill_skip(step, slot, block):
        row = begin + step * tile + block
        inside = jnp.where((row >= 1) & (row < count - 1), 1.0, 0.0)
        row = jnp.clip(row + 1, 0, cot_mine.shape[0] - 1)
        rows = block_rows(block, breadth)
        for lanes in lane_parts(depth):
            cot = cot_mine[row] if lanes.stop <= own else cot_got[row]
            place = slice(depth + lanes.start, depth + lanes.stop)
            skips[slot][rows, lanes], skips[slot][rows, place] = split(cot * inside)

    def multiply(slot):
        conv_tile(buffers[slot], w_high, w_low, totals[slot], tile, breadth)
        skip = skips[slot]
        totals[slot][...] += dot_split(skip[:, :depth], skip[:, depth:], s_high[...], s_low[...])

    def finish(step, slot, block):
        result[step * tile + block] = totals[slot][block_rows(block, breadth), :]

    traffic.wait(3, 4)
    in_turn([(tile + 2, fill), (tile, fill_skip)], multiply, finish, result.shape[0] // tile, tile)

    @pl.loop(0, out_own.shape[0])
    def _(row):
        out_own[row] = result[row + 1, :, :own]
        out_send[row] = result[row + 1, :, own:]

    traffic.store(0 if part == 0 else 0, 0, out_own.shape[0])
    traffic.store(1, 0, out_own.shape[0])
    rows = blocks + 6
    first_rim = edge_products(edge_first, w_high, w_low, 2, rows)
    last_rim = edge_products(edge_last, w_high, w_low, 0, rows)
    if part == 0:
        rim_first[...], rim_last[...] = first_rim, last_rim
        top[...] = result[0]
    else:
        joined = [
            jnp.concatenate([before[: begin + 1], now[1 : begin + 2]], axis=0)
            for before, now in ((before_first, first_rim), (before_last, last_rim))
        ]
        put_rims(flags, to_next, to_prev, *joined, before_top[...], result[blocks - 1])


def weight_kernel(traffic, flags, x, *rest, tile, first):
    if first:
        left, right, upper, behind, after, slope, cot_mine, cot_got = rest[:8]
        parts, _, total, total_skip, grad_out = rest[8:13]
        rest, begin = rest[13:], 3
    else:
        left_in, ahead, grad = rest[:3]
        parts, _, total = rest[3:6]
        left, right = rest[-2:]
        rest, begin = rest[6:-2], 2
    high0, low0, high1, low1, t0, t1, acc = rest[:7]
    buffers, turned = ((high0, low0), (high1, low1)), (t0, t1)
    breadth, depth = x.shape[1:]
    own = depth // 2
    taps = acc.shape[0]
    rows = x.shape[0] - 2 * begin - 2
    pixels = tile * breadth
    traffic.wait(0)
    if first:
        count = rows + 2
        column = lax.broadcasted_iota(jnp.int32, (breadth, 1), 0)
        traffic.wait(3, 6, 7, 8)
        total_skip[...] = jnp.zeros_like(total_skip)

        def read(row, lanes):
            at = row + 1
            edge = (flags[AT_TOP] == 1) & (row == 0) | (flags[AT_BOTTOM] == 1) & (row == rows - 1)
            value = upper[at, :, lanes] + jnp.where(column == 0, behind[pl.ds(at, 1)][:, lanes], 0.0)
            value = value + jnp.where(column == breadth - 1, after[pl.ds(at, 1)][:, lanes], 0.0)
            value = value + behind[count : count + breadth, lanes] * jnp.where(edge, 1.0, 0.0)
            value = value * slope[at + 2, :, lanes]
            grad_out[at, :, lanes] = value
            return value

        for row, pole in ((-1, AT_TOP), (rows, AT_BOTTOM)):
            for lanes in lane_parts(depth):
                value = read(row, lanes)
                grad_out[row + 1, :, lanes] = value * jnp.where(flags[pole] == 1, 0.0, 1.0)
    else:
        left[...] = left_in[...]
        right[...] = ahead[: x.shape[0]]
        patch(flags, x, left, right, ahead[x.shape[0] :], 2, x.shape[0] - 3)
        traffic.wait(3)

        def read(row, lanes):
            return grad[row + 2, :, lanes]

    acc[...] = jnp.zeros_like(acc)
    total[...] = jnp.zeros_like(total)

    def turn(slot, place, lanes, value):
        value_high, value_low = split(value.T)
        turned[slot][place, lanes] = value_high
        turned[slot][place + 1, lanes] = value_low

    def fill(step, slot, block):
        row = step * tile + block + begin
        put_row(
            buffers[slot], block, lambda lanes: x[row, :, lanes],
            lambda lanes: left[pl.ds(row, 1)][:, lanes], lambda lanes: right[pl.ds(row, 1)][:, lanes],
            breadth, depth,
        )

    def fill_turned(step, slot, fresh):
        once = jnp.where(fresh, 1.0, 0.0)
        for lanes in lane_parts(depth):
            value = jnp.concatenate([read(step * tile + block, lanes) for block in range(tile)], axis=0)
            total[:, lanes] += jnp.sum(value, axis=0, keepdims=True) * once
            turn(slot, 0, lanes, value)
            if first:
                source = cot_mine if lanes.stop <= own else cot_got
                value = source[pl.ds(step * tile + 2, tile)].reshape(pixels, LANES)
                total_skip[:, lanes] += jnp.sum(value, axis=0, keepdims=True) * once
                turn(slot, 2, lanes, value)

    def multiply(slot):
        high, low = buffers[slot]
        for tap in range(taps):
            row_tap, column_tap, place = (tap // 3, tap % 3, 0) if tap < 9 else (1, 1, 2)
            window = slice(row_tap * breadth, row_tap * breadth + pixels)
            lanes = slice(column_tap * depth, (column_tap + 1) * depth)
            acc[tap] += dot_split(
                turned[slot][place], turned[slot][place + 1], high[window, lanes], low[window, lanes]
            )

    pipeline([(tile + 2, fill)], multiply, lambda *block: None, rows // tile, 0, more=fill_turned)
    half = depth // 2
    mine = (flags[SIDE] ^ flags[PIX]) & 1
    for tap in range(taps):
        value = acc[tap].T
        parts[mine, tap] = value[:half]
        parts[1 - mine, tap] = value[half:]


def weights_kernel(traffic, flags, mine, *rest, steps, skip):
    shares, rest = rest[: steps + 1], rest[steps + 1 :]
    if skip:
        mine_skip, f_high, f_low, b_high, b_low, s_high, s_low, sb_high, sb_low, other = rest
    else:
        f_high, f_low, b_high, b_low, other = rest
    own = mine.shape[1]
    depth = 2 * own
    taps = mine.shape[0]
    count = 1 << steps
    traffic.wait(*traffic.ins)
    share, share_skip = taps // count, depth // count
    unit = shares[0].shape[0]
    begin = share if skip else 0
    for piece in range(count):
        away = sum(1 << (steps - 1 - step) for step in range(steps) if piece >> step & 1)
        index = (flags[PIX] & (count - 1)) ^ away
        level = piece.bit_length()
        source = shares[level]
        at = (piece - (1 << (level - 1)) if level else 0) * unit + begin
        other[pl.ds(pl.multiple_of(index * share, 8), share)] = source[at : at + share]
        if skip:
            start = pl.multiple_of(taps + index * share_skip, 8)
            other[pl.ds(start, share_skip)] = source[at + share : at + share + share_skip]
    def both(first, second):
        return jnp.concatenate([first, second], axis=1)

    def one_tap(row_tap, column_tap):
        tap, back_row, back_column = row_tap * 3 + column_tap, 2 - row_tap, 2 - column_tap
        for part in range(2):
            at = pl.multiple_of(tap * depth + jnp.where(flags[SIDE] == part, 0, own), own)
            value = both(mine[pl.ds(at, own)], other[pl.ds(at, own)])
            value_high, value_low = split(value)
            place = pl.ds(pl.multiple_of(column_tap * depth + part * own, own), own)
            f_high[row_tap, place] = value_high
            f_low[row_tap, place] = value_low
            turned_high, turned_low = split(value.T)
            place = pl.ds(pl.multiple_of(back_column * depth, depth), depth)
            lanes = slice(part * own, (part + 1) * own)
            b_high[back_row, place, lanes] = turned_high
            b_low[back_row, place, lanes] = turned_low

    for row_tap in range(3):
        pl.loop(0, 3)(functools.partial(one_tap, row_tap))
        for result in range(4):
            traffic.store(result, row_tap if result < 2 else 2 - row_tap, 1)

    if skip:
        for part in range(2):
            at = pl.multiple_of(jnp.where(flags[SIDE] == part, 0, own), own)
            value = both(mine_skip[pl.ds(at, own)], other[pl.ds(pl.multiple_of(taps + at, own), own)])
            lanes = slice(part * own, (part + 1) * own)
            s_high[lanes], s_low[lanes] = split(value)
            sb_high[:, lanes], sb_low[:, lanes] = split(value.T)


def pre_kernel(traffic, flags, features, mask, marked, theirs, stats, inner, to_prev, to_next):
    rows, breadth, own = features.shape
    length = theirs.shape[0]
    traffic.wait(0)
    start = (1 - flags[HALF]) * (rows - length)
    turned = mask[...].astype(F32)
    turned = jnp.concatenate([turned, jnp.zeros((breadth, 128 - rows), F32)], axis=1)
    none = jnp.zeros((8, own), F32)

    def fold(v):
        return jnp.sum(v.reshape(breadth // 8, 8, own), axis=0)

    def first(step, carry):
        count, total = carry
        base = step * 8
        sea_of = pltpu.roll(turned, 128 - base, 1)
        for k in range(8):
            row = base + k
            sea = jnp.broadcast_to(sea_of[:, k : k + 1], (breadth, own))
            value = features[row]
            land = jnp.where(sea > 0.5, value, NOT_SEA)
            marked[row] = land
            to_prev[pl.ds(row, 1)] = land[0:1]
            to_next[pl.ds(row, 1)] = land[breadth - 1 : breadth]
            count, total = count + fold(sea), total + fold(value * sea)
        return count, total

    count, total = lax.fori_loop(0, rows // 8, first, (none, none))
    count = jnp.sum(count, axis=0, keepdims=True)
    mean = jnp.sum(total, axis=0, keepdims=True) / jnp.maximum(count, 1.0)

    def second(step, squares):
        for k in range(8):
            value = marked[step * 8 + k]
            value = jnp.where(value > 0.1 * NOT_SEA, 0.0, value - mean)
            squares = squares + fold(value * value)
        return squares

    @pl.loop(0, length // 4)
    def _(step):
        theirs[pl.ds(step * 4, 4)] = marked[pl.ds(start + step * 4, 4)]

    traffic.store(1, 0, length)
    traffic.store(0, 0, rows)
    squares = lax.fori_loop(0, rows // 8, second, none)

    stats[...] = jnp.zeros_like(stats)
    stats[0:1] = count
    stats[1:2] = mean
    stats[2:3] = jnp.sum(squares, axis=0, keepdims=True)
    strip = flags[SIDE] ^ flags[HALF]
    to_prev[rows:] = marked[strip * (rows - 1)]
    inner[...] = marked[pl.ds((1 - strip) * (rows - inner.shape[0]), inner.shape[0])]


def cot_kernel(traffic, flags, cot, extra, mine, early, late):
    rows, more, count = cot.shape[0], extra.shape[0], mine.shape[0]
    traffic.wait(0)

    def put(target, begin, half):
        length = target.shape[0]

        @pl.loop(0, length)
        def _(row):
            target[row] = cot[jnp.clip(begin + row - more + half * (rows // 2), 0, rows - 1)]

        if begin == 0:

            @pl.when(half == 0)
            def _():
                target[:more] = extra[...]

        if begin + length == count:

            @pl.when(half == 1)
            def _():
                target[length - more :] = extra[...]

    put(early, 0, 1 - flags[HALF])
    put(late, early.shape[0], 1 - flags[HALF])
    put(mine, 0, flags[HALF])


def rims_kernel(traffic, flags, behind, ahead, core, stats, mine, theirs, wide):
    rows, own = behind.shape
    breadth = ahead.shape[0] - rows
    extra = (core.shape[0]) // (breadth + 2)
    length = rows // 2 + 2 * extra
    inner = extra * breadth
    at = inner
    for target in (mine, theirs):
        target[:inner] = core[:inner]
    for source, start in ((behind, inner + extra), (ahead, inner)):
        wide[:extra] = core[start : start + extra]
        wide[extra : extra + rows] = source[:rows]
        wide[extra + rows :] = core[start : start + extra]
        for target, half in ((mine, flags[HALF]), (theirs, 1 - flags[HALF])):
            target[at : at + length] = wide[pl.ds(pl.multiple_of(half * (rows // 2), 8), length)]
        at = at + length
    count, mean, squares = stats[0:1], stats[1:2], stats[2:3]
    inverse = lax.rsqrt(squares / count + EPSILON)
    for target in (mine, theirs):
        target[at : at + breadth] = ahead[rows:]
        target[at + breadth :] = jnp.zeros((8, own), F32)
        target[at + breadth : at + breadth + 1] = mean
        target[at + breadth + 1 : at + breadth + 2] = inverse


def gather_kernel(flags, second_mine, second_other, first_mine, first_other, second, first, skip, sems):
    half = second_mine.shape[1]
    here = (flags[PIX] & 1) * half
    copies = []
    for place, (mine, start) in enumerate(
        (
            (second_mine, here), (second_other, half - here),
            (first_mine, here), (first_other, half - here),
        )
    ):
        rows = pl.ds(pl.multiple_of(start, half), half)
        target = second if place < 2 else first
        copies.append(pltpu.make_async_copy(mine.at[pl.ds(0, 9)], target.at[:, rows], sems.at[place]))
        if place >= 2:
            copies.append(pltpu.make_async_copy(mine.at[9], skip.at[rows], sems.at[place + 2]))
    for copy in copies:
        copy.start()
    for copy in copies:
        copy.wait()


def gather_call(flags, *operands):
    anywhere, whole = pl.BlockSpec(memory_space=pl.ANY), pl.BlockSpec(memory_space=pltpu.VMEM)
    half, own = operands[0].shape[1:]
    shapes = [(9, 2 * half, own), (9, 2 * half, own), (2 * half, own)]
    return pl.pallas_call(
        gather_kernel,
        out_shape=[jax.ShapeDtypeStruct(shape, F32) for shape in shapes],
        in_specs=[pl.BlockSpec(memory_space=pltpu.SMEM)] + [whole] * 4,
        out_specs=[anywhere] * 3,
        scratch_shapes=[pltpu.SemaphoreType.DMA((6,))],
        compiler_params=pltpu.CompilerParams(vmem_limit_bytes=VMEM_LIMIT),
        cost_estimate=pl.CostEstimate(flops=0, bytes_accessed=12_000_000, transcendentals=0),
        name="gather",
    )(flags, *operands)


def final_kernel(flags, marked, lower_upper, lower_lower, rims, stats, sums, *rest, other, parts):
    out, source, result, in_sems, out_sems = rest[-5:]
    rows, breadth, own = marked.shape
    size = rows // 2
    step = size // parts
    last = size + 2 + breadth
    count, mean = stats[0:1], stats[1:2]
    inverse = lax.rsqrt(stats[2:3] / count + EPSILON)
    first_mean, second_mean = sums[3:4] / count, sums[4:5] / count
    column = lax.broadcasted_iota(jnp.int32, (breadth, 1), 0)
    strip = flags[SIDE] ^ flags[HALF]
    edge = strip * (size - 1)
    half = 1 - flags[HALF] if other else flags[HALF]
    at_pole = flags[SIDE] == (1 if other else 0)

    def fetch(part):
        rows = pl.ds(half * size + part * step, step)
        return pltpu.make_async_copy(marked.at[rows], source.at[pl.ds(part * step, step)], in_sems.at[part])

    def store(part):
        rows = pl.ds(half * size + part * step, step)
        return pltpu.make_async_copy(result.at[pl.ds(part * step, step)], out.at[rows], out_sems.at[part])

    for part in range(parts):
        fetch(part).start()
    for part in range(parts):
        fetch(part).wait()

        lower = lower_upper if part < parts // 2 else lower_lower

        @pl.loop(part * step, (part + 1) * step)
        def _(row):
            value = lower[row % (size // 2)] + jnp.where(column == 0, rims[pl.ds(row + 1, 1)], 0.0)
            value = value + jnp.where(column == breadth - 1, rims[pl.ds(row + last + 1, 1)], 0.0)
            at_edge = jnp.where((row == edge) & at_pole, 1.0, 0.0)
            value = value + rims[size + 2 : last] * at_edge
            normed = (source[row] - mean) * inverse
            value = inverse * (value - first_mean - normed * second_mean)
            result[row] = jnp.where(source[row] > 0.1 * NOT_SEA, 0.0, value)

        store(part).start()
    for part in range(parts):
        store(part).wait()


def final_call(other, flags, marked, lower, rims, stats, sums, before=None):
    anywhere, whole = pl.BlockSpec(memory_space=pl.ANY), pl.BlockSpec(memory_space=pltpu.VMEM)
    parts = 4
    operands = [flags, marked, *lower, rims, stats, sums] + ([before] if other else [])
    half = pltpu.VMEM((marked.shape[0] // 2,) + marked.shape[1:], F32)
    return pl.pallas_call(
        functools.partial(final_kernel, other=other, parts=parts),
        out_shape=jax.ShapeDtypeStruct(marked.shape, F32),
        in_specs=[pl.BlockSpec(memory_space=pltpu.SMEM), anywhere] + [whole] * 5 + [anywhere] * other,
        out_specs=anywhere,
        scratch_shapes=[half, half, pltpu.SemaphoreType.DMA((parts,)), pltpu.SemaphoreType.DMA((parts,))],
        input_output_aliases={7: 0} if other else {},
        compiler_params=pltpu.CompilerParams(vmem_limit_bytes=VMEM_LIMIT),
        cost_estimate=pl.CostEstimate(flops=0, bytes_accessed=4 * marked.size * 3, transcendentals=0),
        name="final_got" if other else "final_own",
    )(*operands)


def join_kernel(flags, mine, theirs, out, sems):
    size = out.shape[0] // 2
    skip = (mine.shape[0] - size) // 2
    copies = []
    for place, source in enumerate((mine, theirs)):
        half = flags[HALF] if place == 0 else 1 - flags[HALF]
        target = out.at[pl.ds(half * size, size)]
        copies.append(pltpu.make_async_copy(source.at[pl.ds(skip, size)], target, sems.at[place]))
    for copy in copies:
        copy.start()
    for copy in copies:
        copy.wait()


def call_copy(kernel, shape, flags, *operands):
    anywhere = pl.BlockSpec(memory_space=pl.ANY)
    return pl.pallas_call(
        kernel,
        out_shape=[jax.ShapeDtypeStruct(shape, F32)],
        in_specs=[pl.BlockSpec(memory_space=pltpu.SMEM)]
        + [pl.BlockSpec(memory_space=pltpu.VMEM)] * len(operands),
        out_specs=[anywhere],
        scratch_shapes=[pltpu.SemaphoreType.DMA((len(operands),))],
        compiler_params=pltpu.CompilerParams(vmem_limit_bytes=VMEM_LIMIT),
        cost_estimate=pl.CostEstimate(flops=0, bytes_accessed=0, transcendentals=0),
        name="join",
    )(flags, *operands)


class Traffic:
    def __init__(self, ins, outs):
        self.ins, self.outs, self.parts = ins, outs, {}
        for copies in ins.values():
            for copy in copies:
                copy.start()

    def wait(self, *places):
        for place in places:
            for copy in self.ins.pop(place):
                copy.wait()

    def store(self, place, start, count):
        source, target, sem = self.outs[place]
        rows = pl.ds(start, count)
        pltpu.make_async_copy(source.at[rows], target.at[rows], sem).start()
        self.parts[place] = True

    def finish(self):
        for place in self.outs:
            if place not in self.parts:
                pltpu.make_async_copy(*self.outs[place]).start()
        for place in self.outs:
            pltpu.make_async_copy(*self.outs[place]).wait()


def call(kernel, shapes, scratch, flags, *operands, name=None, paired=False):
    shapes = [s if isinstance(s, jax.ShapeDtypeStruct) else jax.ShapeDtypeStruct(s, F32) for s in shapes]

    operands = [operand if isinstance(operand, tuple) else (operand,) for operand in operands]
    wholes = [
        jax.ShapeDtypeStruct((sum(part.shape[0] for part in parts),) + parts[0].shape[1:], parts[0].dtype)
        for parts in operands
    ]
    counts = [len(parts) for parts in operands]
    operands = [part for parts in operands for part in parts]

    def large(a):
        return a.size * a.dtype.itemsize >= LARGE

    inside, outside = [large(a) for a in wholes], [large(a) for a in shapes]
    split_up = [is_large for is_large, count in zip(inside, counts) for _ in range(count)]
    buffers = [pltpu.VMEM(a.shape, a.dtype) for a in wholes + shapes[2 * paired :] if large(a)]
    if paired:
        buffers.append(pltpu.VMEM((2,) + shapes[0].shape, F32))
    sems = [pltpu.SemaphoreType.DMA((max(1, sum(group)),)) for group in (split_up, outside)]
    anywhere, whole = pl.BlockSpec(memory_space=pl.ANY), pl.BlockSpec(memory_space=pltpu.VMEM)

    def body(flags, *refs):
        refs = list(refs)
        given = len(operands) + len(shapes)
        rest, (in_sems, out_sems) = refs[given : len(refs) - 2], refs[-2:]
        held, extra = rest[: len(buffers)], rest[len(buffers) :]
        ins, outs, seen, sources, started = {}, {}, [], refs[: len(operands)], 0
        for place, is_large in enumerate(inside):
            parts = [sources.pop(0) for _ in range(counts[place])]
            if not is_large:
                seen.append(parts[0])
                continue
            buffer, row = held.pop(0), 0
            ins[place] = []
            for part in parts:
                target = buffer.at[pl.ds(row, part.shape[0])] if len(parts) > 1 else buffer
                ins[place].append(pltpu.make_async_copy(part, target, in_sems.at[started]))
                row, started = row + part.shape[0], started + 1
            seen.append(buffer)
        for place, is_large in enumerate(outside):
            ref = refs[len(operands) + place]
            if paired and place < 2:
                outs[place] = (held[-1].at[place], ref, out_sems.at[len(outs)])
                seen.append(held[-1])
            elif is_large:
                buffer = held.pop(0)
                outs[place] = (buffer, ref, out_sems.at[len(outs)])
                seen.append(buffer)
            else:
                seen.append(ref)
        traffic = Traffic(ins, outs)
        kernel(traffic, flags, *seen, *extra)
        assert not traffic.ins
        traffic.finish()

    return pl.pallas_call(
        body,
        out_shape=shapes,
        in_specs=[pl.BlockSpec(memory_space=pltpu.SMEM)] + [anywhere if k else whole for k in split_up],
        out_specs=[anywhere if k else whole for k in outside],
        scratch_shapes=buffers + list(scratch) + sems,
        compiler_params=pltpu.CompilerParams(vmem_limit_bytes=VMEM_LIMIT),
        cost_estimate=pl.CostEstimate(flops=0, bytes_accessed=0, transcendentals=0),
        name=name,
    )(flags, *operands)


class Place:
    def __init__(self, mesh, rows, breadth):
        self.count = mesh.shape["pix"]
        self.strips = 3 * breadth // rows
        assert mesh.shape["ch"] == 2 and self.strips == 2
        self.pix = lax.axis_index("pix")
        self.side = lax.axis_index("ch")
        self.ribbon = self.pix // self.strips % 4
        self.strip = self.pix % self.strips
        self.half = self.side ^ self.strip
        self.at_top = (self.side == 0) & (self.strip == 0)
        self.at_bottom = (self.side == 0) & (self.strip == 1)

    def ribbon_pairs(self, offset):
        pairs = []
        for index in range(self.count):
            sample, strip = index // (4 * self.strips), index % self.strips
            ribbon = (index // self.strips + offset) % 4
            pairs.append((index, (sample * 4 + ribbon) * self.strips + strip))
        return pairs

    def to_next(self, value):
        return lax.ppermute(value, "pix", self.ribbon_pairs(1))

    def to_prev(self, value):
        return lax.ppermute(value, "pix", self.ribbon_pairs(-1))

    def across(self, value):
        return lax.ppermute(value, "ch", [(0, 1), (1, 0)])

    def flip(self, value, bit):
        return lax.ppermute(value, "pix", [(i, i ^ bit) for i in range(self.count)])

    def bits(self):
        return [1 << step for step in range(self.count.bit_length() - 1)]

    def ordered(self, mine, theirs, bit):
        upper = (self.pix & bit) != 0
        return jnp.where(upper, theirs, mine), jnp.where(upper, mine, theirs)

    def near(self):
        return self.bits()[:3]

    def members(self, bits):
        out = []
        for other in range(1, 1 << len(bits)):
            mask = sum(bit for step, bit in enumerate(bits) if other >> step & 1)
            out.append((other, [(i, i ^ mask) for i in range(self.count)]))
        return out

    def number(self, bits):
        total = 0
        for step, bit in enumerate(bits):
            total = total + (((self.pix & bit) != 0).astype(jnp.int32) << step)
        return total

    def shared(self, values, bits):
        me, length = self.number(bits), values[0].shape[0] >> len(bits)

        def share(number):
            pieces = [lax.dynamic_slice_in_dim(value, number * length, length, 0) for value in values]
            return functools.reduce(jnp.add, pieces)

        total = share(me)
        parts = []
        for other, pairs in self.members(bits):
            piece = share(me ^ other)
            parts.append(lax.ppermute(piece, "pix", pairs))
        for part in parts:
            total = total + part
        return total

    def spread(self, value, bits):
        parts = [value] + [lax.ppermute(value, "pix", pairs) for _, pairs in self.members(bits)]
        for step, bit in enumerate(bits):
            upper = (self.pix & bit) != 0
            parts = [
                jnp.where(upper, parts[k ^ (1 << step)], parts[k]) for k in range(len(parts))
            ]
        return jnp.concatenate(parts, axis=0)

    def groups(self):
        bits = self.bits()
        rest = [bits[k : k + 2] for k in range(2, len(bits), 2)]
        return [bits[:1], bits[1:2]] + rest

    def summed(self, value):
        for bit in self.bits():
            first, second = self.ordered(value, self.flip(value, bit), bit)
            value = first + second
        return value

    def part(self, value, half, start, length):
        return lax.dynamic_slice_in_dim(value, half * start, length, 0)

    def join_rows(self, mine, theirs):
        return jnp.where(
            self.half == 0,
            jnp.concatenate([mine, theirs], axis=0),
            jnp.concatenate([theirs, mine], axis=0),
        )

    def inner_rows(self, value, extra):
        edge = jnp.where(self.strip == 0, value[-extra:], value[:extra])
        return self.flip(edge, 1)


def merged_stats(place, state):
    for bit in place.bits():
        first, second = place.ordered(state, place.flip(state, bit), bit)
        total = first[0] + second[0]
        safe = jnp.maximum(total, 1.0)
        step = second[1] - first[1]
        state = jnp.stack(
            [
                total,
                (first[0] * first[1] + second[0] * second[1]) / safe,
                first[2] + second[2] + step * step * (first[0] * second[0] / safe),
            ]
            + [total] * 5
        )
    return state


def local(
    mesh, features, sea_mask, edge_flip, w_first, b_first, w_second, b_second, w_skip, b_skip,
    run_mean, run_var, cotangent,
):
    rows, breadth, own = features.shape
    place = Place(mesh, rows, breadth)
    size, depth = rows // 2, 2 * own
    taps = 9 * depth
    flip_row = jnp.sum(jnp.where((jnp.arange(4) == place.ribbon)[:, None], edge_flip, 0), axis=0)
    flipped = jnp.where(place.strip == 0, flip_row[0], flip_row[1]) == 1
    flags = jnp.stack(
        [
            jnp.where(flag, 1, 0).astype(jnp.int32)
            for flag in (place.at_top, place.at_bottom, place.side == 1, place.half == 1, flipped)
        ]
        + [place.pix.astype(jnp.int32)]
    )

    w_first, w_second = w_first.reshape(taps, own), w_second.reshape(taps, own)
    near = len(place.near())
    share, share_skip, number = taps >> near, depth >> near, place.number(place.near())
    biases = jnp.stack([b_first, b_second, b_skip])
    message = jnp.concatenate(
        [
            lax.dynamic_slice_in_dim(w_first, number * share, share, 0),
            lax.dynamic_slice_in_dim(w_second, number * share, share, 0),
            lax.dynamic_slice_in_dim(w_skip, number * share_skip, share_skip, 0),
            jnp.pad(biases, ((0, 5), (0, 0))),
        ]
    )
    features, message = lax.optimization_barrier((features, message))
    message = place.across(message)
    marked, theirs, stats, inner, to_prev, to_next = call(
        pre_kernel,
        [
            (rows, breadth, own), (size + 4, breadth, own), (8, own), (4, breadth, own),
            (rows + breadth, own), (rows, own),
        ],
        [], flags, features, sea_mask.T, name="pre",
    )
    theirs, message = lax.optimization_barrier((theirs, message))
    got = place.across(theirs)
    biases = jnp.concatenate([biases, message[2 * share + share_skip :][:3]], axis=1)
    cot_inner = place.inner_rows(cotangent, 2)

    def neighbours(stats, inner, to_prev, to_next, message):
        mine = message[: 2 * share + share_skip]
        bits = place.near()
        ahead, behind = place.to_prev(to_prev), place.to_next(to_next)
        shares = [mine, place.flip(mine, bits[2])]
        shares[1], ahead, behind = lax.optimization_barrier((shares[1], ahead, behind))
        shares.append(place.flip(jnp.concatenate(shares, axis=0), bits[1]))

        def inner_part(value):
            return jnp.where(place.strip == 0, value[rows - 4 : rows], value[:4])

        core = jnp.concatenate(
            [inner.reshape(-1, own), inner_part(ahead), inner_part(behind)], axis=0
        )
        core = place.flip(core, 1)
        stats = merged_stats(place, stats)
        halo_mine, halo_theirs = call(
            rims_kernel, [(rim_rows, own)] * 2, [pltpu.VMEM((rows + 8, own), F32)],
            flags, behind, ahead, core, stats, name="rims",
        )
        late = size // 6
        cot_mine, cot_early, cot_late = call(
            cot_kernel, [(size + 4, breadth, own), (size + 4 - late, breadth, own), (late, breadth, own)],
            [], flags, cotangent, cot_inner, name="cot",
        )
        gate = (shares[2], halo_theirs, cot_early)
        shares[2], halo_theirs, cot_early = lax.optimization_barrier(gate)
        halo_got = place.across(halo_theirs)
        shares.append(place.flip(jnp.concatenate(shares, axis=0), bits[0]))
        first_weights = call(
            functools.partial(weights_kernel, steps=near, skip=False),
            kinds, [pltpu.VMEM((taps, own), F32)], flags, w_first, *shares,
            name="weights_first",
        )
        return stats, halo_mine, halo_got, cot_mine, cot_early, cot_late, shares, first_weights

    def block(steps, *operands):
        shapes = jax.eval_shape(steps, *operands)

        def nothing(*operands):
            return jax.tree.map(lambda leaf: jnp.zeros(leaf.shape, leaf.dtype), shapes)

        return lax.cond(edge_flip[0, 0] < 2, steps, nothing, *operands)

    rim_rows = 4 * breadth + 2 * (size + 8) + breadth + 8
    kinds = [jax.ShapeDtypeStruct((3, 3 * depth, depth), BF16)] * 4
    stats, halo_mine, halo_got, cot_mine, cot_early, cot_late, shares, first_weights = block(
        neighbours, stats, inner, to_prev, to_next, message
    )
    sea_count, batch_mean = stats[0], stats[1]
    batch_var = stats[2] / sea_count
    cot_early, got = lax.optimization_barrier((cot_early, got))
    cot_got = place.across(cot_early)

    small = [jax.ShapeDtypeStruct((depth, depth), BF16)] * 4
    second_weights = call(
        functools.partial(weights_kernel, steps=near, skip=True),
        kinds + small, [pltpu.VMEM((taps + depth, own), F32)], flags,
        w_second, *shares, w_skip,
        name="weights_second",
    )

    def buffers(tile):
        return [pltpu.VMEM(((tile + 2) * breadth, 3 * depth), BF16) for _ in range(4)]

    def pair(count, width, kind=F32):
        return [pltpu.VMEM((count, width), kind) for _ in range(2)]

    def edges(count):
        return [pltpu.VMEM((depth // LANES, count, LANES), F32) for _ in range(2)]

    def conv_scratch(tile):
        return buffers(tile) + pair(tile * breadth, depth)

    def first_conv(got, halo_got):
        return call(
            functools.partial(first_kernel, tile=3),
            [
                (size + 8, breadth, depth), (size + 8, depth), (size + 8, depth),
                (size + 6, breadth, depth), (size + 6, breadth, depth),
                (size + 6 + breadth, depth), (size + 6, depth),
            ],
            [pltpu.VMEM((breadth, depth), F32)] + conv_scratch(3),
            flags, marked, got, halo_mine, halo_got, *first_weights[:2], biases,
            name="first",
        )

    scaled, x_left, x_right, hidden, slope_first, to_prev, to_next = block(first_conv, got, halo_got)
    h_ahead, h_left = place.to_prev(to_prev), place.to_next(to_next)
    h_left, cot_got = lax.optimization_barrier((h_left, cot_got))
    cot_got = (cot_got, place.across(cot_late))
    out_own, out_send, slope_second = call(
        functools.partial(second_kernel, tile=4),
        [(size + 4, breadth, own), (size + 4, breadth, own), (size + 4, breadth, depth)],
        pair(size + 6, depth) + conv_scratch(4) + pair(4 * breadth, 2 * depth, BF16)
        + pair(4 * breadth, depth),
        flags, hidden, h_left, h_ahead, *second_weights[:2], biases, scaled, *second_weights[4:6],
        name="second",
    )
    out_send, _ = lax.optimization_barrier((out_send, cot_got[1]))
    out_got = place.across(out_send)

    rim_shapes = [(size + 2 + breadth, depth), (size + 2, depth)]
    upper, grad_second, to_next, to_prev = call(
        functools.partial(back_second_kernel, tile=4),
        [(size + 4, breadth, depth), (size + 4, breadth, depth)] + rim_shapes,
        conv_scratch(4) + edges(breadth),
        flags, cot_mine, cot_got, slope_second, *second_weights[2:4],
        name="back_second",
    )
    groups = place.groups()

    def weight_scratch(kinds, taps):
        turned = [pltpu.VMEM((kinds, depth, 4 * breadth), BF16) for _ in range(2)]
        return buffers(4) + turned + [pltpu.VMEM((taps, depth, depth), F32)]

    def second_weights_grad(to_next, to_prev, grad_second):
        behind, after = place.to_next(to_next), place.to_prev(to_prev)
        grads = call(
            functools.partial(weight_kernel, tile=4, first=False),
            [(9, own, depth)] * 2 + [(1, depth)],
            weight_scratch(2, 9) + pair(size + 6, depth),
            flags, hidden, h_left, h_ahead, grad_second,
            name="weight_second", paired=True,
        )
        return behind, after, *grads

    behind, after, keep, send, gb_second = block(
        second_weights_grad, to_next, to_prev, grad_second
    )
    out_got, send = lax.optimization_barrier((out_got, send))

    def first_weights_grad(keep, send, upper, behind, after):
        grads = call(
            functools.partial(weight_kernel, tile=4, first=True),
            [(10, own, depth)] * 2 + [(1, depth)] * 2 + [(size + 2, breadth, depth)],
            weight_scratch(4, 10),
            flags, scaled, x_left, x_right, upper, behind, after, slope_first, cot_mine, cot_got,
            name="weight_first", paired=True,
        )
        return place.flip(send, groups[0][0]), *grads

    gw_second = [keep]
    other, keep, send, gb_first, gb_skip, grad_first = block(
        first_weights_grad, keep, send, upper, behind, after
    )
    gw_second = [value.reshape(-1, depth) for value in (*gw_second, other)]

    def input_grad(part, *before):
        shapes = [(size // 2, breadth, own)] * 2
        shapes += rim_shapes if part else [(32, depth)] * 2 + [(breadth, depth)]
        scratch = conv_scratch(13) + pair(13 * breadth, 2 * depth, BF16) + edges(40)
        return call(
            functools.partial(back_first_kernel, tile=13, part=part),
            shapes, scratch + [pltpu.VMEM((26, breadth, depth), F32)],
            flags, grad_first, cot_mine, cot_got, *first_weights[2:4], *second_weights[6:8], *before,
            name="back_first_%d" % part,
        )

    def upper_half(send, grad_first, *gw_second):
        return place.shared(gw_second, groups[1]), place.flip(send, groups[0][0]), *input_grad(0)

    gw_second, other, own_upper, send_upper, *before = block(upper_half, send, grad_first, *gw_second)
    gw_first = [value.reshape(-1, depth) for value in (keep, other)]
    got_upper = place.across(send_upper)

    def lower_half(gw_second, keep, other, *before):
        for bits in groups[2:]:
            gw_second = place.shared((gw_second,), bits)
        return gw_second, place.shared((keep, other), groups[1]), *input_grad(1, *before)

    gw_second, gw_first, own_lower, send_lower, to_next, to_prev = block(
        lower_half, gw_second, *gw_first, *before
    )
    got_lower = place.across(send_lower)
    lower_own, lower_send, lower_got = (own_upper, own_lower), (send_upper, send_lower), (got_upper, got_lower)

    def after_products(gw_first, gw_second, to_next, to_prev, out_own, out_got):
        behind, after = place.to_next(to_next), place.to_prev(to_prev)
        for bits in groups[2:]:
            gw_first = place.shared((gw_first,), bits)
        gw_second = gw_second[:, :own] + place.across(gw_second[:, own:])
        output, = call_copy(join_kernel, (rows, breadth, own), flags, out_own, out_got)
        return behind, after, gw_first, gw_second, output

    gw_first, gw_second, got_upper = lax.optimization_barrier((gw_first, gw_second, got_upper))
    behind, after, gw_first, gw_second, output = block(
        after_products, gw_first, gw_second, to_next, to_prev, out_own, out_got
    )

    def last_sums(gw_second, gw_first, behind, after, lower_own, lower_send):
        adds = jnp.concatenate([behind, after], axis=0)
        adds_got = place.across(adds[:, own:])
        column = jnp.arange(breadth)[None, :, None]
        row = jnp.arange(size)[:, None, None]
        edge = jnp.where(place.strip == 0, 0, size - 1)
        at_pole = place.side == 0

        def with_rims(value, adds):
            last = size + 2 + breadth
            value = value + jnp.where(column == 0, adds[1 : size + 1, None], 0.0)
            value = value + jnp.where(column == breadth - 1, adds[last + 1 : last + 1 + size, None], 0.0)
            return value + jnp.where((row == edge) & at_pole, adds[None, size + 2 : last], 0.0)

        sea_weight = sea_mask.astype(F32)[:, :, None]
        own_weight = lax.dynamic_slice_in_dim(sea_weight, place.half * size, size, 0)
        source = scaled[4 : size + 4]
        parts = []
        for value, lanes in ((lower_own, slice(0, own)), (lower_send, slice(own, depth))):
            value = with_rims(jnp.concatenate(value, axis=0), adds[:, lanes])
            parts.append(
                jnp.stack(
                    [
                        jnp.sum(own_weight * value, axis=(0, 1)),
                        jnp.sum(source[:, :, lanes] * value, axis=(0, 1)),
                    ]
                )
            )
        zeros = jnp.zeros((3, depth), F32)
        sums = [gb_first, gb_second, gb_skip, jnp.concatenate(parts, axis=1), zeros]
        sums = place.summed(jnp.concatenate(sums, axis=0))

        def collected(grad):
            for bits in reversed(groups[1:]):
                grad = place.spread(grad, bits)
            grad = grad.reshape(-1, own, own)
            return grad, place.flip(grad, groups[0][0])

        gw_first, _ = lax.optimization_barrier((gw_first, got_lower))
        gw_first = gw_first[:, :own] + place.across(gw_first[:, own:])
        gw_second, gw_first, gw_skip = gather_call(flags, *collected(gw_second), *collected(gw_first))
        sums = sums[:, :own] + place.across(sums[:, own:])
        adds_own = adds[:, :own]
        grad_half = final_call(0, flags, marked, lower_own, adds_own, stats, sums)
        return gw_second, gw_skip, gw_first, sums, adds_got, grad_half

    gw_second, gw_skip, gw_first, sums, adds_got, grad_half = last_sums(
        gw_second, gw_first, behind, after, lower_own, lower_send
    )
    late = (sums, gw_first, gw_second, gw_skip, grad_half, lower_got, adds_got)
    sums, gw_first, gw_second, gw_skip, grad_half, lower_got, adds_got = lax.optimization_barrier(late)
    grad_features = final_call(1, flags, marked, lower_got, adds_got, stats, sums, grad_half)
    new_mean = (1.0 - MOMENTUM) * run_mean + MOMENTUM * batch_mean
    new_var = (1.0 - MOMENTUM) * run_var + MOMENTUM * batch_var * sea_count / (sea_count - 1.0)
    return (
        output,
        grad_features,
        gw_first.reshape(3, 3, depth, own),
        sums[0],
        gw_second.reshape(3, 3, depth, own),
        sums[1],
        gw_skip,
        sums[2],
        new_mean,
        new_var,
    )


def solution(mesh):
    field, kernel, vector = P("pix", None, "ch"), P(None, None, None, "ch"), P("ch")
    placed = (
        field, P("pix", None), P(), kernel, vector, kernel, vector, P(None, "ch"), vector,
        vector, vector, field,
    )
    return jax.shard_map(
        functools.partial(local, mesh),
        mesh=mesh,
        in_specs=placed,
        out_specs=(
            field, field, kernel, vector, kernel, vector, P(None, "ch"), vector, vector, vector,
        ),
        check_vma=False,
    )
```

```python
import functools

import jax
import jax.numpy as jnp
from jax import lax
from jax.experimental import pallas as pl
from jax.experimental.pallas import tpu as pltpu
from jax.sharding import PartitionSpec as P

EPSILON = 1e-05
MOMENTUM = 0.1
INV_ROOT_TWO_PI = 0.3989422804014327
SQRT_HALF = 0.7071067811865476
F32 = jnp.float32
BF16 = jnp.bfloat16
VMEM_LIMIT = 60 * 1024 * 1024
LARGE = 512 * 1024


def split(value):
    high = value.astype(BF16)
    return high, (value - high.astype(F32)).astype(BF16)


def dot_split(a_high, a_low, b_high, b_low):
    total = jnp.dot(a_high, b_high, preferred_element_type=F32)
    total = total + jnp.dot(a_high, b_low, preferred_element_type=F32)
    return total + jnp.dot(a_low, b_high, preferred_element_type=F32)


def gelu_and_slope(u):
    cdf = 0.5 * (1.0 + lax.erf(u * SQRT_HALF))
    return u * cdf, cdf + u * jnp.exp(-0.5 * u * u) * INV_ROOT_TWO_PI


AT_TOP, AT_BOTTOM, SIDE, HALF, FLIPPED, PIX = range(6)
NOT_SEA = 1e30
LANES = 128


def lane_parts(depth):
    return [slice(start, start + LANES) for start in range(0, depth, LANES)]


def put_row(buffers, block, read, left, right, breadth, depth):
    high, low = buffers
    column = lax.broadcasted_iota(jnp.int32, (breadth, 1), 0)
    rows = block_rows(block, breadth)
    for lanes in lane_parts(depth):
        value = read(lanes)
        shifts = (
            jnp.where(column == 0, left(lanes), pltpu.roll(value, 1, 0)),
            value,
            jnp.where(column == breadth - 1, right(lanes), pltpu.roll(value, breadth - 1, 0)),
        )
        for tap, piece in enumerate(shifts):
            place = slice(tap * depth + lanes.start, tap * depth + lanes.stop)
            high[rows, place], low[rows, place] = split(piece)


def conv_tile(buffers, w_high, w_low, total, tile, breadth):
    high, low = buffers
    value = None
    for row_tap in range(3):
        rows = slice(row_tap * breadth, (row_tap + tile) * breadth)
        part = dot_split(high[rows, :], low[rows, :], w_high[row_tap], w_low[row_tap])
        value = part if value is None else value + part
    total[...] = value


def block_rows(block, breadth):
    start = block * breadth
    return pl.ds(start if isinstance(start, int) else pl.multiple_of(start, breadth), breadth)


def pipeline(fills, multiply, finish, tiles, tile, store=lambda tile: None, more=lambda *step: None):
    def fill(step, slot, fresh):
        for count, lay in fills:
            for block in range(count):
                lay(step, slot, block)
        more(step, slot, fresh)

    def finish_all(step, slot):
        for block in range(tile):
            finish(step, slot, block)

    for count, lay in fills:
        pl.loop(0, count)(functools.partial(lay, 0, 0))
    more(0, 0, True)

    @pl.loop(0, (tiles + 1) // 2)
    def _(step):
        now = 2 * step
        fill(jnp.minimum(now + 1, tiles - 1), 1, now + 1 < tiles)
        multiply(0)
        finish_all(jnp.maximum(now - 1, 0), 1)
        fill(jnp.minimum(now + 2, tiles - 1), 0, now + 2 < tiles)
        multiply(1)
        finish_all(now, 0)

        @pl.when(step > 0)
        def _():
            store(now - 1)

        store(now)

    if tiles % 2 == 0:
        pl.loop(0, tile)(functools.partial(finish, tiles - 1, 1))
        store(tiles - 1)


def in_turn(fills, multiply, finish, tiles, tile):
    @pl.loop(0, tiles)
    def _(step):
        for count, lay in fills:
            pl.loop(0, count)(functools.partial(lay, step, 0))
        multiply(0)
        pl.loop(0, tile)(functools.partial(finish, step, 0))


def patch(flags, x, left, right, pole, top, bottom):
    breadth = x.shape[1]

    def put(at, edge):
        @pl.when(flags[FLIPPED] == 1)
        def _():
            for column in range(breadth):
                x[at, column : column + 1] = pole[breadth - 1 - column : breadth - column]

        @pl.when(flags[FLIPPED] == 0)
        def _():
            x[at] = pole[...]

        left[at : at + 1] = 0.5 * (x[at, 0:1] + left[edge : edge + 1])
        right[at : at + 1] = 0.5 * (x[at, breadth - 1 : breadth] + right[edge : edge + 1])

    @pl.when(flags[AT_TOP] == 1)
    def _():
        put(top, top + 1)

    @pl.when(flags[AT_BOTTOM] == 1)
    def _():
        put(bottom, bottom - 1)


def put_messages(flags, x, to_prev, to_next, first_row, last_row):
    rows, breadth = x.shape[0], x.shape[1]

    @pl.loop(0, rows)
    def _(row):
        to_prev[pl.ds(row, 1)] = x[row, 0:1]
        to_next[pl.ds(row, 1)] = x[row, breadth - 1 : breadth]

    to_prev[rows : rows + breadth] = x[jnp.where(flags[AT_BOTTOM] == 1, last_row, first_row)]


def first_kernel(
    traffic, flags, marked, got, halo_mine, halo_got, w_high, w_low, biases,
    scaled, x_left, x_right, hidden, slope, to_prev, to_next,
    pole, high0, low0, high1, low1, total0, total1, *, tile
):
    blocks, breadth, depth = scaled.shape
    own = depth // 2
    extra = blocks - got.shape[0]
    tail = halo_mine.shape[0] - 8
    start = flags[HALF] * (marked.shape[0] - got.shape[0])

    def normal(value, lanes):
        source = halo_mine if lanes.start == 0 else halo_got
        mean, inverse = source[tail : tail + 1], source[tail + 1 : tail + 2]
        return jnp.where(value > 0.1 * NOT_SEA, 0.0, (value - mean) * inverse)

    traffic.wait(0, 1)
    lower, upper = slice(0, own), slice(own, depth)
    main = jnp.where(flags[HALF] == 0, extra, 0)
    outer = jnp.where(flags[HALF] == 0, 0, blocks - extra)

    @pl.loop(0, got.shape[0])
    def _(row):
        scaled[main + row, :, lower] = normal(marked[start + row], lower)
        scaled[main + row, :, upper] = normal(got[row], upper)

    for row in range(extra):
        rows = slice(row * breadth, (row + 1) * breadth)
        scaled[outer + row, :, lower] = normal(halo_mine[rows], lower)
        scaled[outer + row, :, upper] = normal(halo_got[rows], upper)

    begin = extra * breadth
    for target, count in ((x_left, blocks), (x_right, blocks), (pole, breadth)):
        rows = slice(begin, begin + count)
        target[:, lower] = normal(halo_mine[rows], lower)
        target[:, upper] = normal(halo_got[rows], upper)
        begin = begin + count

    patch(flags, scaled, x_left, x_right, pole, 3, blocks - 4)
    traffic.store(0, 0, blocks)
    traffic.wait(4, 5)
    buffers, totals = ((high0, low0), (high1, low1)), (total0, total1)

    def fill(step, slot, block):
        row = jnp.minimum(step * tile + block, blocks - 1)
        put_row(
            buffers[slot], block, lambda lanes: scaled[row, :, lanes],
            lambda lanes: x_left[pl.ds(row, 1)][:, lanes], lambda lanes: x_right[pl.ds(row, 1)][:, lanes],
            breadth, depth,
        )

    def finish(step, slot, block):
        for lanes in lane_parts(depth):
            pre = totals[slot][block_rows(block, breadth), lanes] + biases[0:1, lanes]
            value, grad = gelu_and_slope(pre)
            hidden[step * tile + block, :, lanes] = value
            slope[step * tile + block, :, lanes] = grad

    def store(step):
        traffic.store(3, step * tile, tile)
        traffic.store(4, step * tile, tile)

    pipeline(
        [(tile + 2, fill)],
        lambda slot: conv_tile(buffers[slot], w_high, w_low, totals[slot], tile, breadth),
        finish, hidden.shape[0] // tile, tile, store,
    )
    put_messages(flags, hidden, to_prev, to_next, 3, blocks - 6)


def second_kernel(
    traffic, flags, x, left_in, ahead, w_high, w_low, biases, source, s_high, s_low,
    out_own, out_send, slope,
    left, right, high0, low0, high1, low1, total0, total1, skip0, skip1, sum0, sum1, *, tile
):
    blocks, breadth, depth = x.shape
    own = depth // 2
    left[...] = left_in[...]
    right[...] = ahead[:blocks]
    traffic.wait(0)
    patch(flags, x, left, right, ahead[blocks:], 2, blocks - 3)
    traffic.wait(3, 4, 6)
    buffers, totals, skips = ((high0, low0), (high1, low1)), (total0, total1), (skip0, skip1)
    sums = (sum0, sum1)

    def fill(step, slot, block):
        row = jnp.minimum(step * tile + block, blocks - 1)
        put_row(
            buffers[slot], block, lambda lanes: x[row, :, lanes],
            lambda lanes: left[pl.ds(row, 1)][:, lanes], lambda lanes: right[pl.ds(row, 1)][:, lanes],
            breadth, depth,
        )

    def fill_skip(step, slot, block):
        row = jnp.minimum(step * tile + block + 2, source.shape[0] - 1)
        rows = block_rows(block, breadth)
        for lanes in lane_parts(depth):
            place = slice(depth + lanes.start, depth + lanes.stop)
            skips[slot][rows, lanes], skips[slot][rows, place] = split(source[row, :, lanes])

    def multiply(slot):
        conv_tile(buffers[slot], w_high, w_low, totals[slot], tile, breadth)
        skip = skips[slot]
        sums[slot][...] = dot_split(skip[:, :depth], skip[:, depth:], s_high[...], s_low[...])

    def finish(step, slot, block):
        row = step * tile + block
        rows = block_rows(block, breadth)
        for lanes in lane_parts(depth):
            pre = totals[slot][rows, lanes] + biases[1:2, lanes]
            value, grad = gelu_and_slope(pre)
            slope[row, :, lanes] = grad
            value = value + sums[slot][rows, lanes] + biases[2:3, lanes]
            if lanes.stop <= own:
                out_own[row, :, lanes] = value
            else:
                out_send[row, :, lanes.start - own : lanes.stop - own] = value

    def store(step):
        for result in range(3):
            traffic.store(result, step * tile, tile)

    pipeline([(tile + 2, fill), (tile, fill_skip)], multiply, finish, slope.shape[0] // tile, tile, store)


def edge_products(edges, w_high, w_low, slot, count):
    depth = edges.shape[0] * LANES
    total = None
    for tap in range(3):
        rows = slice(slot * depth, (slot + 1) * depth)
        pieces = [edges[part, tap : tap + count] for part in range(edges.shape[0])]
        edge_high, edge_low = split(jnp.concatenate(pieces, axis=1))
        part = dot_split(edge_high, edge_low, w_high[tap, rows], w_low[tap, rows])
        total = part if total is None else total + part
    return total


def put_rims(flags, to_next, to_prev, first_rim, last_rim, top, bottom):
    count, breadth = to_prev.shape[0], top.shape[0]
    to_prev[...] = first_rim[:count]
    to_next[:count] = last_rim[:count]
    to_next[count:] = jnp.zeros((breadth, to_next.shape[1]), F32)
    column = lax.broadcasted_iota(jnp.int32, (breadth, 1), 0)

    def put(row, at, inner):
        corner_first, corner_last = 0.5 * first_rim[at : at + 1], 0.5 * last_rim[at : at + 1]
        to_prev[inner : inner + 1] += corner_first
        to_next[inner : inner + 1] += corner_last
        row = row[...] + jnp.where(column == 0, corner_first, 0.0)
        row = row + jnp.where(column == breadth - 1, corner_last, 0.0)

        @pl.when(flags[FLIPPED] == 0)
        def _():
            to_next[count:] = row

        @pl.when(flags[FLIPPED] == 1)
        def _():
            for k in range(breadth):
                to_next[count + k : count + k + 1] = row[breadth - 1 - k : breadth - k]

    @pl.when(flags[AT_TOP] == 1)
    def _():
        put(top, 0, 1)

    @pl.when(flags[AT_BOTTOM] == 1)
    def _():
        put(bottom, count - 1, count - 2)


def back_second_kernel(
    traffic, flags, cot_mine, cot_got, slope, w_high, w_low,
    out, grad, to_next, to_prev,
    high0, low0, high1, low1, total0, total1, edge_first, edge_last, *, tile
):
    blocks, breadth, depth = slope.shape
    own = depth // 2
    traffic.wait(0, 1, 2)
    edge_first[...] = jnp.zeros_like(edge_first)
    edge_last[...] = jnp.zeros_like(edge_last)
    buffers, totals = ((high0, low0), (high1, low1)), (total0, total1)

    def fill(step, slot, block):
        row = jnp.minimum(step * tile + block, blocks - 1)
        outside = (flags[AT_TOP] == 1) & (row < 2) | (flags[AT_BOTTOM] == 1) & (row >= blocks - 2)
        inside = jnp.where(outside, 0.0, 1.0)

        def read(lanes):
            cot = cot_mine[row] if lanes.stop <= own else cot_got[row]
            value = cot * slope[row, :, lanes] * inside
            grad[row, :, lanes] = value
            edge_first[lanes.start // LANES, pl.ds(row, 1)] = value[0:1]
            edge_last[lanes.start // LANES, pl.ds(row, 1)] = value[breadth - 1 : breadth]
            return value

        put_row(buffers[slot], block, read, lambda lanes: 0.0, lambda lanes: 0.0, breadth, depth)

    def finish(step, slot, block):
        out[step * tile + block] = totals[slot][block_rows(block, breadth), :]

    traffic.wait(3, 4)
    pipeline(
        [(tile + 2, fill)],
        lambda slot: conv_tile(buffers[slot], w_high, w_low, totals[slot], tile, breadth),
        finish, out.shape[0] // tile, tile, lambda step: traffic.store(0, step * tile, tile),
    )
    traffic.store(1, 0, blocks)
    rows = blocks + 4
    first_rim = edge_products(edge_first, w_high, w_low, 2, rows)
    last_rim = edge_products(edge_last, w_high, w_low, 0, rows)
    put_rims(flags, to_next, to_prev, first_rim, last_rim, out[0], out[blocks - 3])


def back_first_kernel(
    traffic, flags, grad, cot_mine, cot_got, w_high, w_low, s_high, s_low, *rest, tile, part
):
    if part:
        before_first, before_last, before_top, out_own, out_send, to_next, to_prev = rest[:7]
    else:
        out_own, out_send, rim_first, rim_last, top = rest[:5]
    high0, low0, high1, low1, total0, total1, skip0, skip1, edge_first, edge_last, result = rest[-11:]
    count, breadth, depth = grad.shape
    own = depth // 2
    begin = part * ((count - 2) // 2)
    blocks = out_own.shape[0] + 2
    edge_first[...] = jnp.zeros_like(edge_first)
    edge_last[...] = jnp.zeros_like(edge_last)
    buffers, totals, skips = ((high0, low0), (high1, low1)), (total0, total1), (skip0, skip1)
    traffic.wait(0, 1, 2)

    def fill(step, slot, block):
        at = step * tile + block
        row = begin + at - 1
        inside = jnp.where((row >= 0) & (row < count), 1.0, 0.0)
        row = jnp.clip(row, 0, count - 1)

        def read(lanes):
            value = grad[row, :, lanes] * inside
            edge_first[lanes.start // LANES, pl.ds(at, 1)] = value[0:1]
            edge_last[lanes.start // LANES, pl.ds(at, 1)] = value[breadth - 1 : breadth]
            return value

        put_row(buffers[slot], block, read, lambda lanes: 0.0, lambda lanes: 0.0, breadth, depth)

    def fill_skip(step, slot, block):
        row = begin + step * tile + block
        inside = jnp.where((row >= 1) & (row < count - 1), 1.0, 0.0)
        row = jnp.clip(row + 1, 0, cot_mine.shape[0] - 1)
        rows = block_rows(block, breadth)
        for lanes in lane_parts(depth):
            cot = cot_mine[row] if lanes.stop <= own else cot_got[row]
            place = slice(depth + lanes.start, depth + lanes.stop)
            skips[slot][rows, lanes], skips[slot][rows, place] = split(cot * inside)

    def multiply(slot):
        conv_tile(buffers[slot], w_high, w_low, totals[slot], tile, breadth)
        skip = skips[slot]
        totals[slot][...] += dot_split(skip[:, :depth], skip[:, depth:], s_high[...], s_low[...])

    def finish(step, slot, block):
        result[step * tile + block] = totals[slot][block_rows(block, breadth), :]

    traffic.wait(3, 4)
    in_turn([(tile + 2, fill), (tile, fill_skip)], multiply, finish, result.shape[0] // tile, tile)

    @pl.loop(0, out_own.shape[0])
    def _(row):
        out_own[row] = result[row + 1, :, :own]
        out_send[row] = result[row + 1, :, own:]

    traffic.store(0 if part == 0 else 0, 0, out_own.shape[0])
    traffic.store(1, 0, out_own.shape[0])
    rows = blocks + 6
    first_rim = edge_products(edge_first, w_high, w_low, 2, rows)
    last_rim = edge_products(edge_last, w_high, w_low, 0, rows)
    if part == 0:
        rim_first[...], rim_last[...] = first_rim, last_rim
        top[...] = result[0]
    else:
        joined = [
            jnp.concatenate([before[: begin + 1], now[1 : begin + 2]], axis=0)
            for before, now in ((before_first, first_rim), (before_last, last_rim))
        ]
        put_rims(flags, to_next, to_prev, *joined, before_top[...], result[blocks - 1])


def weight_kernel(traffic, flags, x, *rest, tile, first):
    if first:
        left, right, upper, behind, after, slope, cot_mine, cot_got = rest[:8]
        parts, _, total, total_skip, grad_out = rest[8:13]
        rest, begin = rest[13:], 3
    else:
        left_in, ahead, grad = rest[:3]
        parts, _, total = rest[3:6]
        left, right = rest[-2:]
        rest, begin = rest[6:-2], 2
    high0, low0, high1, low1, t0, t1, acc = rest[:7]
    buffers, turned = ((high0, low0), (high1, low1)), (t0, t1)
    breadth, depth = x.shape[1:]
    own = depth // 2
    taps = acc.shape[0]
    rows = x.shape[0] - 2 * begin - 2
    pixels = tile * breadth
    traffic.wait(0)
    if first:
        count = rows + 2
        column = lax.broadcasted_iota(jnp.int32, (breadth, 1), 0)
        traffic.wait(3, 6, 7, 8)
        total_skip[...] = jnp.zeros_like(total_skip)

        def read(row, lanes):
            at = row + 1
            edge = (flags[AT_TOP] == 1) & (row == 0) | (flags[AT_BOTTOM] == 1) & (row == rows - 1)
            value = upper[at, :, lanes] + jnp.where(column == 0, behind[pl.ds(at, 1)][:, lanes], 0.0)
            value = value + jnp.where(column == breadth - 1, after[pl.ds(at, 1)][:, lanes], 0.0)
            value = value + behind[count : count + breadth, lanes] * jnp.where(edge, 1.0, 0.0)
            value = value * slope[at + 2, :, lanes]
            grad_out[at, :, lanes] = value
            return value

        for row, pole in ((-1, AT_TOP), (rows, AT_BOTTOM)):
            for lanes in lane_parts(depth):
                value = read(row, lanes)
                grad_out[row + 1, :, lanes] = value * jnp.where(flags[pole] == 1, 0.0, 1.0)
    else:
        left[...] = left_in[...]
        right[...] = ahead[: x.shape[0]]
        patch(flags, x, left, right, ahead[x.shape[0] :], 2, x.shape[0] - 3)
        traffic.wait(3)

        def read(row, lanes):
            return grad[row + 2, :, lanes]

    acc[...] = jnp.zeros_like(acc)
    total[...] = jnp.zeros_like(total)

    def turn(slot, place, lanes, value):
        value_high, value_low = split(value.T)
        turned[slot][place, lanes] = value_high
        turned[slot][place + 1, lanes] = value_low

    def fill(step, slot, block):
        row = step * tile + block + begin
        put_row(
            buffers[slot], block, lambda lanes: x[row, :, lanes],
            lambda lanes: left[pl.ds(row, 1)][:, lanes], lambda lanes: right[pl.ds(row, 1)][:, lanes],
            breadth, depth,
        )

    def fill_turned(step, slot, fresh):
        once = jnp.where(fresh, 1.0, 0.0)
        for lanes in lane_parts(depth):
            value = jnp.concatenate([read(step * tile + block, lanes) for block in range(tile)], axis=0)
            total[:, lanes] += jnp.sum(value, axis=0, keepdims=True) * once
            turn(slot, 0, lanes, value)
            if first:
                source = cot_mine if lanes.stop <= own else cot_got
                value = source[pl.ds(step * tile + 2, tile)].reshape(pixels, LANES)
                total_skip[:, lanes] += jnp.sum(value, axis=0, keepdims=True) * once
                turn(slot, 2, lanes, value)

    def multiply(slot):
        high, low = buffers[slot]
        for tap in range(taps):
            row_tap, column_tap, place = (tap // 3, tap % 3, 0) if tap < 9 else (1, 1, 2)
            window = slice(row_tap * breadth, row_tap * breadth + pixels)
            lanes = slice(column_tap * depth, (column_tap + 1) * depth)
            acc[tap] += dot_split(
                turned[slot][place], turned[slot][place + 1], high[window, lanes], low[window, lanes]
            )

    pipeline([(tile + 2, fill)], multiply, lambda *block: None, rows // tile, 0, more=fill_turned)
    half = depth // 2
    mine = (flags[SIDE] ^ flags[PIX]) & 1
    for tap in range(taps):
        value = acc[tap].T
        parts[mine, tap] = value[:half]
        parts[1 - mine, tap] = value[half:]


def weights_kernel(traffic, flags, mine, *rest, steps, skip):
    shares, rest = rest[: steps + 1], rest[steps + 1 :]
    if skip:
        mine_skip, f_high, f_low, b_high, b_low, s_high, s_low, sb_high, sb_low, other = rest
    else:
        f_high, f_low, b_high, b_low, other = rest
    own = mine.shape[1]
    depth = 2 * own
    taps = mine.shape[0]
    count = 1 << steps
    traffic.wait(*traffic.ins)
    share, share_skip = taps // count, depth // count
    unit = shares[0].shape[0]
    begin = share if skip else 0
    for piece in range(count):
        away = sum(1 << (steps - 1 - step) for step in range(steps) if piece >> step & 1)
        index = (flags[PIX] & (count - 1)) ^ away
        level = piece.bit_length()
        source = shares[level]
        at = (piece - (1 << (level - 1)) if level else 0) * unit + begin
        other[pl.ds(pl.multiple_of(index * share, 8), share)] = source[at : at + share]
        if skip:
            start = pl.multiple_of(taps + index * share_skip, 8)
            other[pl.ds(start, share_skip)] = source[at + share : at + share + share_skip]
    def both(first, second):
        return jnp.concatenate([first, second], axis=1)

    def one_tap(row_tap, column_tap):
        tap, back_row, back_column = row_tap * 3 + column_tap, 2 - row_tap, 2 - column_tap
        for part in range(2):
            at = pl.multiple_of(tap * depth + jnp.where(flags[SIDE] == part, 0, own), own)
            value = both(mine[pl.ds(at, own)], other[pl.ds(at, own)])
            value_high, value_low = split(value)
            place = pl.ds(pl.multiple_of(column_tap * depth + part * own, own), own)
            f_high[row_tap, place] = value_high
            f_low[row_tap, place] = value_low
            turned_high, turned_low = split(value.T)
            place = pl.ds(pl.multiple_of(back_column * depth, depth), depth)
            lanes = slice(part * own, (part + 1) * own)
            b_high[back_row, place, lanes] = turned_high
            b_low[back_row, place, lanes] = turned_low

    for row_tap in range(3):
        pl.loop(0, 3)(functools.partial(one_tap, row_tap))
        for result in range(4):
            traffic.store(result, row_tap if result < 2 else 2 - row_tap, 1)

    if skip:
        for part in range(2):
            at = pl.multiple_of(jnp.where(flags[SIDE] == part, 0, own), own)
            value = both(mine_skip[pl.ds(at, own)], other[pl.ds(pl.multiple_of(taps + at, own), own)])
            lanes = slice(part * own, (part + 1) * own)
            s_high[lanes], s_low[lanes] = split(value)
            sb_high[:, lanes], sb_low[:, lanes] = split(value.T)


def pre_kernel(traffic, flags, features, mask, marked, theirs, stats, inner, to_prev, to_next):
    rows, breadth, own = features.shape
    length = theirs.shape[0]
    traffic.wait(0)
    start = (1 - flags[HALF]) * (rows - length)
    turned = mask[...].astype(F32)
    turned = jnp.concatenate([turned, jnp.zeros((breadth, 128 - rows), F32)], axis=1)
    none = jnp.zeros((8, own), F32)

    def fold(v):
        return jnp.sum(v.reshape(breadth // 8, 8, own), axis=0)

    def first(step, carry):
        count, total = carry
        base = step * 8
        sea_of = pltpu.roll(turned, 128 - base, 1)
        for k in range(8):
            row = base + k
            sea = jnp.broadcast_to(sea_of[:, k : k + 1], (breadth, own))
            value = features[row]
            land = jnp.where(sea > 0.5, value, NOT_SEA)
            marked[row] = land
            to_prev[pl.ds(row, 1)] = land[0:1]
            to_next[pl.ds(row, 1)] = land[breadth - 1 : breadth]
            count, total = count + fold(sea), total + fold(value * sea)
        return count, total

    count, total = lax.fori_loop(0, rows // 8, first, (none, none))
    count = jnp.sum(count, axis=0, keepdims=True)
    mean = jnp.sum(total, axis=0, keepdims=True) / jnp.maximum(count, 1.0)

    def second(step, squares):
        for k in range(8):
            value = marked[step * 8 + k]
            value = jnp.where(value > 0.1 * NOT_SEA, 0.0, value - mean)
            squares = squares + fold(value * value)
        return squares

    @pl.loop(0, length // 4)
    def _(step):
        theirs[pl.ds(step * 4, 4)] = marked[pl.ds(start + step * 4, 4)]

    traffic.store(1, 0, length)
    traffic.store(0, 0, rows)
    squares = lax.fori_loop(0, rows // 8, second, none)

    stats[...] = jnp.zeros_like(stats)
    stats[0:1] = count
    stats[1:2] = mean
    stats[2:3] = jnp.sum(squares, axis=0, keepdims=True)
    strip = flags[SIDE] ^ flags[HALF]
    to_prev[rows:] = marked[strip * (rows - 1)]
    inner[...] = marked[pl.ds((1 - strip) * (rows - inner.shape[0]), inner.shape[0])]


def cot_kernel(traffic, flags, cot, extra, mine, early, late):
    rows, more, count = cot.shape[0], extra.shape[0], mine.shape[0]
    traffic.wait(0)

    def put(target, begin, half):
        length = target.shape[0]

        @pl.loop(0, length)
        def _(row):
            target[row] = cot[jnp.clip(begin + row - more + half * (rows // 2), 0, rows - 1)]

        if begin == 0:

            @pl.when(half == 0)
            def _():
                target[:more] = extra[...]

        if begin + length == count:

            @pl.when(half == 1)
            def _():
                target[length - more :] = extra[...]

    put(early, 0, 1 - flags[HALF])
    put(late, early.shape[0], 1 - flags[HALF])
    put(mine, 0, flags[HALF])


def rims_kernel(traffic, flags, behind, ahead, core, stats, mine, theirs, wide):
    rows, own = behind.shape
    breadth = ahead.shape[0] - rows
    extra = (core.shape[0]) // (breadth + 2)
    length = rows // 2 + 2 * extra
    inner = extra * breadth
    at = inner
    for target in (mine, theirs):
        target[:inner] = core[:inner]
    for source, start in ((behind, inner + extra), (ahead, inner)):
        wide[:extra] = core[start : start + extra]
        wide[extra : extra + rows] = source[:rows]
        wide[extra + rows :] = core[start : start + extra]
        for target, half in ((mine, flags[HALF]), (theirs, 1 - flags[HALF])):
            target[at : at + length] = wide[pl.ds(pl.multiple_of(half * (rows // 2), 8), length)]
        at = at + length
    count, mean, squares = stats[0:1], stats[1:2], stats[2:3]
    inverse = lax.rsqrt(squares / count + EPSILON)
    for target in (mine, theirs):
        target[at : at + breadth] = ahead[rows:]
        target[at + breadth :] = jnp.zeros((8, own), F32)
        target[at + breadth : at + breadth + 1] = mean
        target[at + breadth + 1 : at + breadth + 2] = inverse


def gather_kernel(flags, second_mine, second_other, first_mine, first_other, second, first, skip, sems):
    half = second_mine.shape[1]
    here = (flags[PIX] & 1) * half
    copies = []
    for place, (mine, start) in enumerate(
        (
            (second_mine, here), (second_other, half - here),
            (first_mine, here), (first_other, half - here),
        )
    ):
        rows = pl.ds(pl.multiple_of(start, half), half)
        target = second if place < 2 else first
        copies.append(pltpu.make_async_copy(mine.at[pl.ds(0, 9)], target.at[:, rows], sems.at[place]))
        if place >= 2:
            copies.append(pltpu.make_async_copy(mine.at[9], skip.at[rows], sems.at[place + 2]))
    for copy in copies:
        copy.start()
    for copy in copies:
        copy.wait()


def gather_call(flags, *operands):
    anywhere, whole = pl.BlockSpec(memory_space=pl.ANY), pl.BlockSpec(memory_space=pltpu.VMEM)
    half, own = operands[0].shape[1:]
    shapes = [(9, 2 * half, own), (9, 2 * half, own), (2 * half, own)]
    return pl.pallas_call(
        gather_kernel,
        out_shape=[jax.ShapeDtypeStruct(shape, F32) for shape in shapes],
        in_specs=[pl.BlockSpec(memory_space=pltpu.SMEM)] + [whole] * 4,
        out_specs=[anywhere] * 3,
        scratch_shapes=[pltpu.SemaphoreType.DMA((6,))],
        compiler_params=pltpu.CompilerParams(vmem_limit_bytes=VMEM_LIMIT),
        cost_estimate=pl.CostEstimate(flops=0, bytes_accessed=12_000_000, transcendentals=0),
        name="gather",
    )(flags, *operands)


def final_kernel(flags, marked, lower_upper, lower_lower, rims, stats, sums, *rest, other, parts):
    out, source, result, in_sems, out_sems = rest[-5:]
    rows, breadth, own = marked.shape
    size = rows // 2
    step = size // parts
    last = size + 2 + breadth
    count, mean = stats[0:1], stats[1:2]
    inverse = lax.rsqrt(stats[2:3] / count + EPSILON)
    first_mean, second_mean = sums[3:4] / count, sums[4:5] / count
    column = lax.broadcasted_iota(jnp.int32, (breadth, 1), 0)
    strip = flags[SIDE] ^ flags[HALF]
    edge = strip * (size - 1)
    half = 1 - flags[HALF] if other else flags[HALF]
    at_pole = flags[SIDE] == (1 if other else 0)

    def fetch(part):
        rows = pl.ds(half * size + part * step, step)
        return pltpu.make_async_copy(marked.at[rows], source.at[pl.ds(part * step, step)], in_sems.at[part])

    def store(part):
        rows = pl.ds(half * size + part * step, step)
        return pltpu.make_async_copy(result.at[pl.ds(part * step, step)], out.at[rows], out_sems.at[part])

    for part in range(parts):
        fetch(part).start()
    for part in range(parts):
        fetch(part).wait()

        lower = lower_upper if part < parts // 2 else lower_lower

        @pl.loop(part * step, (part + 1) * step)
        def _(row):
            value = lower[row % (size // 2)] + jnp.where(column == 0, rims[pl.ds(row + 1, 1)], 0.0)
            value = value + jnp.where(column == breadth - 1, rims[pl.ds(row + last + 1, 1)], 0.0)
            at_edge = jnp.where((row == edge) & at_pole, 1.0, 0.0)
            value = value + rims[size + 2 : last] * at_edge
            normed = (source[row] - mean) * inverse
            value = inverse * (value - first_mean - normed * second_mean)
            result[row] = jnp.where(source[row] > 0.1 * NOT_SEA, 0.0, value)

        store(part).start()
    for part in range(parts):
        store(part).wait()


def final_call(other, flags, marked, lower, rims, stats, sums, before=None):
    anywhere, whole = pl.BlockSpec(memory_space=pl.ANY), pl.BlockSpec(memory_space=pltpu.VMEM)
    parts = 4
    operands = [flags, marked, *lower, rims, stats, sums] + ([before] if other else [])
    half = pltpu.VMEM((marked.shape[0] // 2,) + marked.shape[1:], F32)
    return pl.pallas_call(
        functools.partial(final_kernel, other=other, parts=parts),
        out_shape=jax.ShapeDtypeStruct(marked.shape, F32),
        in_specs=[pl.BlockSpec(memory_space=pltpu.SMEM), anywhere] + [whole] * 5 + [anywhere] * other,
        out_specs=anywhere,
        scratch_shapes=[half, half, pltpu.SemaphoreType.DMA((parts,)), pltpu.SemaphoreType.DMA((parts,))],
        input_output_aliases={7: 0} if other else {},
        compiler_params=pltpu.CompilerParams(vmem_limit_bytes=VMEM_LIMIT),
        cost_estimate=pl.CostEstimate(flops=0, bytes_accessed=4 * marked.size * 3, transcendentals=0),
        name="final_got" if other else "final_own",
    )(*operands)


def join_kernel(flags, mine, theirs, out, sems):
    size = out.shape[0] // 2
    skip = (mine.shape[0] - size) // 2
    copies = []
    for place, source in enumerate((mine, theirs)):
        half = flags[HALF] if place == 0 else 1 - flags[HALF]
        target = out.at[pl.ds(half * size, size)]
        copies.append(pltpu.make_async_copy(source.at[pl.ds(skip, size)], target, sems.at[place]))
    for copy in copies:
        copy.start()
    for copy in copies:
        copy.wait()


def call_copy(kernel, shape, flags, *operands):
    anywhere = pl.BlockSpec(memory_space=pl.ANY)
    return pl.pallas_call(
        kernel,
        out_shape=[jax.ShapeDtypeStruct(shape, F32)],
        in_specs=[pl.BlockSpec(memory_space=pltpu.SMEM)]
        + [pl.BlockSpec(memory_space=pltpu.VMEM)] * len(operands),
        out_specs=[anywhere],
        scratch_shapes=[pltpu.SemaphoreType.DMA((len(operands),))],
        compiler_params=pltpu.CompilerParams(vmem_limit_bytes=VMEM_LIMIT),
        cost_estimate=pl.CostEstimate(flops=0, bytes_accessed=0, transcendentals=0),
        name="join",
    )(flags, *operands)


class Traffic:
    def __init__(self, ins, outs):
        self.ins, self.outs, self.parts = ins, outs, {}
        for copies in ins.values():
            for copy in copies:
                copy.start()

    def wait(self, *places):
        for place in places:
            for copy in self.ins.pop(place):
                copy.wait()

    def store(self, place, start, count):
        source, target, sem = self.outs[place]
        rows = pl.ds(start, count)
        pltpu.make_async_copy(source.at[rows], target.at[rows], sem).start()
        self.parts[place] = True

    def finish(self):
        for place in self.outs:
            if place not in self.parts:
                pltpu.make_async_copy(*self.outs[place]).start()
        for place in self.outs:
            pltpu.make_async_copy(*self.outs[place]).wait()


def call(kernel, shapes, scratch, flags, *operands, name=None, paired=False):
    shapes = [s if isinstance(s, jax.ShapeDtypeStruct) else jax.ShapeDtypeStruct(s, F32) for s in shapes]

    operands = [operand if isinstance(operand, tuple) else (operand,) for operand in operands]
    wholes = [
        jax.ShapeDtypeStruct((sum(part.shape[0] for part in parts),) + parts[0].shape[1:], parts[0].dtype)
        for parts in operands
    ]
    counts = [len(parts) for parts in operands]
    operands = [part for parts in operands for part in parts]

    def large(a):
        return a.size * a.dtype.itemsize >= LARGE

    inside, outside = [large(a) for a in wholes], [large(a) for a in shapes]
    split_up = [is_large for is_large, count in zip(inside, counts) for _ in range(count)]
    buffers = [pltpu.VMEM(a.shape, a.dtype) for a in wholes + shapes[2 * paired :] if large(a)]
    if paired:
        buffers.append(pltpu.VMEM((2,) + shapes[0].shape, F32))
    sems = [pltpu.SemaphoreType.DMA((max(1, sum(group)),)) for group in (split_up, outside)]
    anywhere, whole = pl.BlockSpec(memory_space=pl.ANY), pl.BlockSpec(memory_space=pltpu.VMEM)

    def body(flags, *refs):
        refs = list(refs)
        given = len(operands) + len(shapes)
        rest, (in_sems, out_sems) = refs[given : len(refs) - 2], refs[-2:]
        held, extra = rest[: len(buffers)], rest[len(buffers) :]
        ins, outs, seen, sources, started = {}, {}, [], refs[: len(operands)], 0
        for place, is_large in enumerate(inside):
            parts = [sources.pop(0) for _ in range(counts[place])]
            if not is_large:
                seen.append(parts[0])
                continue
            buffer, row = held.pop(0), 0
            ins[place] = []
            for part in parts:
                target = buffer.at[pl.ds(row, part.shape[0])] if len(parts) > 1 else buffer
                ins[place].append(pltpu.make_async_copy(part, target, in_sems.at[started]))
                row, started = row + part.shape[0], started + 1
            seen.append(buffer)
        for place, is_large in enumerate(outside):
            ref = refs[len(operands) + place]
            if paired and place < 2:
                outs[place] = (held[-1].at[place], ref, out_sems.at[len(outs)])
                seen.append(held[-1])
            elif is_large:
                buffer = held.pop(0)
                outs[place] = (buffer, ref, out_sems.at[len(outs)])
                seen.append(buffer)
            else:
                seen.append(ref)
        traffic = Traffic(ins, outs)
        kernel(traffic, flags, *seen, *extra)
        assert not traffic.ins
        traffic.finish()

    return pl.pallas_call(
        body,
        out_shape=shapes,
        in_specs=[pl.BlockSpec(memory_space=pltpu.SMEM)] + [anywhere if k else whole for k in split_up],
        out_specs=[anywhere if k else whole for k in outside],
        scratch_shapes=buffers + list(scratch) + sems,
        compiler_params=pltpu.CompilerParams(vmem_limit_bytes=VMEM_LIMIT),
        cost_estimate=pl.CostEstimate(flops=0, bytes_accessed=0, transcendentals=0),
        name=name,
    )(flags, *operands)


class Place:
    def __init__(self, mesh, rows, breadth):
        self.count = mesh.shape["pix"]
        self.strips = 3 * breadth // rows
        assert mesh.shape["ch"] == 2 and self.strips == 2
        self.pix = lax.axis_index("pix")
        self.side = lax.axis_index("ch")
        self.ribbon = self.pix // self.strips % 4
        self.strip = self.pix % self.strips
        self.half = self.side ^ self.strip
        self.at_top = (self.side == 0) & (self.strip == 0)
        self.at_bottom = (self.side == 0) & (self.strip == 1)

    def ribbon_pairs(self, offset):
        pairs = []
        for index in range(self.count):
            sample, strip = index // (4 * self.strips), index % self.strips
            ribbon = (index // self.strips + offset) % 4
            pairs.append((index, (sample * 4 + ribbon) * self.strips + strip))
        return pairs

    def to_next(self, value):
        return lax.ppermute(value, "pix", self.ribbon_pairs(1))

    def to_prev(self, value):
        return lax.ppermute(value, "pix", self.ribbon_pairs(-1))

    def across(self, value):
        return lax.ppermute(value, "ch", [(0, 1), (1, 0)])

    def flip(self, value, bit):
        return lax.ppermute(value, "pix", [(i, i ^ bit) for i in range(self.count)])

    def bits(self):
        return [1 << step for step in range(self.count.bit_length() - 1)]

    def ordered(self, mine, theirs, bit):
        upper = (self.pix & bit) != 0
        return jnp.where(upper, theirs, mine), jnp.where(upper, mine, theirs)

    def near(self):
        return self.bits()[:3]

    def members(self, bits):
        out = []
        for other in range(1, 1 << len(bits)):
            mask = sum(bit for step, bit in enumerate(bits) if other >> step & 1)
            out.append((other, [(i, i ^ mask) for i in range(self.count)]))
        return out

    def number(self, bits):
        total = 0
        for step, bit in enumerate(bits):
            total = total + (((self.pix & bit) != 0).astype(jnp.int32) << step)
        return total

    def shared(self, values, bits):
        me, length = self.number(bits), values[0].shape[0] >> len(bits)

        def share(number):
            pieces = [lax.dynamic_slice_in_dim(value, number * length, length, 0) for value in values]
            return functools.reduce(jnp.add, pieces)

        total = share(me)
        parts = []
        for other, pairs in self.members(bits):
            piece = share(me ^ other)
            parts.append(lax.ppermute(piece, "pix", pairs))
        for part in parts:
            total = total + part
        return total

    def spread(self, value, bits):
        parts = [value] + [lax.ppermute(value, "pix", pairs) for _, pairs in self.members(bits)]
        for step, bit in enumerate(bits):
            upper = (self.pix & bit) != 0
            parts = [
                jnp.where(upper, parts[k ^ (1 << step)], parts[k]) for k in range(len(parts))
            ]
        return jnp.concatenate(parts, axis=0)

    def groups(self):
        bits = self.bits()
        rest = [bits[k : k + 2] for k in range(2, len(bits), 2)]
        return [bits[:1], bits[1:2]] + rest

    def summed(self, value):
        for bit in self.bits():
            first, second = self.ordered(value, self.flip(value, bit), bit)
            value = first + second
        return value

    def part(self, value, half, start, length):
        return lax.dynamic_slice_in_dim(value, half * start, length, 0)

    def join_rows(self, mine, theirs):
        return jnp.where(
            self.half == 0,
            jnp.concatenate([mine, theirs], axis=0),
            jnp.concatenate([theirs, mine], axis=0),
        )

    def inner_rows(self, value, extra):
        edge = jnp.where(self.strip == 0, value[-extra:], value[:extra])
        return self.flip(edge, 1)


def merged_stats(place, state):
    for bit in place.bits():
        first, second = place.ordered(state, place.flip(state, bit), bit)
        total = first[0] + second[0]
        safe = jnp.maximum(total, 1.0)
        step = second[1] - first[1]
        state = jnp.stack(
            [
                total,
                (first[0] * first[1] + second[0] * second[1]) / safe,
                first[2] + second[2] + step * step * (first[0] * second[0] / safe),
            ]
            + [total] * 5
        )
    return state


def local(
    mesh, features, sea_mask, edge_flip, w_first, b_first, w_second, b_second, w_skip, b_skip,
    run_mean, run_var, cotangent,
):
    rows, breadth, own = features.shape
    place = Place(mesh, rows, breadth)
    size, depth = rows // 2, 2 * own
    taps = 9 * depth
    flip_row = jnp.sum(jnp.where((jnp.arange(4) == place.ribbon)[:, None], edge_flip, 0), axis=0)
    flipped = jnp.where(place.strip == 0, flip_row[0], flip_row[1]) == 1
    flags = jnp.stack(
        [
            jnp.where(flag, 1, 0).astype(jnp.int32)
            for flag in (place.at_top, place.at_bottom, place.side == 1, place.half == 1, flipped)
        ]
        + [place.pix.astype(jnp.int32)]
    )

    w_first, w_second = w_first.reshape(taps, own), w_second.reshape(taps, own)
    near = len(place.near())
    share, share_skip, number = taps >> near, depth >> near, place.number(place.near())
    biases = jnp.stack([b_first, b_second, b_skip])
    message = jnp.concatenate(
        [
            lax.dynamic_slice_in_dim(w_first, number * share, share, 0),
            lax.dynamic_slice_in_dim(w_second, number * share, share, 0),
            lax.dynamic_slice_in_dim(w_skip, number * share_skip, share_skip, 0),
            jnp.pad(biases, ((0, 5), (0, 0))),
        ]
    )
    features, message = lax.optimization_barrier((features, message))
    message = place.across(message)
    marked, theirs, stats, inner, to_prev, to_next = call(
        pre_kernel,
        [
            (rows, breadth, own), (size + 4, breadth, own), (8, own), (4, breadth, own),
            (rows + breadth, own), (rows, own),
        ],
        [], flags, features, sea_mask.T, name="pre",
    )
    theirs, message = lax.optimization_barrier((theirs, message))
    got = place.across(theirs)
    biases = jnp.concatenate([biases, message[2 * share + share_skip :][:3]], axis=1)
    cot_inner = place.inner_rows(cotangent, 2)

    def neighbours(stats, inner, to_prev, to_next, message):
        mine = message
        bits = place.near()
        ahead, behind = place.to_prev(to_prev), place.to_next(to_next)
        shares = [mine, place.flip(mine, bits[2])]
        shares[1], ahead, behind = lax.optimization_barrier((shares[1], ahead, behind))
        both = jnp.concatenate(shares, axis=0)
        both, inner_rows = lax.optimization_barrier((both, cot_inner))
        shares.append(place.flip(both, bits[1]))

        def inner_part(value):
            return jnp.where(place.strip == 0, value[rows - 4 : rows], value[:4])

        core = jnp.concatenate(
            [inner.reshape(-1, own), inner_part(ahead), inner_part(behind)], axis=0
        )
        core = place.flip(core, 1)
        stats = merged_stats(place, stats)
        halo_mine, halo_theirs = call(
            rims_kernel, [(rim_rows, own)] * 2, [pltpu.VMEM((rows + 8, own), F32)],
            flags, behind, ahead, core, stats, name="rims",
        )
        late = size // 6
        cot_mine, cot_early, cot_late = call(
            cot_kernel, [(size + 4, breadth, own), (size + 4 - late, breadth, own), (late, breadth, own)],
            [], flags, cotangent, inner_rows, name="cot",
        )
        gate = (shares[2], halo_theirs, cot_early)
        shares[2], halo_theirs, cot_early = lax.optimization_barrier(gate)
        halo_got = place.across(halo_theirs)
        shares.append(place.flip(jnp.concatenate(shares, axis=0), bits[0]))
        first_weights = call(
            functools.partial(weights_kernel, steps=near, skip=False),
            kinds, [pltpu.VMEM((taps, own), F32)], flags, w_first, *shares,
            name="weights_first",
        )
        return stats, halo_mine, halo_got, cot_mine, cot_early, cot_late, shares, first_weights

    def block(steps, *operands):
        shapes = jax.eval_shape(steps, *operands)

        def nothing(*operands):
            return jax.tree.map(lambda leaf: jnp.zeros(leaf.shape, leaf.dtype), shapes)

        return lax.cond(edge_flip[0, 0] < 2, steps, nothing, *operands)

    rim_rows = 4 * breadth + 2 * (size + 8) + breadth + 8
    kinds = [jax.ShapeDtypeStruct((3, 3 * depth, depth), BF16)] * 4
    stats, halo_mine, halo_got, cot_mine, cot_early, cot_late, shares, first_weights = block(
        neighbours, stats, inner, to_prev, to_next, message
    )
    sea_count, batch_mean = stats[0], stats[1]
    batch_var = stats[2] / sea_count
    cot_early, got = lax.optimization_barrier((cot_early, got))
    cot_got = place.across(cot_early)

    small = [jax.ShapeDtypeStruct((depth, depth), BF16)] * 4
    second_weights = call(
        functools.partial(weights_kernel, steps=near, skip=True),
        kinds + small, [pltpu.VMEM((taps + depth, own), F32)], flags,
        w_second, *shares, w_skip,
        name="weights_second",
    )

    def buffers(tile):
        return [pltpu.VMEM(((tile + 2) * breadth, 3 * depth), BF16) for _ in range(4)]

    def pair(count, width, kind=F32):
        return [pltpu.VMEM((count, width), kind) for _ in range(2)]

    def edges(count):
        return [pltpu.VMEM((depth // LANES, count, LANES), F32) for _ in range(2)]

    def conv_scratch(tile):
        return buffers(tile) + pair(tile * breadth, depth)

    def first_conv(got, halo_got):
        return call(
            functools.partial(first_kernel, tile=3),
            [
                (size + 8, breadth, depth), (size + 8, depth), (size + 8, depth),
                (size + 6, breadth, depth), (size + 6, breadth, depth),
                (size + 6 + breadth, depth), (size + 6, depth),
            ],
            [pltpu.VMEM((breadth, depth), F32)] + conv_scratch(3),
            flags, marked, got, halo_mine, halo_got, *first_weights[:2], biases,
            name="first",
        )

    scaled, x_left, x_right, hidden, slope_first, to_prev, to_next = block(first_conv, got, halo_got)
    h_ahead, h_left = place.to_prev(to_prev), place.to_next(to_next)
    h_left, cot_got = lax.optimization_barrier((h_left, cot_got))
    cot_got = (cot_got, place.across(cot_late))
    out_own, out_send, slope_second = call(
        functools.partial(second_kernel, tile=4),
        [(size + 4, breadth, own), (size + 4, breadth, own), (size + 4, breadth, depth)],
        pair(size + 6, depth) + conv_scratch(4) + pair(4 * breadth, 2 * depth, BF16)
        + pair(4 * breadth, depth),
        flags, hidden, h_left, h_ahead, *second_weights[:2], biases, scaled, *second_weights[4:6],
        name="second",
    )
    out_send, _ = lax.optimization_barrier((out_send, cot_got[1]))
    out_got = place.across(out_send)

    rim_shapes = [(size + 2 + breadth, depth), (size + 2, depth)]
    upper, grad_second, to_next, to_prev = call(
        functools.partial(back_second_kernel, tile=4),
        [(size + 4, breadth, depth), (size + 4, breadth, depth)] + rim_shapes,
        conv_scratch(4) + edges(breadth),
        flags, cot_mine, cot_got, slope_second, *second_weights[2:4],
        name="back_second",
    )
    groups = place.groups()

    def weight_scratch(kinds, taps):
        turned = [pltpu.VMEM((kinds, depth, 4 * breadth), BF16) for _ in range(2)]
        return buffers(4) + turned + [pltpu.VMEM((taps, depth, depth), F32)]

    def second_weights_grad(to_next, to_prev, grad_second):
        behind, after = place.to_next(to_next), place.to_prev(to_prev)
        grads = call(
            functools.partial(weight_kernel, tile=4, first=False),
            [(9, own, depth)] * 2 + [(1, depth)],
            weight_scratch(2, 9) + pair(size + 6, depth),
            flags, hidden, h_left, h_ahead, grad_second,
            name="weight_second", paired=True,
        )
        return behind, after, *grads

    behind, after, keep, send, gb_second = block(
        second_weights_grad, to_next, to_prev, grad_second
    )
    out_got, send = lax.optimization_barrier((out_got, send))

    def first_weights_grad(keep, send, upper, behind, after):
        grads = call(
            functools.partial(weight_kernel, tile=4, first=True),
            [(10, own, depth)] * 2 + [(1, depth)] * 2 + [(size + 2, breadth, depth)],
            weight_scratch(4, 10),
            flags, scaled, x_left, x_right, upper, behind, after, slope_first, cot_mine, cot_got,
            name="weight_first", paired=True,
        )
        return place.flip(send, groups[0][0]), *grads

    gw_second = [keep]
    other, keep, send, gb_first, gb_skip, grad_first = block(
        first_weights_grad, keep, send, upper, behind, after
    )
    gw_second = [value.reshape(-1, depth) for value in (*gw_second, other)]

    def input_grad(part, *before):
        shapes = [(size // 2, breadth, own)] * 2
        shapes += rim_shapes if part else [(32, depth)] * 2 + [(breadth, depth)]
        scratch = conv_scratch(13) + pair(13 * breadth, 2 * depth, BF16) + edges(40)
        return call(
            functools.partial(back_first_kernel, tile=13, part=part),
            shapes, scratch + [pltpu.VMEM((26, breadth, depth), F32)],
            flags, grad_first, cot_mine, cot_got, *first_weights[2:4], *second_weights[6:8], *before,
            name="back_first_%d" % part,
        )

    def upper_half(send, grad_first, *gw_second):
        return place.shared(gw_second, groups[1]), place.flip(send, groups[0][0]), *input_grad(0)

    gw_second, other, own_upper, send_upper, *before = block(upper_half, send, grad_first, *gw_second)
    gw_first = [value.reshape(-1, depth) for value in (keep, other)]
    got_upper = place.across(send_upper)

    def lower_half(gw_second, keep, other, *before):
        for bits in groups[2:]:
            gw_second = place.shared((gw_second,), bits)
        return gw_second, place.shared((keep, other), groups[1]), *input_grad(1, *before)

    gw_second, gw_first, own_lower, send_lower, to_next, to_prev = block(
        lower_half, gw_second, *gw_first, *before
    )
    got_lower = place.across(send_lower)
    lower_own, lower_send, lower_got = (own_upper, own_lower), (send_upper, send_lower), (got_upper, got_lower)

    def after_products(gw_first, gw_second, to_next, to_prev, out_own, out_got):
        behind, after = place.to_next(to_next), place.to_prev(to_prev)
        for bits in groups[2:]:
            gw_first = place.shared((gw_first,), bits)
        gw_second = gw_second[:, :own] + place.across(gw_second[:, own:])
        output, = call_copy(join_kernel, (rows, breadth, own), flags, out_own, out_got)
        return behind, after, gw_first, gw_second, output

    gw_first, gw_second, got_upper = lax.optimization_barrier((gw_first, gw_second, got_upper))
    behind, after, gw_first, gw_second, output = block(
        after_products, gw_first, gw_second, to_next, to_prev, out_own, out_got
    )

    def last_sums(gw_second, gw_first, behind, after, lower_own, lower_send):
        adds = jnp.concatenate([behind, after], axis=0)
        adds_got = place.across(adds[:, own:])
        column = jnp.arange(breadth)[None, :, None]
        row = jnp.arange(size)[:, None, None]
        edge = jnp.where(place.strip == 0, 0, size - 1)
        at_pole = place.side == 0

        def with_rims(value, adds):
            last = size + 2 + breadth
            value = value + jnp.where(column == 0, adds[1 : size + 1, None], 0.0)
            value = value + jnp.where(column == breadth - 1, adds[last + 1 : last + 1 + size, None], 0.0)
            return value + jnp.where((row == edge) & at_pole, adds[None, size + 2 : last], 0.0)

        sea_weight = sea_mask.astype(F32)[:, :, None]
        own_weight = lax.dynamic_slice_in_dim(sea_weight, place.half * size, size, 0)
        source = scaled[4 : size + 4]
        parts = []
        for value, lanes in ((lower_own, slice(0, own)), (lower_send, slice(own, depth))):
            value = with_rims(jnp.concatenate(value, axis=0), adds[:, lanes])
            parts.append(
                jnp.stack(
                    [
                        jnp.sum(own_weight * value, axis=(0, 1)),
                        jnp.sum(source[:, :, lanes] * value, axis=(0, 1)),
                    ]
                )
            )
        zeros = jnp.zeros((3, depth), F32)
        sums = [gb_first, gb_second, gb_skip, jnp.concatenate(parts, axis=1), zeros]
        sums = place.summed(jnp.concatenate(sums, axis=0))

        def collected(grad):
            for bits in reversed(groups[1:]):
                grad = place.spread(grad, bits)
            return grad.reshape(-1, own, own)

        gw_first, _ = lax.optimization_barrier((gw_first, got_lower))
        gw_first = gw_first[:, :own] + place.across(gw_first[:, own:])
        gw_second, gw_first = collected(gw_second), collected(gw_first)
        second_other = place.flip(gw_second, groups[0][0])
        sums = sums[:, :own] + place.across(sums[:, own:])
        grad_half = final_call(0, flags, marked, lower_own, adds[:, :own], stats, sums)

        first_other = place.flip(gw_first, groups[0][0])
        grad_features = final_call(1, flags, marked, lower_got, adds_got, stats, sums, grad_half)
        return sums, grad_features, *gather_call(flags, gw_second, second_other, gw_first, first_other)

    sums, grad_features, gw_second, gw_first, gw_skip = last_sums(
        gw_second, gw_first, behind, after, lower_own, lower_send
    )
    new_mean = (1.0 - MOMENTUM) * run_mean + MOMENTUM * batch_mean
    new_var = (1.0 - MOMENTUM) * run_var + MOMENTUM * batch_var * sea_count / (sea_count - 1.0)
    return (
        output,
        grad_features,
        gw_first.reshape(3, 3, depth, own),
        sums[0],
        gw_second.reshape(3, 3, depth, own),
        sums[1],
        gw_skip,
        sums[2],
        new_mean,
        new_var,
    )


def solution(mesh):
    field, kernel, vector = P("pix", None, "ch"), P(None, None, None, "ch"), P("ch")
    placed = (
        field, P("pix", None), P(), kernel, vector, kernel, vector, P(None, "ch"), vector,
        vector, vector, field,
    )
    return jax.shard_map(
        functools.partial(local, mesh),
        mesh=mesh,
        in_specs=placed,
        out_specs=(
            field, field, kernel, vector, kernel, vector, P(None, "ch"), vector, vector, vector,
        ),
        check_vma=False,
    )
```
